512 devices in a mesh: gx: 64 (over z, x_lo, core), gy: 8 (over x_hi, y).
Axes of the slice: x: 4 (x_hi: 2, x_lo: 2; x = x_hi * 2 + x_lo), y: 4, z: 16, core: 2. Of those that a mesh axis runs over, the one named last changes fastest.
Arguments:
- source: float32 [128, 128, 128], P('gx', 'gy'), may hold values from -8 to 8
- absorb: float32 [128, 128, 128], P('gx', 'gy'), may hold values from 0.001 to 0.01
- beta: float32 [128, 128, 128], P('gx', 'gy'), may hold values from 0.25 to 4.5
Outputs:
- solution_field: float32 [128, 128, 128], P('gx', 'gy')
The draws below stay inside these ranges and needn't reach their ends.
All inputs are finite; a program needn't handle non-finite values.
Results may differ from the reference program's by a relative error of at most 0.00004.
Values sent between devices are 32-bit elements; how exact they have to be, the bound alone decides.
No kernel may reach another device: no remote copies, remote signals or barrier semaphores. Data moves between devices by JAX's collectives and lax.ppermute only.
A program may use at most 64 MiB of HBM per device.

```python
import math
import jax
import jax.numpy as jnp

LEVELS = 4
SWEEPS = 4
BOTTOM = 8
NX = 128
NY = 128
NZ = 128


def slow_field(key):
    phases = jax.random.uniform(key, (3, 3), jnp.float32, 0.0, 2.0 * math.pi)
    first = jnp.arange(NX, dtype=jnp.float32)[:, None, None] / NX
    second = jnp.arange(NY, dtype=jnp.float32)[None, :, None] / NY
    third = jnp.arange(NZ, dtype=jnp.float32)[None, None, :] / NZ
    total = jnp.zeros((NX, NY, NZ), jnp.float32)
    for mode in range(3):
        wave = 2.0 * math.pi * (mode + 1)
        total = total + jnp.cos(wave * first + phases[mode, 0]) * jnp.cos(wave * second + phases[mode, 1]) * jnp.cos(wave * third + phases[mode, 2])
    return total / 3.0


def draw_source(key, part):
    key = jax.random.fold_in(key, 11)
    slow_key, rough_key = jax.random.split(key)
    slow = slow_field(slow_key)
    rough = jax.random.truncated_normal(rough_key, -4.0, 4.0, (NX, NY, NZ), jnp.float32)
    value = 1.2 * slow + rough
    return value.astype(jnp.float32)


def draw_beta(key, part):
    key = jax.random.fold_in(key, 12)
    slow_key, rough_key = jax.random.split(key)
    slow = slow_field(slow_key)
    spread = 1.1
    rough = jax.random.uniform(rough_key, (NX, NY, NZ), jnp.float32, -spread, spread)
    value = jnp.exp(rough + 0.6 * slow + 0.05)
    return jnp.clip(value, 0.25, 4.5).astype(jnp.float32)


def shard_levels(own_key, shape, cuts, low, high):
    def one(position, shards_of):
        steps = jax.random.uniform(jax.random.fold_in(jax.random.fold_in(own_key, 6), position), (shards_of,), jnp.float32, low / len(cuts), high / len(cuts))
        return jnp.repeat(jnp.exp(steps), shape[position] // shards_of).reshape((-1,) + (1,) * (len(shape) - position - 1))

    gain = one(*cuts[0])
    for cut in cuts[1:]:
        gain = gain * one(*cut)
    return gain


def setup_inputs(seed: int = 0) -> dict:
    arg_keys = jax.random.split(jax.random.key(seed), 4)
    return {
        "source": draw_source(jax.random.fold_in(arg_keys[3], 71), 0),
        "absorb": jnp.clip(jnp.exp(math.log(0.01) - 2.30258502 * jax.random.uniform(arg_keys[1], (NX, NY, NZ), jnp.float32) ** shard_levels(arg_keys[1], (NX, NY, NZ), ((0, 64), (1, 8)), -0.2, 0.2)), 0.001, 0.01),
        "beta": draw_beta(jax.random.fold_in(arg_keys[3], 71), 0),
    }


def chebyshev_table(count):
    centre = 1.125
    half_width = 0.875
    ratio = centre / half_width
    factor = 1.0 / ratio
    table = [(0.0, 1.0 / centre)]
    for order in range(1, count):
        fresh_factor = 1.0 / (2.0 * ratio - factor)
        table.append((fresh_factor * factor, 2.0 * fresh_factor / half_width))
        factor = fresh_factor
    return table


def neighbours(padded):
    return [padded[:-2, 1:-1, 1:-1], padded[2:, 1:-1, 1:-1],
            padded[1:-1, :-2, 1:-1], padded[1:-1, 2:, 1:-1],
            padded[1:-1, 1:-1, :-2], padded[1:-1, 1:-1, 2:]]


def prepare(absorb, beta, half):
    weights = [half * (beta + other) for other in neighbours(jnp.pad(beta, 1))]
    diagonal = absorb
    for weight in weights:
        diagonal = diagonal + weight
    return weights, diagonal, 1.0 / diagonal


def operate(field, parts):
    weights, diagonal, inverse = parts
    result = diagonal * field
    for weight, other in zip(weights, neighbours(jnp.pad(field, 1))):
        result = result - weight * other
    return result


def smooth(guess, source, parts, count, fresh):
    inverse = parts[2]
    current = guess
    previous = guess
    for order, (carry, push) in enumerate(chebyshev_table(count)):
        if order == 0 and fresh:
            residual = source
        else:
            residual = source - operate(current, parts)
        update = current + carry * (current - previous) + push * (inverse * residual)
        previous = current
        current = update
    return current


def restrict(value):
    planes, rows, depth = value.shape
    return value.reshape(planes // 2, 2, rows // 2, 2, depth // 2, 2).sum((1, 3, 5)) * 0.125


def prolong(value):
    return jnp.repeat(jnp.repeat(jnp.repeat(value, 2, 0), 2, 1), 2, 2)


def cycle(source, absorb, beta, level):
    parts = prepare(absorb, beta, 0.5 * 0.25 ** level)
    zeros = jnp.zeros_like(source)
    if level == LEVELS - 1:
        return smooth(zeros, source, parts, BOTTOM, True)
    current = smooth(zeros, source, parts, SWEEPS, True)
    residual = source - operate(current, parts)
    correction = cycle(restrict(residual), restrict(absorb), restrict(beta), level + 1)
    current = current + prolong(correction)
    return smooth(current, source, parts, SWEEPS, False)


def reference(source, absorb, beta):
    return cycle(source, absorb, beta, 0)
```

```python
import jax
import jax.numpy as jnp
from jax import lax
from jax.experimental import pallas as pl
from jax.experimental.pallas import tpu as pltpu
from jax.sharding import PartitionSpec as P

SWEEPS = 4
BOTTOM = 8
LANES = 128
VMEM = 24 * 1024 * 1024

LAYER = 4
PACK = (1, 2, 4, 8)


def face(level):
    return 0.5 * 0.25**level


def chebyshev_table(count):
    centre = 1.125
    half_width = 0.875
    ratio = centre / half_width
    factor = 1.0 / ratio
    table = [(0.0, 1.0 / centre)]
    for order in range(1, count):
        fresh_factor = 1.0 / (2.0 * ratio - factor)
        table.append((fresh_factor * factor, 2.0 * fresh_factor / half_width))
        factor = fresh_factor
    return table


def position():
    return lax.axis_index("gx")


def column_position():
    return lax.axis_index("gy")


def lanes_of(rows):
    return lax.broadcasted_iota(jnp.int32, (rows, LANES), 1)


def rows_of(rows):
    return lax.broadcasted_iota(jnp.int32, (rows, LANES), 0)


def along(value, steps):
    return pltpu.roll(value, (-steps) % LANES, 1)


def across(value, steps):
    rows = value.shape[0]
    return pltpu.roll(value, (-steps) % rows, 0)


class Packed:
    def __init__(self, rows, pack, period, whole):
        lane = lanes_of(rows)
        row = rows_of(rows) % period
        self.pack = pack
        self.inner = lane % pack
        self.third_last = lane >= LANES - pack
        self.third_first = lane < pack
        self.whole = whole
        self.second_last = (row == period - 1) & (self.inner == pack - 1)
        self.second_first = (row == 0) & (self.inner == 0)

    def second_up(self, value):
        if self.pack == 1:
            return across(value, 1)
        return jnp.where(
            self.inner < self.pack - 1, along(value, 1), across(along(value, 1 - self.pack), 1)
        )

    def second_down(self, value):
        if self.pack == 1:
            return across(value, -1)
        return jnp.where(
            self.inner > 0, along(value, -1), across(along(value, self.pack - 1), -1)
        )

    def faces(self, beta, half):
        up = self.second_up(beta)
        if self.whole:
            up = jnp.where(self.second_last, 0.0, up)
        second = half * (beta + up)
        down = self.second_down(beta)
        if self.whole:
            down = jnp.where(self.second_first, 0.0, down)
        share = half * (beta + down) + second
        if self.whole:
            second = jnp.where(self.second_last, 0.0, second)
        third_up = jnp.where(self.third_last, 0.0, along(beta, self.pack))
        third = half * (beta + third_up)
        third_down = jnp.where(self.third_first, 0.0, along(beta, -self.pack))
        share = share + half * (beta + third_down) + third
        return second, jnp.where(self.third_last, 0.0, third), share

    def coupled(self, value, second, third):
        total = second * self.second_up(value) + self.second_down(second * value)
        total = total + third * along(value, self.pack)
        return total + along(third * value, -self.pack)


def pair_sum(value, width):
    low = (lanes_of(value.shape[0]) & width) == 0
    return value + jnp.where(low, along(value, width), along(value, -width))


def residual(shape, source, diag, first, second, third, field, plane, low, high):
    here = field[plane]
    total = source - diag[plane] * here
    if plane + 1 < high:
        total = total + first[plane] * field[plane + 1]
    if plane > low:
        total = total + first[plane - 1] * field[plane - 1]
    return total + shape.coupled(here, second[plane], third[plane])


def sweep(shape, orders, source, parts, buffers, ranges, low, high):
    diag, inverse, first, second, third = parts
    current, previous = buffers
    for (order, (carry, push)), (start, stop) in zip(orders, ranges):
        for plane in range(start, stop):
            rest = residual(
                shape, source(plane), diag, first, second, third, current, plane, low, high
            )
            here = current[plane]
            fresh = here + push * (inverse[plane] * rest)
            if order > 0:
                fresh = fresh + carry * (here - previous[plane])
            previous[plane] = fresh
        current, previous = previous, current
    return current, previous


DEPTH0 = 18
ROWS0 = 32


def gather_level0(region, own, below, above, left, right):
    for part, piece in enumerate((below, own, above)):
        for member in range(LAYER):
            at = part * LAYER + member
            region[at, :, :, 8:24, :] = piece[member]
            region[at, :, :, 0:8, :] = left[part, member]
            region[at, :, :, 24:32, :] = right[part, member]


def level0_parts(shape, beta, absorb, parts, start, stop):
    diag, inverse, first, second, third = parts
    half = face(0)
    before = beta(start - 1)
    here = beta(start)
    lower = half * (before + here)
    first[start - 1] = lower
    for plane in range(start, stop):
        after = beta(plane + 1)
        upper = half * (here + after)
        first[plane] = upper
        second[plane], third[plane], share = shape.faces(here, half)
        total = absorb(plane) + lower + upper + share
        diag[plane] = total
        inverse[plane] = jnp.where(here > 0.0, 1.0 / total, 0.0)
        here, lower = after, upper


def coarse_rows(ref, value, start, count):
    ref[...] = pair_sum(value, 1)
    take = lambda offset: ref[pl.ds(start + offset, count, stride=4), :]
    even = lanes_of(count) % 2 == 0
    return 0.125 * jnp.where(even, take(0) + take(1), take(2) + take(3))


def pre0_kernel(
    own, below, above, left, right, field_out, pay_out,
    region, diag, inverse, first, second, third, one, two, tmp, tile,
):
    gather_level0(region, own, below, above, left, right)
    member = position() % LAYER
    source = lambda plane: region[member + plane // 2, 0, plane % 2]
    absorb = lambda plane: region[member + plane // 2, 1, plane % 2]
    beta = lambda plane: region[member + plane // 2, 2, plane % 2]
    shape = Packed(ROWS0, 1, ROWS0, False)
    parts = (diag, inverse, first, second, third)
    level0_parts(shape, beta, absorb, parts, 1, 17)
    table = chebyshev_table(SWEEPS)
    for plane in range(1, 17):
        one[plane] = table[0][1] * (inverse[plane] * source(plane))
        two[plane] = jnp.zeros((ROWS0, LANES), jnp.float32)
    ranges = [(1 + order, 17 - order) for order in range(1, SWEEPS)]
    current, _ = sweep(
        shape, list(enumerate(table))[1:], source, parts, (one, two), ranges, -1, 99
    )
    for plane in range(4, 14):
        field_out[plane - 4] = current[plane]
    rest = [
        residual(shape, source(plane), diag, first, second, third, current, plane, -1, 99)
        for plane in (8, 9)
    ]
    tile[0:4, :] = coarse_rows(tmp, rest[0] + rest[1], 8, 4)
    betas = [coarse_rows(tmp, beta(plane) + beta(plane + 1), 0, 8) for plane in (6, 8, 10)]
    wide = coarse_rows(tmp, absorb(8) + absorb(9), 0, 8)
    coarse = Packed(8, 2, 8, False)
    half = face(1)
    _, _, share = coarse.faces(betas[1], half)
    total = wide + half * (betas[1] + betas[0]) + half * (betas[1] + betas[2]) + share
    tmp[0:8, :] = betas[1]
    tmp[8:16, :] = total
    tmp[16:24, :] = wide
    tile[4:8, :] = tmp[2:6, :]
    tile[8:12, :] = tmp[10:14, :]
    tile[12:16, :] = tmp[18:22, :]
    whole = tile[...]
    for slot in range(32):
        pay_out[slot] = whole


def post0_kernel(
    own, below, above, left, right, field, coarse_own, coarse_below, coarse_above, out,
    region, diag, inverse, first, second, third, one, two, tmp, wide,
):
    gather_level0(region, own, below, above, left, right)
    member = position() % LAYER
    source = lambda plane: region[member + plane // 2, 0, plane % 2]
    absorb = lambda plane: region[member + plane // 2, 1, plane % 2]
    beta = lambda plane: region[member + plane // 2, 2, plane % 2]
    shape = Packed(ROWS0, 1, ROWS0, False)
    parts = (diag, inverse, first, second, third)
    level0_parts(shape, beta, absorb, parts, 5, 13)
    zero = jnp.zeros((8, LANES), jnp.float32)
    for plane in range(8):
        wide[plane, 0:8, :] = zero
        wide[plane, 40:48, :] = zero
        if plane < 2:
            wide[plane, 8:40, :] = coarse_below[plane]
        elif plane < 6:
            wide[plane, 8:40, :] = coarse_own[plane - 2]
        else:
            wide[plane, 8:40, :] = coarse_above[plane - 6]
    row = column_position() * 4 + 6
    even = lanes_of(8) % 2 == 0
    for pair in range(5):
        value = wide[member + pair, pl.ds(row, 8), :]
        first_rows = jnp.where(even, value, along(value, -1))
        last_rows = jnp.where(even, along(value, 1), value)
        for offset in range(4):
            tmp[pl.ds(offset, 8, stride=4), :] = first_rows if offset < 2 else last_rows
        for plane in (2 * pair + 4, 2 * pair + 5):
            one[plane] = field[plane - 4] + tmp[...]
    table = chebyshev_table(SWEEPS)
    ranges = [(5 + order, 13 - order) for order in range(SWEEPS)]
    current, _ = sweep(
        shape, list(enumerate(table)), source, parts, (one, two), ranges, -1, 99
    )
    for plane in (8, 9):
        out[plane - 8] = current[plane][8:24, :]


DEPTH1 = 12
ROWS1 = 32


def gather_level1(region, own, below, above):
    for part, piece in enumerate((below, own, above)):
        for member in range(LAYER):
            for block in range(8):
                for kind in range(3):
                    region[kind, part * LAYER + member, 4 * block : 4 * block + 4, :] = piece[
                        member * 8 + block, 4 * kind : 4 * kind + 4, :
                    ]


def level1_parts(shape, region, inverse, first, second, third):
    half = face(1)
    for plane in range(DEPTH1):
        beta = region[1, plane]
        if plane + 1 < DEPTH1:
            first[plane] = half * (beta + region[1, plane + 1])
        if 0 < plane < DEPTH1 - 1:
            second[plane], third[plane], _ = shape.faces(beta, half)
        inverse[plane] = jnp.where(beta > 0.0, 1.0 / region[2, plane], 0.0)


def coarser_rows(ref, value):
    ref[...] = pair_sum(pair_sum(value, 1), 2)
    inner = lanes_of(8) % 4
    total = ref[pl.ds(0, 8, stride=4), :]
    for offset in range(1, 4):
        total = jnp.where(inner == offset, ref[pl.ds(offset, 8, stride=4), :], total)
    return 0.125 * total


def pre1_kernel(
    own, below, above, field_out, pay_out,
    region, inverse, first, second, third, one, two, tmp, tile,
):
    gather_level1(region, own, below, above)
    shape = Packed(ROWS1, 2, ROWS1, True)
    level1_parts(shape, region, inverse, first, second, third)
    diag = region.at[2]
    source = lambda plane: region[0, plane]
    parts = (diag, inverse, first, second, third)
    table = chebyshev_table(SWEEPS)
    for plane in range(DEPTH1):
        one[plane] = table[0][1] * (inverse[plane] * source(plane))
        two[plane] = jnp.zeros((ROWS1, LANES), jnp.float32)
    ranges = [(order, DEPTH1 - order) for order in range(1, SWEEPS)]
    current, _ = sweep(
        shape, list(enumerate(table))[1:], source, parts, (one, two), ranges, -1, 99
    )
    for plane in range(4, 8):
        field_out[plane - 4] = current[plane]
    for pair in range(2):
        planes = (4 + 2 * pair, 5 + 2 * pair)
        rest = [
            residual(shape, source(plane), diag, first, second, third, current, plane, -1, 99)
            for plane in planes
        ]
        tile[8 * pair : 8 * pair + 8, :] = coarser_rows(tmp, rest[0] + rest[1])
        tile[16 + 8 * pair : 24 + 8 * pair, :] = coarser_rows(
            tmp, region[1, planes[0]] + region[1, planes[1]]
        )
        for block in range(8):
            two[0, 4 * block : 4 * block + 4, :] = (
                own[2 * pair * 8 + block, 12:16, :] + own[(2 * pair + 1) * 8 + block, 12:16, :]
            )
        tile[32 + 8 * pair : 40 + 8 * pair, :] = coarser_rows(tmp, two[0])
    whole = tile[...]
    for slot in range(16):
        pay_out[slot] = whole


DEPTH2 = 32
ROWS2 = 8


def level2_parts(shape, beta, absorb, parts):
    diag, inverse, first, second, third = parts
    half = face(2)
    lower = half * beta(0)
    for plane in range(DEPTH2):
        here = beta(plane)
        upper = half * (here + beta(plane + 1)) if plane + 1 < DEPTH2 else half * here
        first[plane] = upper
        second[plane], third[plane], share = shape.faces(here, half)
        total = absorb(plane) + lower + upper + share
        diag[plane] = total
        inverse[plane] = 1.0 / total
        lower = upper


def bottom_rows(ref, planes):
    for pair in range(16):
        ref[8 * pair : 8 * pair + 8, :] = pair_sum(
            pair_sum(planes(2 * pair) + planes(2 * pair + 1), 1), 4
        )
    inner = lanes_of(32) % 8
    total = None
    for offset in range(4):
        value = ref[pl.ds(offset, 32, stride=4), :]
        moved = along(value, 1 if offset % 2 == 0 else -1)
        same = 2 * offset + offset % 2
        value = jnp.where(inner == same, value, moved)
        total = value if total is None else jnp.where(inner // 2 == offset, value, total)
    return 0.125 * total


def bottom_solve(source, absorb, beta):
    shape = Packed(32, 8, 2, True)
    half = face(3)
    plane = rows_of(32) // 2
    last, initial = plane == 15, plane == 0
    up = jnp.where(last, 0.0, across(beta, 2))
    down = jnp.where(initial, 0.0, across(beta, -2))
    second, third, share = shape.faces(beta, half)
    upper = half * (beta + up)
    diag = absorb + half * (beta + down) + upper + share
    first = jnp.where(last, 0.0, upper)
    inverse = 1.0 / diag
    table = chebyshev_table(BOTTOM)
    current = table[0][1] * (inverse * source)
    previous = jnp.zeros_like(current)
    for carry, push in table[1:]:
        rest = source - diag * current + first * across(current, 2) + across(first * current, -2)
        rest = rest + shape.coupled(current, second, third)
        fresh = current + carry * (current - previous) + push * (inverse * rest)
        current, previous = fresh, current
    return current


def bottom_prolong(ref, value):
    inner = lanes_of(32) % 8
    part = inner % 4
    back1, back2 = along(value, -1), along(value, -2)
    fore1, fore2 = along(value, 1), along(value, 2)
    low = jnp.where(part == 0, value, jnp.where(part == 3, back2, back1))
    high = jnp.where(part == 3, value, jnp.where(part == 0, fore2, fore1))
    left = inner < 4
    for offset in range(4):
        base = low if offset % 2 == 0 else high
        if offset < 2:
            moved = jnp.where(left, base, along(base, -4))
        else:
            moved = jnp.where(left, along(base, 4), base)
        ref[pl.ds(offset, 32, stride=4), :] = moved


def solve_kernel(
    packed, own, below, above, field_own, field_below, field_above,
    out, out_first, out_last,
    diag2, inverse2, first2, second2, third2, one2, two2, tall,
    region, inverse, first, second, third, one, two, tmp,
):
    shape = Packed(ROWS2, 4, ROWS2, True)

    def kind(number):
        return lambda plane: packed[
            plane // 2, 16 * number + 8 * (plane % 2) : 16 * number + 8 * (plane % 2) + 8, :
        ]

    source2, beta2, absorb2 = kind(0), kind(1), kind(2)
    parts2 = (diag2, inverse2, first2, second2, third2)
    level2_parts(shape, beta2, absorb2, parts2)
    table = chebyshev_table(SWEEPS)
    zero = jnp.zeros((ROWS2, LANES), jnp.float32)
    for plane in range(DEPTH2):
        one2[plane + 2] = table[0][1] * (inverse2[plane] * source2(plane))
        two2[plane + 2] = zero
    inside = (one2.at[pl.ds(2, DEPTH2)], two2.at[pl.ds(2, DEPTH2)])
    everywhere = [(0, DEPTH2)] * SWEEPS
    current, previous = sweep(
        shape, list(enumerate(table))[1:], source2, parts2, inside, everywhere, 0, DEPTH2
    )
    source3 = bottom_rows(
        tall,
        lambda plane: residual(
            shape, source2(plane), diag2, first2, second2, third2, current, plane, 0, DEPTH2
        ),
    )
    absorb3 = bottom_rows(tall, absorb2)
    beta3 = bottom_rows(tall, beta2)
    bottom_prolong(tall, bottom_solve(source3, absorb3, beta3))
    for plane in range(DEPTH2):
        pair = plane // 2
        current[plane] = current[plane] + tall[8 * pair : 8 * pair + 8, :]
    current, previous = sweep(
        shape, list(enumerate(table)), source2, parts2, (current, previous), everywhere, 0, DEPTH2
    )
    whole = two2
    for plane in (0, 1, DEPTH2 + 2, DEPTH2 + 3):
        whole[plane] = zero

    gather_level1(region, own, below, above)
    shape = Packed(ROWS1, 2, ROWS1, True)
    level1_parts(shape, region, inverse, first, second, third)
    layer = position() // LAYER
    inner = lanes_of(8) % 4
    for pair in range(6):
        value = whole[2 * layer + pair]
        moved = {steps: along(value, steps) for steps in range(-3, 4)}
        for offset in range(4):
            picked = moved[offset]
            for lane in range(1, 4):
                picked = jnp.where(inner == lane, moved[offset - lane], picked)
            tmp[pl.ds(offset, 8, stride=4), :] = picked
        for plane in (2 * pair, 2 * pair + 1):
            if plane < 4:
                old = field_below[plane]
            elif plane < 8:
                old = field_own[plane - 4]
            else:
                old = field_above[plane - 8]
            one[plane] = old + tmp[...]
    parts = (region.at[2], inverse, first, second, third)
    ranges = [(order, DEPTH1 - order) for order in range(1, SWEEPS + 1)]
    current, _ = sweep(
        shape, list(enumerate(table)), lambda plane: region[0, plane], parts, (one, two), ranges,
        -1, 99,
    )
    for plane in range(4):
        value = current[plane + 4]
        out[plane] = value
        if plane < 2:
            out_first[plane] = value
        else:
            out_last[plane - 2] = value


def f32(*shape):
    return jax.ShapeDtypeStruct(shape, jnp.float32)


def buffer(*shape):
    return pltpu.VMEM(shape, jnp.float32)


def call(kernel, out, scratch, name, *operands):
    return pl.pallas_call(
        kernel,
        out_shape=out,
        scratch_shapes=scratch,
        name=name,
        compiler_params=pltpu.CompilerParams(vmem_limit_bytes=VMEM),
    )(*operands)


def pre0(*pieces):
    plane = buffer(DEPTH0, ROWS0, LANES)
    scratch = [buffer(12, 3, 2, ROWS0, LANES)] + [plane] * 7 + [buffer(32, LANES), buffer(16, LANES)]
    return call(pre0_kernel, (f32(10, ROWS0, LANES), f32(32, 16, LANES)), scratch, "pre0", *pieces)


def pre1(*pieces):
    plane = buffer(DEPTH1, ROWS1, LANES)
    scratch = [buffer(3, DEPTH1, ROWS1, LANES)] + [plane] * 6 + [buffer(32, LANES), buffer(48, LANES)]
    return call(pre1_kernel, (f32(4, ROWS1, LANES), f32(16, 48, LANES)), scratch, "pre1", *pieces)


def solve(*pieces):
    small = buffer(DEPTH2, ROWS2, LANES)
    padded = buffer(DEPTH2 + 4, ROWS2, LANES)
    plane = buffer(DEPTH1, ROWS1, LANES)
    scratch = [small] * 5 + [padded] * 2 + [buffer(128, LANES)]
    scratch += [buffer(3, DEPTH1, ROWS1, LANES)] + [plane] * 6 + [buffer(32, LANES)]
    out = (f32(4, ROWS1, LANES), f32(2, ROWS1, LANES), f32(2, ROWS1, LANES))
    return call(solve_kernel, out, scratch, "solve", *pieces)


def post0(*pieces):
    plane = buffer(DEPTH0, ROWS0, LANES)
    scratch = [buffer(12, 3, 2, ROWS0, LANES)] + [plane] * 7
    scratch += [buffer(32, LANES), buffer(8, 48, LANES)]
    return call(post0_kernel, f32(2, 16, LANES), scratch, "post0", *pieces)


def shifted(value, axis, steps):
    count = lax.axis_size(axis)
    pairs = [(i, i + steps) for i in range(count) if 0 <= i + steps < count]
    return lax.ppermute(value, axis, pairs)


def body(source, absorb, beta):
    members = lax.axis_size("gx")
    across_y = lax.axis_size("gy")
    layers = members // LAYER
    near = [[LAYER * z + c for c in range(LAYER)] for z in range(layers)]
    layer = [
        [(LAYER * z + c) * across_y + y for c in range(LAYER) for y in range(across_y)]
        for z in range(layers)
    ]
    column = [[LAYER * z + c for z in range(layers)] for c in range(LAYER)]

    local = jnp.stack([source, absorb, beta])
    own = lax.all_gather(local, "gx", axis_index_groups=near)
    below = shifted(own, "gx", LAYER)
    above = shifted(own, "gx", -LAYER)
    left = shifted(jnp.stack([x[..., 8:, :] for x in (below, own, above)]), "gy", 1)
    right = shifted(jnp.stack([x[..., :8, :] for x in (below, own, above)]), "gy", -1)
    pieces0 = (own, below, above, left, right)
    field0, pay = pre0(*pieces0)

    own1 = lax.all_to_all(pay, ("gx", "gy"), 0, 0, axis_index_groups=layer)
    below1 = shifted(own1, "gx", LAYER)
    above1 = shifted(own1, "gx", -LAYER)
    pieces1 = (own1, below1, above1)
    field1, pay = pre1(*pieces1)

    field_below = shifted(field1, "gx", LAYER)
    field_above = shifted(field1, "gx", -LAYER)
    packed = lax.all_to_all(pay, "gx", 0, 0, axis_index_groups=column)
    coarse, coarse_first, coarse_last = solve(
        packed, *pieces1, field1, field_below, field_above
    )

    coarse_below = shifted(coarse_last, "gx", LAYER)
    coarse_above = shifted(coarse_first, "gx", -LAYER)
    return post0(*pieces0, field0, coarse, coarse_below, coarse_above)


def solution(mesh):
    placed = (P("gx", "gy", None), P("gx", "gy", None), P("gx", "gy", None))
    return jax.shard_map(
        body, mesh=mesh, in_specs=placed, out_specs=P("gx", "gy", None), check_vma=False
    )
```

```python
import jax
import jax.numpy as jnp
from jax import lax
from jax.experimental import pallas as pl
from jax.experimental.pallas import tpu as pltpu
from jax.sharding import PartitionSpec as P

SWEEPS = 4
BOTTOM = 8
LANES = 128
VMEM = 24 * 1024 * 1024

LAYER = 4
PACK = (1, 2, 4, 8)


def face(level):
    return 0.5 * 0.25**level


def chebyshev_table(count):
    centre = 1.125
    half_width = 0.875
    ratio = centre / half_width
    factor = 1.0 / ratio
    table = [(0.0, 1.0 / centre)]
    for order in range(1, count):
        fresh_factor = 1.0 / (2.0 * ratio - factor)
        table.append((fresh_factor * factor, 2.0 * fresh_factor / half_width))
        factor = fresh_factor
    return table


def position():
    return lax.axis_index("gx")


def column_position():
    return lax.axis_index("gy")


def lanes_of(rows):
    return lax.broadcasted_iota(jnp.int32, (rows, LANES), 1)


def rows_of(rows):
    return lax.broadcasted_iota(jnp.int32, (rows, LANES), 0)


def along(value, steps):
    return pltpu.roll(value, (-steps) % LANES, 1)


def across(value, steps):
    rows = value.shape[0]
    return pltpu.roll(value, (-steps) % rows, 0)


class Packed:
    def __init__(self, rows, pack, period, whole):
        lane = lanes_of(rows)
        row = rows_of(rows) % period
        self.pack = pack
        self.inner = lane % pack
        self.third_last = lane >= LANES - pack
        self.third_first = lane < pack
        self.whole = whole
        self.second_last = (row == period - 1) & (self.inner == pack - 1)
        self.second_first = (row == 0) & (self.inner == 0)

    def second_up(self, value):
        if self.pack == 1:
            return across(value, 1)
        return jnp.where(
            self.inner < self.pack - 1, along(value, 1), across(along(value, 1 - self.pack), 1)
        )

    def second_down(self, value):
        if self.pack == 1:
            return across(value, -1)
        return jnp.where(
            self.inner > 0, along(value, -1), across(along(value, self.pack - 1), -1)
        )

    def faces(self, beta, half):
        up = self.second_up(beta)
        if self.whole:
            up = jnp.where(self.second_last, 0.0, up)
        second = half * (beta + up)
        down = self.second_down(beta)
        if self.whole:
            down = jnp.where(self.second_first, 0.0, down)
        share = half * (beta + down) + second
        if self.whole:
            second = jnp.where(self.second_last, 0.0, second)
        third_up = jnp.where(self.third_last, 0.0, along(beta, self.pack))
        third = half * (beta + third_up)
        third_down = jnp.where(self.third_first, 0.0, along(beta, -self.pack))
        share = share + half * (beta + third_down) + third
        return second, jnp.where(self.third_last, 0.0, third), share

    def coupled(self, value, second, third):
        total = second * self.second_up(value) + self.second_down(second * value)
        total = total + third * along(value, self.pack)
        return total + along(third * value, -self.pack)


def pair_sum(value, width):
    low = (lanes_of(value.shape[0]) & width) == 0
    return value + jnp.where(low, along(value, width), along(value, -width))


def residual(shape, source, diag, first, second, third, field, plane, low, high):
    here = field[plane]
    total = source - diag[plane] * here
    if plane + 1 < high:
        total = total + first[plane] * field[plane + 1]
    if plane > low:
        total = total + first[plane - 1] * field[plane - 1]
    return total + shape.coupled(here, second[plane], third[plane])


def sweep(shape, orders, source, parts, buffers, ranges, low, high):
    diag, inverse, first, second, third = parts
    current, previous = buffers
    for (order, (carry, push)), (start, stop) in zip(orders, ranges):
        for plane in range(start, stop):
            rest = residual(
                shape, source(plane), diag, first, second, third, current, plane, low, high
            )
            here = current[plane]
            fresh = here + push * (inverse[plane] * rest)
            if order > 0:
                fresh = fresh + carry * (here - previous[plane])
            previous[plane] = fresh
        current, previous = previous, current
    return current, previous


ROWS0 = 32


def gather_level0(region, own, below, above, left, right):
    for part, piece in enumerate((below, own, above)):
        for member in range(LAYER):
            at = part * LAYER + member
            region[at, :, :, 8:24, :] = piece[member]
            region[at, :, :, 0:8, :] = left[part, member]
            region[at, :, :, 24:32, :] = right[part, member]


def level0_parts(shape, beta, absorb, parts, start, stop):
    diag, inverse, first, second, third = parts
    half = face(0)
    before = beta(start - 1)
    here = beta(start)
    lower = half * (before + here)
    first[start - 1] = lower
    for plane in range(start, stop):
        after = beta(plane + 1)
        upper = half * (here + after)
        first[plane] = upper
        second[plane], third[plane], share = shape.faces(here, half)
        total = absorb(plane) + lower + upper + share
        diag[plane] = total
        inverse[plane] = jnp.where(here > 0.0, 1.0 / total, 0.0)
        here, lower = after, upper


def coarse_rows(ref, value):
    ref[...] = pair_sum(value, 1)
    take = lambda offset: ref[pl.ds(offset, 8, stride=4), :]
    even = lanes_of(8) % 2 == 0
    return 0.125 * jnp.where(even, take(0) + take(1), take(2) + take(3))


def pre0_kernel(
    own, below, above, left, right, field_out, tile_out, absorb_out,
    region, diag, inverse, first, second, third, one, two, tmp,
):
    gather_level0(region, own, below, above, left, right)
    source = lambda plane: region[plane // 2, 0, plane % 2]
    absorb = lambda plane: region[plane // 2, 1, plane % 2]
    beta = lambda plane: region[plane // 2, 2, plane % 2]
    shape = Packed(ROWS0, 1, ROWS0, False)
    parts = (diag, inverse, first, second, third)
    level0_parts(shape, beta, absorb, parts, 1, 23)
    table = chebyshev_table(SWEEPS)
    for plane in range(1, 23):
        one[plane] = table[0][1] * (inverse[plane] * source(plane))
        two[plane] = jnp.zeros((ROWS0, LANES), jnp.float32)
    ranges = [(1 + order, 23 - order) for order in range(1, SWEEPS)]
    current, _ = sweep(
        shape, list(enumerate(table))[1:], source, parts, (one, two), ranges, -1, 99
    )
    base = 2 * (position() % LAYER) + 4
    for plane in range(10):
        field_out[plane] = current[base + plane]
    coarse = Packed(8, 2, 8, False)
    half = face(1)
    betas = [coarse_rows(tmp.at[0], beta(p) + beta(p + 1)) for p in range(4, 20, 2)]
    for pair in range(6):
        plane = 6 + 2 * pair
        rest = [
            residual(shape, source(p), diag, first, second, third, current, p, -1, 99)
            for p in (plane, plane + 1)
        ]
        tile_out[pair, 0] = coarse_rows(tmp.at[1 + pair % 3], rest[0] + rest[1])
        here = betas[pair + 1]
        tile_out[pair, 1] = here
        wide = coarse_rows(tmp.at[1 + (pair + 1) % 3], absorb(plane) + absorb(plane + 1))
        _, _, share = coarse.faces(here, half)
        tile_out[pair, 2] = wide + half * (here + betas[pair]) + half * (here + betas[pair + 2]) + share
        if 0 < pair < 5:
            absorb_out[pair - 1] = wide


DEPTH1 = 22
ROWS1 = 16


def gather_level1(region, middle, left, right):
    row = rows_of(8)
    for plane in range(DEPTH1):
        for kind in range(3):
            moved = across(middle[plane, kind], 4)
            region[kind, plane, 0:8, :] = jnp.where(row < 6, left[plane, kind], moved)
            region[kind, plane, 8:16, :] = jnp.where(row < 2, moved, right[plane, kind])


def level1_parts(shape, region, inverse, first, second, third):
    half = face(1)
    for plane in range(DEPTH1):
        beta = region[1, plane]
        if plane + 1 < DEPTH1:
            first[plane] = half * (beta + region[1, plane + 1])
        if 0 < plane < DEPTH1 - 1:
            second[plane], third[plane], _ = shape.faces(beta, half)
        inverse[plane] = jnp.where(beta > 0.0, 1.0 / region[2, plane], 0.0)


def coarser_row(ref, value, start):
    ref[0 : value.shape[0], :] = pair_sum(pair_sum(value, 1), 2)
    inner = lanes_of(1) % 4
    total = ref[start : start + 1, :]
    for offset in range(1, 4):
        total = jnp.where(inner == offset, ref[start + offset : start + offset + 1, :], total)
    return 0.125 * total


def pre1_kernel(
    middle, left, right, absorb, pay_out, field, region, inverse, first, second, third,
    two, tmp, tile,
):
    gather_level1(region, middle, left, right)
    shape = Packed(ROWS1, 2, ROWS1, False)
    level1_parts(shape, region, inverse, first, second, third)
    diag = region.at[2]
    source = lambda plane: region[0, plane]
    parts = (diag, inverse, first, second, third)
    table = chebyshev_table(SWEEPS)
    for plane in range(DEPTH1):
        two[plane] = table[0][1] * (inverse[plane] * source(plane))
        field[plane] = jnp.zeros((ROWS1, LANES), jnp.float32)
    ranges = [(order, DEPTH1 - order) for order in range(1, SWEEPS)]
    current, _ = sweep(
        shape, list(enumerate(table))[1:], source, parts, (two, field), ranges, -1, 99
    )
    for pair in range(2):
        plane = 9 + 2 * pair
        rest = [
            residual(shape, source(p), diag, first, second, third, current, p, -1, 99)
            for p in (plane, plane + 1)
        ]
        tile[pair : pair + 1, :] = coarser_row(tmp.at[pair], rest[0] + rest[1], 6)
        tile[2 + pair : 3 + pair, :] = coarser_row(
            tmp.at[2 + pair], region[1, plane] + region[1, plane + 1], 6
        )
        tile[4 + pair : 5 + pair, :] = coarser_row(
            tmp.at[4 + pair], absorb[2 * pair] + absorb[2 * pair + 1], 2
        )
    tile[6:8, :] = jnp.zeros((2, LANES), jnp.float32)
    whole = tile[...]
    for slot in range(16):
        pay_out[slot] = whole


DEPTH2 = 32
ROWS2 = 8


def level2_parts(shape, beta, absorb, parts):
    diag, inverse, first, second, third = parts
    half = face(2)
    lower = half * beta(0)
    for plane in range(DEPTH2):
        here = beta(plane)
        upper = half * (here + beta(plane + 1)) if plane + 1 < DEPTH2 else half * here
        first[plane] = upper
        second[plane], third[plane], share = shape.faces(here, half)
        total = absorb(plane) + lower + upper + share
        diag[plane] = total
        inverse[plane] = 1.0 / total
        lower = upper


def bottom_rows(ref, planes):
    for pair in range(16):
        ref[8 * pair : 8 * pair + 8, :] = pair_sum(
            pair_sum(planes(2 * pair) + planes(2 * pair + 1), 1), 4
        )
    inner = lanes_of(32) % 8
    total = None
    for offset in range(4):
        value = ref[pl.ds(offset, 32, stride=4), :]
        moved = along(value, 1 if offset % 2 == 0 else -1)
        same = 2 * offset + offset % 2
        value = jnp.where(inner == same, value, moved)
        total = value if total is None else jnp.where(inner // 2 == offset, value, total)
    return 0.125 * total


def bottom_solve(source, absorb, beta):
    shape = Packed(32, 8, 2, True)
    half = face(3)
    plane = rows_of(32) // 2
    last, initial = plane == 15, plane == 0
    up = jnp.where(last, 0.0, across(beta, 2))
    down = jnp.where(initial, 0.0, across(beta, -2))
    second, third, share = shape.faces(beta, half)
    upper = half * (beta + up)
    diag = absorb + half * (beta + down) + upper + share
    first = jnp.where(last, 0.0, upper)
    inverse = 1.0 / diag
    table = chebyshev_table(BOTTOM)
    current = table[0][1] * (inverse * source)
    previous = jnp.zeros_like(current)
    for carry, push in table[1:]:
        rest = source - diag * current + first * across(current, 2) + across(first * current, -2)
        rest = rest + shape.coupled(current, second, third)
        fresh = current + carry * (current - previous) + push * (inverse * rest)
        current, previous = fresh, current
    return current


def bottom_prolong(ref, value):
    inner = lanes_of(32) % 8
    part = inner % 4
    back1, back2 = along(value, -1), along(value, -2)
    fore1, fore2 = along(value, 1), along(value, 2)
    low = jnp.where(part == 0, value, jnp.where(part == 3, back2, back1))
    high = jnp.where(part == 3, value, jnp.where(part == 0, fore2, fore1))
    left = inner < 4
    for offset in range(4):
        base = low if offset % 2 == 0 else high
        if offset < 2:
            moved = jnp.where(left, base, along(base, -4))
        else:
            moved = jnp.where(left, along(base, 4), base)
        ref[pl.ds(offset, 32, stride=4), :] = moved


def solve23(packed, rows2, parts2, one2, two2, tall):
    shape = Packed(ROWS2, 4, ROWS2, True)
    for number in range(3):
        for plane in range(DEPTH2):
            at = 8 * (plane // 2) + 2 * number + plane % 2
            rows2[number, plane] = packed[pl.ds(at, 8, stride=128), :]

    source2 = lambda plane: rows2[0, plane]
    beta2 = lambda plane: rows2[1, plane]
    absorb2 = lambda plane: rows2[2, plane]
    diag2, inverse2, first2, second2, third2 = parts2
    level2_parts(shape, beta2, absorb2, parts2)
    table = chebyshev_table(SWEEPS)
    for plane in range(DEPTH2):
        one2[plane] = table[0][1] * (inverse2[plane] * source2(plane))
        two2[plane] = jnp.zeros((ROWS2, LANES), jnp.float32)
    everywhere = [(0, DEPTH2)] * SWEEPS
    current, previous = sweep(
        shape, list(enumerate(table))[1:], source2, parts2, (one2, two2), everywhere, 0, DEPTH2
    )
    source3 = bottom_rows(
        tall.at[0],
        lambda plane: residual(
            shape, source2(plane), diag2, first2, second2, third2, current, plane, 0, DEPTH2
        ),
    )
    absorb3 = bottom_rows(tall.at[1], absorb2)
    beta3 = bottom_rows(tall.at[2], beta2)
    bottom_prolong(tall.at[0], bottom_solve(source3, absorb3, beta3))
    for plane in range(DEPTH2):
        pair = plane // 2
        current[plane] = current[plane] + tall[0, 8 * pair : 8 * pair + 8, :]
    current, previous = sweep(
        shape, list(enumerate(table)), source2, parts2, (current, previous), everywhere, 0, DEPTH2
    )
    return current


def post1(middle, left, right, field, whole, region, parts, one, two, wide, tmp):
    inverse, first, second, third = parts
    gather_level1(region, middle, left, right)
    shape = Packed(ROWS1, 2, ROWS1, False)
    level1_parts(shape, region, inverse, first, second, third)
    layer = position() // LAYER
    row = column_position() + 6
    zero = jnp.zeros((8, LANES), jnp.float32)
    for plane in range(DEPTH2 + 6):
        wide[plane, 0:8, :] = zero
        wide[plane, 16:24, :] = zero
        inside = 3 <= plane < DEPTH2 + 3
        wide[plane, 8:16, :] = whole[plane - 3] if inside else zero
    inner = lanes_of(8) % 4
    for pair in range(8):
        value = wide[2 * layer + pair, pl.ds(row, 8), :]
        moved = {steps: along(value, steps) for steps in range(-3, 4)}
        part = tmp.at[pair]
        for offset in range(4):
            picked = moved[offset]
            for lane in range(1, 4):
                picked = jnp.where(inner == lane, moved[offset - lane], picked)
            part[pl.ds(offset, 8, stride=4), :] = picked
        for plane in (2 * pair + 3, 2 * pair + 4):
            one[plane] = field[plane] + part[2:18, :]
    table = chebyshev_table(SWEEPS)
    ranges = [(3 + order, 19 - order) for order in range(1, SWEEPS + 1)]
    current, _ = sweep(
        shape, list(enumerate(table)), lambda plane: region[0, plane],
        (region.at[2], inverse, first, second, third), (one, two), ranges, -1, 99,
    )
    return current


def post0(pieces, field, coarse, out, region, parts, one, two, tmp):
    gather_level0(region, *pieces)
    member = position() % LAYER
    source = lambda plane: region[member + plane // 2, 0, plane % 2]
    absorb = lambda plane: region[member + plane // 2, 1, plane % 2]
    beta = lambda plane: region[member + plane // 2, 2, plane % 2]
    shape = Packed(ROWS0, 1, ROWS0, False)
    level0_parts(shape, beta, absorb, parts, 5, 13)
    even = lanes_of(8) % 2 == 0
    for pair in range(5):
        value = coarse[7 + member + pair, 4:12, :]
        upper_rows = jnp.where(even, value, along(value, -1))
        lower_rows = jnp.where(even, along(value, 1), value)
        part = tmp.at[pair]
        for offset in range(4):
            part[pl.ds(offset, 8, stride=4), :] = upper_rows if offset < 2 else lower_rows
        for plane in (2 * pair + 4, 2 * pair + 5):
            one[plane] = field[plane - 4] + part[...]
    table = chebyshev_table(SWEEPS)
    ranges = [(5 + order, 13 - order) for order in range(SWEEPS)]
    current, _ = sweep(
        shape, list(enumerate(table)), source, parts, (one, two), ranges, -1, 99
    )
    for plane in (8, 9):
        out[plane - 8] = current[plane][8:24, :]


def finish_kernel(
    packed, middle, left1, right1, field1, own, below, above, left, right, field0, out,
    rows2, diag2, inverse2, first2, second2, third2, one2, two2, tall,
    region1, inverse1, first1, second1, third1, one1, two1, wide1, tmp1,
    region0, diag0, inverse0, first0, second0, third0, one0, two0, tmp0,
):
    parts2 = (diag2, inverse2, first2, second2, third2)
    whole = solve23(packed, rows2, parts2, one2, two2, tall)
    parts1 = (inverse1, first1, second1, third1)
    coarse = post1(
        middle, left1, right1, field1, whole, region1, parts1, one1, two1, wide1, tmp1
    )
    parts0 = (diag0, inverse0, first0, second0, third0)
    post0(
        (own, below, above, left, right), field0, coarse, out, region0, parts0, one0, two0, tmp0
    )


def f32(*shape):
    return jax.ShapeDtypeStruct(shape, jnp.float32)


def buffer(*shape):
    return pltpu.VMEM(shape, jnp.float32)


def call(kernel, out, scratch, name, *operands):
    return pl.pallas_call(
        kernel,
        out_shape=out,
        scratch_shapes=scratch,
        name=name,
        compiler_params=pltpu.CompilerParams(vmem_limit_bytes=VMEM),
    )(*operands)


def pre0(*pieces):
    plane = buffer(24, ROWS0, LANES)
    scratch = [buffer(12, 3, 2, ROWS0, LANES)] + [plane] * 7 + [buffer(4, ROWS0, LANES)]
    out = (f32(10, ROWS0, LANES), f32(6, 3, 8, LANES), f32(4, 8, LANES))
    return call(pre0_kernel, out, scratch, "pre0", *pieces)


def pre1(*pieces):
    plane = buffer(DEPTH1, ROWS1, LANES)
    scratch = [buffer(3, DEPTH1, ROWS1, LANES)] + [plane] * 5
    scratch += [buffer(6, ROWS1, LANES), buffer(8, LANES)]
    out = (f32(16, 8, LANES), f32(DEPTH1, ROWS1, LANES))
    return call(pre1_kernel, out, scratch, "pre1", *pieces)


def finish(*pieces):
    plane2 = buffer(DEPTH2, ROWS2, LANES)
    plane1 = buffer(DEPTH1, ROWS1, LANES)
    plane0 = buffer(18, ROWS0, LANES)
    scratch = [buffer(3, DEPTH2, ROWS2, LANES)] + [plane2] * 7 + [buffer(3, 128, LANES)]
    scratch += [buffer(3, DEPTH1, ROWS1, LANES)] + [plane1] * 6
    scratch += [buffer(DEPTH2 + 6, 24, LANES), buffer(8, 32, LANES)]
    scratch += [buffer(12, 3, 2, ROWS0, LANES)] + [plane0] * 7 + [buffer(5, ROWS0, LANES)]
    return call(finish_kernel, f32(2, 16, LANES), scratch, "finish", *pieces)


def shifted(value, axis, steps):
    count = lax.axis_size(axis)
    pairs = [(i, i + steps) for i in range(count) if 0 <= i + steps < count]
    return lax.ppermute(value, axis, pairs)


def body(source, absorb, beta):
    members = lax.axis_size("gx")
    across_y = lax.axis_size("gy")
    layers = members // LAYER
    near = [[LAYER * z + c for c in range(LAYER)] for z in range(layers)]
    column = [[LAYER * z + c for z in range(layers)] for c in range(LAYER)]

    local = jnp.stack([source, absorb, beta])
    own = lax.all_gather(local, "gx", axis_index_groups=near)
    below = shifted(own, "gx", LAYER)
    above = shifted(own, "gx", -LAYER)
    left = shifted(jnp.stack([x[..., 8:, :] for x in (below, own, above)]), "gy", 1)
    right = shifted(jnp.stack([x[..., :8, :] for x in (below, own, above)]), "gy", -1)
    pieces0 = (own, below, above, left, right)
    field0, tile, absorb1 = pre0(*pieces0)

    layer_tiles = [
        shifted(tile, "gx", 2 * LAYER)[0:5],
        shifted(tile, "gx", LAYER)[1:5],
        tile[1:5],
        shifted(tile, "gx", -LAYER)[1:5],
        shifted(tile, "gx", -2 * LAYER)[1:6],
    ]
    middle = jnp.concatenate(layer_tiles)
    pieces1 = (middle, shifted(middle, "gy", 1), shifted(middle, "gy", -1))
    pay, field1 = pre1(*pieces1, absorb1)

    rows = lax.all_to_all(pay, "gx", 0, 0, axis_index_groups=column)
    rows = jnp.broadcast_to(rows, (across_y,) + rows.shape)
    packed = lax.all_to_all(rows, "gy", 0, 0).reshape(-1, LANES)
    return finish(packed, *pieces1, field1, *pieces0, field0)


def solution(mesh):
    placed = (P("gx", "gy", None), P("gx", "gy", None), P("gx", "gy", None))
    return jax.shard_map(
        body, mesh=mesh, in_specs=placed, out_specs=P("gx", "gy", None), check_vma=False
    )
```

```python
import jax
import jax.numpy as jnp
from jax import lax
from jax.experimental import pallas as pl
from jax.experimental.pallas import tpu as pltpu
from jax.sharding import PartitionSpec as P

SWEEPS = 4
BOTTOM = 8
LANES = 128
VMEM = 24 * 1024 * 1024

LAYER = 4
PACK = (1, 2, 4, 8)


def face(level):
    return 0.5 * 0.25**level


def chebyshev_table(count):
    centre = 1.125
    half_width = 0.875
    ratio = centre / half_width
    factor = 1.0 / ratio
    table = [(0.0, 1.0 / centre)]
    for order in range(1, count):
        fresh_factor = 1.0 / (2.0 * ratio - factor)
        table.append((fresh_factor * factor, 2.0 * fresh_factor / half_width))
        factor = fresh_factor
    return table


def position():
    return lax.axis_index("gx")


def column_position():
    return lax.axis_index("gy")


def lanes_of(rows):
    return lax.broadcasted_iota(jnp.int32, (rows, LANES), 1)


def rows_of(rows):
    return lax.broadcasted_iota(jnp.int32, (rows, LANES), 0)


def along(value, steps):
    return pltpu.roll(value, (-steps) % LANES, 1)


def across(value, steps):
    rows = value.shape[0]
    return pltpu.roll(value, (-steps) % rows, 0)


class Packed:
    def __init__(self, rows, pack, period, whole):
        lane = lanes_of(rows)
        row = rows_of(rows) % period
        self.pack = pack
        self.inner = lane % pack
        self.third_last = lane >= LANES - pack
        self.third_first = lane < pack
        self.whole = whole
        self.second_last = (row == period - 1) & (self.inner == pack - 1)
        self.second_first = (row == 0) & (self.inner == 0)

    def second_up(self, value):
        if self.pack == 1:
            return across(value, 1)
        return jnp.where(
            self.inner < self.pack - 1, along(value, 1), across(along(value, 1 - self.pack), 1)
        )

    def second_down(self, value):
        if self.pack == 1:
            return across(value, -1)
        return jnp.where(
            self.inner > 0, along(value, -1), across(along(value, self.pack - 1), -1)
        )

    def faces(self, beta, half):
        up = self.second_up(beta)
        if self.whole:
            up = jnp.where(self.second_last, 0.0, up)
        second = half * (beta + up)
        down = self.second_down(beta)
        if self.whole:
            down = jnp.where(self.second_first, 0.0, down)
        share = half * (beta + down) + second
        if self.whole:
            second = jnp.where(self.second_last, 0.0, second)
        third_up = jnp.where(self.third_last, 0.0, along(beta, self.pack))
        third = half * (beta + third_up)
        third_down = jnp.where(self.third_first, 0.0, along(beta, -self.pack))
        share = share + half * (beta + third_down) + third
        return second, jnp.where(self.third_last, 0.0, third), share

    def coupled(self, value, second, third):
        total = second * self.second_up(value) + self.second_down(second * value)
        total = total + third * along(value, self.pack)
        return total + along(third * value, -self.pack)


def pair_sum(value, width):
    low = (lanes_of(value.shape[0]) & width) == 0
    return value + jnp.where(low, along(value, width), along(value, -width))


def residual(shape, source, diag, first, second, third, field, plane, low, high):
    here = field[plane]
    total = source - diag[plane] * here
    if plane + 1 < high:
        total = total + first[plane] * field[plane + 1]
    if plane > low:
        total = total + first[plane - 1] * field[plane - 1]
    return total + shape.coupled(here, second[plane], third[plane])


def sweep(shape, orders, source, parts, buffers, ranges, low, high):
    diag, inverse, first, second, third = parts
    current, previous = buffers
    for (order, (carry, push)), (start, stop) in zip(orders, ranges):
        for plane in range(start, stop):
            rest = residual(
                shape, source(plane), diag, first, second, third, current, plane, low, high
            )
            here = current[plane]
            fresh = here + push * (inverse[plane] * rest)
            if order > 0:
                fresh = fresh + carry * (here - previous[plane])
            previous[plane] = fresh
        current, previous = previous, current
    return current, previous


ROWS0 = 32


def gather_level0(region, own, outer, sides):
    for part, piece in enumerate((outer.at[0], own, outer.at[1])):
        for member in range(LAYER):
            at = part * LAYER + member
            region[at, :, :, 8:24, :] = piece[member]
            region[at, :, :, 0:8, :] = sides[0, part, member]
            region[at, :, :, 24:32, :] = sides[1, part, member]


def level0_parts(shape, beta, absorb, parts, start, stop):
    diag, inverse, first, second, third = parts
    half = face(0)
    before = beta(start - 1)
    here = beta(start)
    lower = half * (before + here)
    first[start - 1] = lower
    for plane in range(start, stop):
        after = beta(plane + 1)
        upper = half * (here + after)
        first[plane] = upper
        second[plane], third[plane], share = shape.faces(here, half)
        total = absorb(plane) + lower + upper + share
        diag[plane] = total
        inverse[plane] = jnp.where(here > 0.0, 1.0 / total, 0.0)
        here, lower = after, upper


def coarse_rows(ref, value):
    ref[...] = pair_sum(value, 1)
    take = lambda offset: ref[pl.ds(offset, 8, stride=4), :]
    even = lanes_of(8) % 2 == 0
    return 0.125 * jnp.where(even, take(0) + take(1), take(2) + take(3))


def pre0_kernel(
    own, outer, sides, field_out, tile_out, absorb_out,
    region, diag, inverse, first, second, third, one, two, tmp,
):
    gather_level0(region, own, outer, sides)
    source = lambda plane: region[plane // 2, 0, plane % 2]
    absorb = lambda plane: region[plane // 2, 1, plane % 2]
    beta = lambda plane: region[plane // 2, 2, plane % 2]
    shape = Packed(ROWS0, 1, ROWS0, False)
    parts = (diag, inverse, first, second, third)
    level0_parts(shape, beta, absorb, parts, 1, 23)
    table = chebyshev_table(SWEEPS)
    for plane in range(1, 23):
        one[plane] = table[0][1] * (inverse[plane] * source(plane))
        two[plane] = jnp.zeros((ROWS0, LANES), jnp.float32)
    ranges = [(1 + order, 23 - order) for order in range(1, SWEEPS)]
    current, _ = sweep(
        shape, list(enumerate(table))[1:], source, parts, (one, two), ranges, -1, 99
    )
    base = 2 * (position() % LAYER) + 4
    for plane in range(10):
        field_out[plane] = current[base + plane]
    coarse = Packed(8, 2, 8, False)
    half = face(1)
    betas = [coarse_rows(tmp.at[0], beta(p) + beta(p + 1)) for p in range(4, 20, 2)]
    for pair in range(6):
        plane = 6 + 2 * pair
        rest = [
            residual(shape, source(p), diag, first, second, third, current, p, -1, 99)
            for p in (plane, plane + 1)
        ]
        tile_out[pair, 0] = coarse_rows(tmp.at[1 + pair % 3], rest[0] + rest[1])
        here = betas[pair + 1]
        tile_out[pair, 1] = here
        wide = coarse_rows(tmp.at[1 + (pair + 1) % 3], absorb(plane) + absorb(plane + 1))
        _, _, share = coarse.faces(here, half)
        tile_out[pair, 2] = wide + half * (here + betas[pair]) + half * (here + betas[pair + 2]) + share
        if 0 < pair < 5:
            absorb_out[pair - 1] = wide


DEPTH1 = 22
ROWS1 = 16


def gather_level1(region, middle, sides):
    row = rows_of(8)
    for plane in range(DEPTH1):
        for kind in range(3):
            moved = across(middle[plane, kind], 4)
            region[kind, plane, 0:8, :] = jnp.where(row < 6, sides[0, plane, kind], moved)
            region[kind, plane, 8:16, :] = jnp.where(row < 2, moved, sides[1, plane, kind])


def level1_parts(shape, region, inverse, first, second, third):
    half = face(1)
    for plane in range(DEPTH1):
        beta = region[1, plane]
        if plane + 1 < DEPTH1:
            first[plane] = half * (beta + region[1, plane + 1])
        if 0 < plane < DEPTH1 - 1:
            second[plane], third[plane], _ = shape.faces(beta, half)
        inverse[plane] = jnp.where(beta > 0.0, 1.0 / region[2, plane], 0.0)


def coarser_row(ref, value, start):
    ref[0 : value.shape[0], :] = pair_sum(pair_sum(value, 1), 2)
    inner = lanes_of(1) % 4
    total = ref[start : start + 1, :]
    for offset in range(1, 4):
        total = jnp.where(inner == offset, ref[start + offset : start + offset + 1, :], total)
    return 0.125 * total


def pre1_kernel(
    middle, sides, absorb, pay_out, field, region, inverse, first, second, third,
    two, tmp, tile,
):
    gather_level1(region, middle, sides)
    shape = Packed(ROWS1, 2, ROWS1, False)
    level1_parts(shape, region, inverse, first, second, third)
    diag = region.at[2]
    source = lambda plane: region[0, plane]
    parts = (diag, inverse, first, second, third)
    table = chebyshev_table(SWEEPS)
    for plane in range(DEPTH1):
        two[plane] = table[0][1] * (inverse[plane] * source(plane))
        field[plane] = jnp.zeros((ROWS1, LANES), jnp.float32)
    ranges = [(order, DEPTH1 - order) for order in range(1, SWEEPS)]
    current, _ = sweep(
        shape, list(enumerate(table))[1:], source, parts, (two, field), ranges, -1, 99
    )
    for pair in range(2):
        plane = 9 + 2 * pair
        rest = [
            residual(shape, source(p), diag, first, second, third, current, p, -1, 99)
            for p in (plane, plane + 1)
        ]
        tile[pair : pair + 1, :] = coarser_row(tmp.at[pair], rest[0] + rest[1], 6)
        tile[2 + pair : 3 + pair, :] = coarser_row(
            tmp.at[2 + pair], region[1, plane] + region[1, plane + 1], 6
        )
        tile[4 + pair : 5 + pair, :] = coarser_row(
            tmp.at[4 + pair], absorb[2 * pair] + absorb[2 * pair + 1], 2
        )
    tile[6:8, :] = jnp.zeros((2, LANES), jnp.float32)
    whole = tile[...]
    for slot in range(16):
        pay_out[slot] = whole


DEPTH2 = 32
ROWS2 = 8


def level2_parts(shape, beta, absorb, parts):
    diag, inverse, first, second, third = parts
    half = face(2)
    lower = half * beta(0)
    for plane in range(DEPTH2):
        here = beta(plane)
        upper = half * (here + beta(plane + 1)) if plane + 1 < DEPTH2 else half * here
        first[plane] = upper
        second[plane], third[plane], share = shape.faces(here, half)
        total = absorb(plane) + lower + upper + share
        diag[plane] = total
        inverse[plane] = 1.0 / total
        lower = upper


def bottom_rows(ref, planes):
    for pair in range(16):
        ref[8 * pair : 8 * pair + 8, :] = pair_sum(
            pair_sum(planes(2 * pair) + planes(2 * pair + 1), 1), 4
        )
    inner = lanes_of(32) % 8
    total = None
    for offset in range(4):
        value = ref[pl.ds(offset, 32, stride=4), :]
        moved = along(value, 1 if offset % 2 == 0 else -1)
        same = 2 * offset + offset % 2
        value = jnp.where(inner == same, value, moved)
        total = value if total is None else jnp.where(inner // 2 == offset, value, total)
    return 0.125 * total


def bottom_solve(source, absorb, beta):
    shape = Packed(32, 8, 2, True)
    half = face(3)
    plane = rows_of(32) // 2
    last, initial = plane == 15, plane == 0
    up = jnp.where(last, 0.0, across(beta, 2))
    down = jnp.where(initial, 0.0, across(beta, -2))
    second, third, share = shape.faces(beta, half)
    upper = half * (beta + up)
    diag = absorb + half * (beta + down) + upper + share
    first = jnp.where(last, 0.0, upper)
    inverse = 1.0 / diag
    table = chebyshev_table(BOTTOM)
    current = table[0][1] * (inverse * source)
    previous = jnp.zeros_like(current)
    for carry, push in table[1:]:
        rest = source - diag * current + first * across(current, 2) + across(first * current, -2)
        rest = rest + shape.coupled(current, second, third)
        fresh = current + carry * (current - previous) + push * (inverse * rest)
        current, previous = fresh, current
    return current


def bottom_prolong(ref, value):
    inner = lanes_of(32) % 8
    part = inner % 4
    back1, back2 = along(value, -1), along(value, -2)
    fore1, fore2 = along(value, 1), along(value, 2)
    low = jnp.where(part == 0, value, jnp.where(part == 3, back2, back1))
    high = jnp.where(part == 3, value, jnp.where(part == 0, fore2, fore1))
    left = inner < 4
    for offset in range(4):
        base = low if offset % 2 == 0 else high
        if offset < 2:
            moved = jnp.where(left, base, along(base, -4))
        else:
            moved = jnp.where(left, along(base, 4), base)
        ref[pl.ds(offset, 32, stride=4), :] = moved


def solve23(packed, rows2, parts2, one2, two2, tall):
    shape = Packed(ROWS2, 4, ROWS2, True)
    for number in range(3):
        for plane in range(DEPTH2):
            at = 8 * (plane // 2) + 2 * number + plane % 2
            rows2[number, plane] = packed[pl.ds(at, 8, stride=128), :]

    source2 = lambda plane: rows2[0, plane]
    beta2 = lambda plane: rows2[1, plane]
    absorb2 = lambda plane: rows2[2, plane]
    diag2, inverse2, first2, second2, third2 = parts2
    level2_parts(shape, beta2, absorb2, parts2)
    table = chebyshev_table(SWEEPS)
    for plane in range(DEPTH2):
        one2[plane] = table[0][1] * (inverse2[plane] * source2(plane))
        two2[plane] = jnp.zeros((ROWS2, LANES), jnp.float32)
    everywhere = [(0, DEPTH2)] * SWEEPS
    current, previous = sweep(
        shape, list(enumerate(table))[1:], source2, parts2, (one2, two2), everywhere, 0, DEPTH2
    )
    source3 = bottom_rows(
        tall.at[0],
        lambda plane: residual(
            shape, source2(plane), diag2, first2, second2, third2, current, plane, 0, DEPTH2
        ),
    )
    absorb3 = bottom_rows(tall.at[1], absorb2)
    beta3 = bottom_rows(tall.at[2], beta2)
    bottom_prolong(tall.at[0], bottom_solve(source3, absorb3, beta3))
    for plane in range(DEPTH2):
        pair = plane // 2
        current[plane] = current[plane] + tall[0, 8 * pair : 8 * pair + 8, :]
    current, previous = sweep(
        shape, list(enumerate(table)), source2, parts2, (current, previous), everywhere, 0, DEPTH2
    )
    return current


def post1(middle, sides, field, whole, region, parts, one, two, wide, tmp):
    inverse, first, second, third = parts
    gather_level1(region, middle, sides)
    shape = Packed(ROWS1, 2, ROWS1, False)
    level1_parts(shape, region, inverse, first, second, third)
    layer = position() // LAYER
    row = column_position() + 6
    zero = jnp.zeros((8, LANES), jnp.float32)
    for plane in range(DEPTH2 + 6):
        wide[plane, 0:8, :] = zero
        wide[plane, 16:24, :] = zero
        inside = 3 <= plane < DEPTH2 + 3
        wide[plane, 8:16, :] = whole[plane - 3] if inside else zero
    inner = lanes_of(8) % 4
    for pair in range(8):
        value = wide[2 * layer + pair, pl.ds(row, 8), :]
        moved = {steps: along(value, steps) for steps in range(-3, 4)}
        part = tmp.at[pair]
        for offset in range(4):
            picked = moved[offset]
            for lane in range(1, 4):
                picked = jnp.where(inner == lane, moved[offset - lane], picked)
            part[pl.ds(offset, 8, stride=4), :] = picked
        for plane in (2 * pair + 3, 2 * pair + 4):
            one[plane] = field[plane] + part[2:18, :]
    table = chebyshev_table(SWEEPS)
    ranges = [(3 + order, 19 - order) for order in range(1, SWEEPS + 1)]
    current, _ = sweep(
        shape, list(enumerate(table)), lambda plane: region[0, plane],
        (region.at[2], inverse, first, second, third), (one, two), ranges, -1, 99,
    )
    return current


def post0(pieces, field, coarse, out, region, parts, one, two, tmp):
    gather_level0(region, *pieces)
    member = position() % LAYER
    source = lambda plane: region[member + plane // 2, 0, plane % 2]
    absorb = lambda plane: region[member + plane // 2, 1, plane % 2]
    beta = lambda plane: region[member + plane // 2, 2, plane % 2]
    shape = Packed(ROWS0, 1, ROWS0, False)
    level0_parts(shape, beta, absorb, parts, 5, 13)
    even = lanes_of(8) % 2 == 0
    for pair in range(5):
        value = coarse[7 + member + pair, 4:12, :]
        upper_rows = jnp.where(even, value, along(value, -1))
        lower_rows = jnp.where(even, along(value, 1), value)
        part = tmp.at[pair]
        for offset in range(4):
            part[pl.ds(offset, 8, stride=4), :] = upper_rows if offset < 2 else lower_rows
        for plane in (2 * pair + 4, 2 * pair + 5):
            one[plane] = field[plane - 4] + part[...]
    table = chebyshev_table(SWEEPS)
    ranges = [(5 + order, 13 - order) for order in range(SWEEPS)]
    current, _ = sweep(
        shape, list(enumerate(table)), source, parts, (one, two), ranges, -1, 99
    )
    for plane in (8, 9):
        out[plane - 8] = current[plane][8:24, :]


def finish_kernel(
    packed, middle, sides1, field1, own, outer, sides0, field0, out,
    rows2, diag2, inverse2, first2, second2, third2, one2, two2, tall,
    region1, inverse1, first1, second1, third1, one1, two1, wide1, tmp1,
    region0, diag0, inverse0, first0, second0, third0, one0, two0, tmp0,
):
    parts2 = (diag2, inverse2, first2, second2, third2)
    whole = solve23(packed, rows2, parts2, one2, two2, tall)
    parts1 = (inverse1, first1, second1, third1)
    coarse = post1(
        middle, sides1, field1, whole, region1, parts1, one1, two1, wide1, tmp1
    )
    parts0 = (diag0, inverse0, first0, second0, third0)
    post0(
        (own, outer, sides0), field0, coarse, out, region0, parts0, one0, two0, tmp0
    )


def f32(*shape):
    return jax.ShapeDtypeStruct(shape, jnp.float32)


def buffer(*shape):
    return pltpu.VMEM(shape, jnp.float32)


def call(kernel, out, scratch, name, *operands):
    return pl.pallas_call(
        kernel,
        out_shape=out,
        scratch_shapes=scratch,
        name=name,
        compiler_params=pltpu.CompilerParams(vmem_limit_bytes=VMEM),
    )(*operands)


def pre0(*pieces):
    plane = buffer(24, ROWS0, LANES)
    scratch = [buffer(12, 3, 2, ROWS0, LANES)] + [plane] * 7 + [buffer(4, ROWS0, LANES)]
    out = (f32(10, ROWS0, LANES), f32(6, 3, 8, LANES), f32(4, 8, LANES))
    return call(pre0_kernel, out, scratch, "pre0", *pieces)


def pre1(*pieces):
    plane = buffer(DEPTH1, ROWS1, LANES)
    scratch = [buffer(3, DEPTH1, ROWS1, LANES)] + [plane] * 5
    scratch += [buffer(6, ROWS1, LANES), buffer(8, LANES)]
    out = (f32(16, 8, LANES), f32(DEPTH1, ROWS1, LANES))
    return call(pre1_kernel, out, scratch, "pre1", *pieces)


def finish(*pieces):
    plane2 = buffer(DEPTH2, ROWS2, LANES)
    plane1 = buffer(DEPTH1, ROWS1, LANES)
    plane0 = buffer(18, ROWS0, LANES)
    scratch = [buffer(3, DEPTH2, ROWS2, LANES)] + [plane2] * 7 + [buffer(3, 128, LANES)]
    scratch += [buffer(3, DEPTH1, ROWS1, LANES)] + [plane1] * 6
    scratch += [buffer(DEPTH2 + 6, 24, LANES), buffer(8, 32, LANES)]
    scratch += [buffer(12, 3, 2, ROWS0, LANES)] + [plane0] * 7 + [buffer(5, ROWS0, LANES)]
    return call(finish_kernel, f32(2, 16, LANES), scratch, "finish", *pieces)


def layers_apart(value, steps):
    count = lax.axis_size("gx")
    ways = [(i, i + (LAYER * steps if i % 2 == 0 else -LAYER * steps)) for i in range(count)]
    return lax.ppermute(value, "gx", [(i, j) for i, j in ways if 0 <= j < count])


def columns_apart(value):
    count, wide = lax.axis_size("gx"), lax.axis_size("gy")
    ways = [
        (i * wide + j, i * wide + j + (1 if i % 2 == 0 else -1))
        for i in range(count)
        for j in range(wide)
        if 0 <= j + (1 if i % 2 == 0 else -1) < wide
    ]
    return lax.ppermute(value, ("gx", "gy"), ways)


def body(source, absorb, beta):
    members = lax.axis_size("gx")
    across_y = lax.axis_size("gy")
    layers = members // LAYER
    near = [[LAYER * z + c for c in range(LAYER)] for z in range(layers)]
    chips = [[2 * chip, 2 * chip + 1] for chip in range(members // 2)]
    column = [[LAYER * z + c for z in range(layers)] for c in range(LAYER)]
    first_core = lax.axis_index("gx") % 2 == 0

    def both(value):
        return lax.all_gather(value, "gx", axis_index_groups=chips)

    local = jnp.stack([source, absorb, beta])
    own = lax.all_gather(local, "gx", axis_index_groups=near)
    outer = both(layers_apart(own, 1))
    edges = [jnp.where(first_core, x[..., 8:, :], x[..., :8, :]) for x in (outer[0], own, outer[1])]
    sides0 = both(columns_apart(jnp.stack(edges)))
    pieces0 = (own, outer, sides0)
    field0, tile, absorb1 = pre0(*pieces0)

    tiles = both(jnp.stack([layers_apart(tile, 1), layers_apart(tile, 2)]))
    middle = jnp.concatenate(
        [tiles[0, 1, 0:5], tiles[0, 0, 1:5], tile[1:5], tiles[1, 0, 1:5], tiles[1, 1, 1:6]]
    )
    pieces1 = (middle, both(columns_apart(middle)))
    pay, field1 = pre1(*pieces1, absorb1)

    rows = lax.all_to_all(pay, "gx", 0, 0, axis_index_groups=column)
    rows = jnp.broadcast_to(rows, (across_y,) + rows.shape)
    packed = lax.all_to_all(rows, "gy", 0, 0).reshape(-1, LANES)
    return finish(packed, *pieces1, field1, *pieces0, field0)


def solution(mesh):
    placed = (P("gx", "gy", None), P("gx", "gy", None), P("gx", "gy", None))
    return jax.shard_map(
        body, mesh=mesh, in_specs=placed, out_specs=P("gx", "gy", None), check_vma=False
    )
```

```python
import jax
import jax.numpy as jnp
from jax import lax
from jax.experimental import pallas as pl
from jax.experimental.pallas import tpu as pltpu
from jax.sharding import PartitionSpec as P

SWEEPS = 4
BOTTOM = 8
LANES = 128
VMEM = 24 * 1024 * 1024

LAYER = 4
PACK = (1, 2, 4, 8)


def face(level):
    return 0.5 * 0.25**level


def chebyshev_table(count):
    centre = 1.125
    half_width = 0.875
    ratio = centre / half_width
    factor = 1.0 / ratio
    table = [(0.0, 1.0 / centre)]
    for order in range(1, count):
        fresh_factor = 1.0 / (2.0 * ratio - factor)
        table.append((fresh_factor * factor, 2.0 * fresh_factor / half_width))
        factor = fresh_factor
    return table


def position():
    return lax.axis_index("gx")


def column_position():
    return lax.axis_index("gy")


def lanes_of(rows):
    return lax.broadcasted_iota(jnp.int32, (rows, LANES), 1)


def rows_of(rows):
    return lax.broadcasted_iota(jnp.int32, (rows, LANES), 0)


def along(value, steps):
    return pltpu.roll(value, (-steps) % LANES, 1)


def across(value, steps):
    rows = value.shape[0]
    return pltpu.roll(value, (-steps) % rows, 0)


class Packed:
    def __init__(self, rows, pack, period, whole):
        lane = lanes_of(rows)
        row = rows_of(rows) % period
        self.pack = pack
        self.inner = lane % pack
        self.third_last = lane >= LANES - pack
        self.third_first = lane < pack
        self.whole = whole
        self.second_last = (row == period - 1) & (self.inner == pack - 1)
        self.second_first = (row == 0) & (self.inner == 0)

    def second_up(self, value):
        if self.pack == 1:
            return across(value, 1)
        return jnp.where(
            self.inner < self.pack - 1, along(value, 1), across(along(value, 1 - self.pack), 1)
        )

    def second_down(self, value):
        if self.pack == 1:
            return across(value, -1)
        return jnp.where(
            self.inner > 0, along(value, -1), across(along(value, self.pack - 1), -1)
        )

    def faces(self, beta, half):
        up = self.second_up(beta)
        if self.whole:
            up = jnp.where(self.second_last, 0.0, up)
        second = half * (beta + up)
        down = self.second_down(beta)
        if self.whole:
            down = jnp.where(self.second_first, 0.0, down)
        share = half * (beta + down) + second
        if self.whole:
            second = jnp.where(self.second_last, 0.0, second)
        third_up = jnp.where(self.third_last, 0.0, along(beta, self.pack))
        third = half * (beta + third_up)
        third_down = jnp.where(self.third_first, 0.0, along(beta, -self.pack))
        share = share + half * (beta + third_down) + third
        return second, jnp.where(self.third_last, 0.0, third), share

    def coupled(self, value, second, third):
        total = second * self.second_up(value) + self.second_down(second * value)
        total = total + third * along(value, self.pack)
        return total + along(third * value, -self.pack)


def pair_sum(value, width):
    low = (lanes_of(value.shape[0]) & width) == 0
    return value + jnp.where(low, along(value, width), along(value, -width))


def residual(shape, source, diag, first, second, third, field, plane, low, high):
    here = field[plane]
    total = source - diag[plane] * here
    if plane + 1 < high:
        total = total + first[plane] * field[plane + 1]
    if plane > low:
        total = total + first[plane - 1] * field[plane - 1]
    return total + shape.coupled(here, second[plane], third[plane])


def sweep(shape, orders, source, parts, buffers, ranges, low, high):
    diag, inverse, first, second, third = parts
    current, previous = buffers
    for (order, (carry, push)), (start, stop) in zip(orders, ranges):
        for plane in range(start, stop):
            rest = residual(
                shape, source(plane), diag, first, second, third, current, plane, low, high
            )
            here = current[plane]
            fresh = here + push * (inverse[plane] * rest)
            if order > 0:
                fresh = fresh + carry * (here - previous[plane])
            previous[plane] = fresh
        current, previous = previous, current
    return current, previous


ROWS0 = 32


def level0_parts(shape, beta, absorb, parts, start, stop):
    diag, inverse, first, second, third = parts
    half = face(0)
    before = beta(start - 1)
    here = beta(start)
    lower = half * (before + here)
    first[start - 1] = lower
    for plane in range(start, stop):
        after = beta(plane + 1)
        upper = half * (here + after)
        first[plane] = upper
        second[plane], third[plane], share = shape.faces(here, half)
        total = absorb(plane) + lower + upper + share
        diag[plane] = total
        inverse[plane] = jnp.where(here > 0.0, 1.0 / total, 0.0)
        here, lower = after, upper


def coarse_rows(ref, value):
    ref[...] = pair_sum(value, 1)
    take = lambda offset: ref[pl.ds(offset, 8, stride=4), :]
    even = lanes_of(8) % 2 == 0
    return 0.125 * jnp.where(even, take(0) + take(1), take(2) + take(3))


KEPT0 = 10


def pre0_kernel(
    own, outer, kept_out, tile_out, absorb_out,
    diag, inverse, first, second, third, one, two, tmp,
):
    def piece(plane, kind):
        part, member = plane // 8, plane % 8 // 2
        block = own.at[member] if part == 1 else outer.at[part // 2, member]
        return block[kind, plane % 2]

    source = lambda plane: piece(plane, 0)
    absorb = lambda plane: piece(plane, 1)
    beta = lambda plane: piece(plane, 2)
    shape = Packed(ROWS0, 1, ROWS0, False)
    parts = (diag, inverse, first, second, third)
    level0_parts(shape, beta, absorb, parts, 1, 23)
    table = chebyshev_table(SWEEPS)
    for plane in range(1, 23):
        one[plane] = table[0][1] * (inverse[plane] * source(plane))
        two[plane] = jnp.zeros((ROWS0, LANES), jnp.float32)
    ranges = [(1 + order, 23 - order) for order in range(1, SWEEPS)]
    current, previous = sweep(
        shape, list(enumerate(table))[1:], source, parts, (one, two), ranges, -1, 99
    )
    for plane in range(4, 20):
        previous[plane] = source(plane)
    base = 2 * (position() % LAYER) + 4
    for plane in range(KEPT0):
        for number, kept in enumerate((current, previous) + parts):
            kept_out[number, plane] = kept[base + plane]
    coarse = Packed(8, 2, 8, False)
    half = face(1)
    betas = [coarse_rows(tmp.at[0], beta(p) + beta(p + 1)) for p in range(4, 20, 2)]
    for pair in range(6):
        plane = 6 + 2 * pair
        rest = [
            residual(shape, source(p), diag, first, second, third, current, p, -1, 99)
            for p in (plane, plane + 1)
        ]
        tile_out[pair, 0] = coarse_rows(tmp.at[1 + pair % 3], rest[0] + rest[1])
        here = betas[pair + 1]
        tile_out[pair, 1] = here
        wide = coarse_rows(tmp.at[1 + (pair + 1) % 3], absorb(plane) + absorb(plane + 1))
        _, _, share = coarse.faces(here, half)
        tile_out[pair, 2] = wide + half * (here + betas[pair]) + half * (here + betas[pair + 2]) + share
        if 0 < pair < 5:
            absorb_out[pair - 1] = wide


DEPTH1 = 22
ROWS1 = 16


def gather_level1(region, own, outer):
    zero = jnp.zeros((4, LANES), jnp.float32)
    for plane in range(DEPTH1):
        for kind in range(3):
            if 5 <= plane < 17:
                part, index = divmod(plane - 5, 4)
                if part == 1:
                    region[kind, plane] = own[index + 1, kind]
                else:
                    at = 6 * index + 2 * kind
                    region[kind, plane, 0:8, :] = outer[part // 2, at]
                    region[kind, plane, 8:16, :] = outer[part // 2, at + 1]
            else:
                part, index = (0, plane) if plane < 5 else (1, plane - 16)
                region[kind, plane, 0:4, :] = zero
                region[kind, plane, 4:12, :] = outer[part, 24 + 3 * index + kind]
                region[kind, plane, 12:16, :] = zero


def level1_parts(shape, region, inverse, first, second, third):
    half = face(1)
    for plane in range(DEPTH1):
        beta = region[1, plane]
        if plane + 1 < DEPTH1:
            first[plane] = half * (beta + region[1, plane + 1])
        if 0 < plane < DEPTH1 - 1:
            second[plane], third[plane], _ = shape.faces(beta, half)
        inverse[plane] = jnp.where(beta > 0.0, 1.0 / region[2, plane], 0.0)


def coarser_row(ref, value, start):
    ref[0 : value.shape[0], :] = pair_sum(pair_sum(value, 1), 2)
    inner = lanes_of(1) % 4
    total = ref[start : start + 1, :]
    for offset in range(1, 4):
        total = jnp.where(inner == offset, ref[start + offset : start + offset + 1, :], total)
    return 0.125 * total


def pre1_kernel(
    own, outer, absorb, pay_out, field, region, inverse, first, second, third,
    two, tmp, tile,
):
    gather_level1(region, own, outer)
    shape = Packed(ROWS1, 2, ROWS1, False)
    level1_parts(shape, region, inverse, first, second, third)
    diag = region.at[2]
    source = lambda plane: region[0, plane]
    parts = (diag, inverse, first, second, third)
    table = chebyshev_table(SWEEPS)
    for plane in range(DEPTH1):
        two[plane] = table[0][1] * (inverse[plane] * source(plane))
        field[plane] = jnp.zeros((ROWS1, LANES), jnp.float32)
    ranges = [(order, DEPTH1 - order) for order in range(1, SWEEPS)]
    current, _ = sweep(
        shape, list(enumerate(table))[1:], source, parts, (two, field), ranges, -1, 99
    )
    for pair in range(2):
        plane = 9 + 2 * pair
        rest = [
            residual(shape, source(p), diag, first, second, third, current, p, -1, 99)
            for p in (plane, plane + 1)
        ]
        tile[pair : pair + 1, :] = coarser_row(tmp.at[pair], rest[0] + rest[1], 6)
        tile[2 + pair : 3 + pair, :] = coarser_row(
            tmp.at[2 + pair], region[1, plane] + region[1, plane + 1], 6
        )
        tile[4 + pair : 5 + pair, :] = coarser_row(
            tmp.at[4 + pair], absorb[2 * pair] + absorb[2 * pair + 1], 2
        )
    tile[6:8, :] = jnp.zeros((2, LANES), jnp.float32)
    part = tile[pl.ds(2 * (position() % LAYER), 2), :]
    for slot in range(16):
        pay_out[slot] = part


DEPTH2 = 32
KIND_AT = (0, 2, 1)
ROWS2 = 8


def level2_parts(shape, beta, absorb, parts):
    diag, inverse, first, second, third = parts
    half = face(2)
    lower = half * beta(0)
    for plane in range(DEPTH2):
        here = beta(plane)
        upper = half * (here + beta(plane + 1)) if plane + 1 < DEPTH2 else half * here
        first[plane] = upper
        second[plane], third[plane], share = shape.faces(here, half)
        total = absorb(plane) + lower + upper + share
        diag[plane] = total
        inverse[plane] = 1.0 / total
        lower = upper


def bottom_rows(ref, planes):
    for pair in range(16):
        ref[8 * pair : 8 * pair + 8, :] = pair_sum(
            pair_sum(planes(2 * pair) + planes(2 * pair + 1), 1), 4
        )
    inner = lanes_of(32) % 8
    total = None
    for offset in range(4):
        value = ref[pl.ds(offset, 32, stride=4), :]
        moved = along(value, 1 if offset % 2 == 0 else -1)
        same = 2 * offset + offset % 2
        value = jnp.where(inner == same, value, moved)
        total = value if total is None else jnp.where(inner // 2 == offset, value, total)
    return 0.125 * total


def bottom_solve(source, absorb, beta):
    shape = Packed(32, 8, 2, True)
    half = face(3)
    plane = rows_of(32) // 2
    last, initial = plane == 15, plane == 0
    up = jnp.where(last, 0.0, across(beta, 2))
    down = jnp.where(initial, 0.0, across(beta, -2))
    second, third, share = shape.faces(beta, half)
    upper = half * (beta + up)
    diag = absorb + half * (beta + down) + upper + share
    first = jnp.where(last, 0.0, upper)
    inverse = 1.0 / diag
    table = chebyshev_table(BOTTOM)
    current = table[0][1] * (inverse * source)
    previous = jnp.zeros_like(current)
    for carry, push in table[1:]:
        rest = source - diag * current + first * across(current, 2) + across(first * current, -2)
        rest = rest + shape.coupled(current, second, third)
        fresh = current + carry * (current - previous) + push * (inverse * rest)
        current, previous = fresh, current
    return current


def bottom_prolong(ref, value):
    inner = lanes_of(32) % 8
    part = inner % 4
    back1, back2 = along(value, -1), along(value, -2)
    fore1, fore2 = along(value, 1), along(value, 2)
    low = jnp.where(part == 0, value, jnp.where(part == 3, back2, back1))
    high = jnp.where(part == 3, value, jnp.where(part == 0, fore2, fore1))
    left = inner < 4
    for offset in range(4):
        base = low if offset % 2 == 0 else high
        if offset < 2:
            moved = jnp.where(left, base, along(base, -4))
        else:
            moved = jnp.where(left, along(base, 4), base)
        ref[pl.ds(offset, 32, stride=4), :] = moved


def solve23(packed, rows2, parts2, one2, two2, tall):
    shape = Packed(ROWS2, 4, ROWS2, True)
    for number in range(3):
        for plane in range(DEPTH2):
            at = 256 * KIND_AT[number] + plane
            rows2[number, plane] = packed[pl.ds(at, 8, stride=32), :]

    source2 = lambda plane: rows2[0, plane]
    beta2 = lambda plane: rows2[1, plane]
    absorb2 = lambda plane: rows2[2, plane]
    diag2, inverse2, first2, second2, third2 = parts2
    level2_parts(shape, beta2, absorb2, parts2)
    table = chebyshev_table(SWEEPS)
    for plane in range(DEPTH2):
        one2[plane] = table[0][1] * (inverse2[plane] * source2(plane))
        two2[plane] = jnp.zeros((ROWS2, LANES), jnp.float32)
    everywhere = [(0, DEPTH2)] * SWEEPS
    current, previous = sweep(
        shape, list(enumerate(table))[1:], source2, parts2, (one2, two2), everywhere, 0, DEPTH2
    )
    source3 = bottom_rows(
        tall.at[0],
        lambda plane: residual(
            shape, source2(plane), diag2, first2, second2, third2, current, plane, 0, DEPTH2
        ),
    )
    absorb3 = bottom_rows(tall.at[1], absorb2)
    beta3 = bottom_rows(tall.at[2], beta2)
    bottom_prolong(tall.at[0], bottom_solve(source3, absorb3, beta3))
    for plane in range(DEPTH2):
        pair = plane // 2
        current[plane] = current[plane] + tall[0, 8 * pair : 8 * pair + 8, :]
    current, previous = sweep(
        shape, list(enumerate(table)), source2, parts2, (current, previous), everywhere, 0, DEPTH2
    )
    return current


def post1(field, whole, region, parts, one, two, wide, tmp):
    inverse, first, second, third = parts
    shape = Packed(ROWS1, 2, ROWS1, False)
    layer = position() // LAYER
    row = column_position() + 6
    zero = jnp.zeros((8, LANES), jnp.float32)
    for plane in range(DEPTH2 + 6):
        wide[plane, 0:8, :] = zero
        wide[plane, 16:24, :] = zero
        inside = 3 <= plane < DEPTH2 + 3
        wide[plane, 8:16, :] = whole[plane - 3] if inside else zero
    inner = lanes_of(8) % 4
    for pair in range(8):
        value = wide[2 * layer + pair, pl.ds(row, 8), :]
        moved = {steps: along(value, steps) for steps in range(-3, 4)}
        part = tmp.at[pair]
        for offset in range(4):
            picked = moved[offset]
            for lane in range(1, 4):
                picked = jnp.where(inner == lane, moved[offset - lane], picked)
            part[pl.ds(offset, 8, stride=4), :] = picked
        for plane in (2 * pair + 3, 2 * pair + 4):
            one[plane] = field[plane] + part[2:18, :]
    table = chebyshev_table(SWEEPS)
    ranges = [(3 + order, 19 - order) for order in range(1, SWEEPS + 1)]
    current, _ = sweep(
        shape, list(enumerate(table)), lambda plane: region[0, plane],
        (region.at[2], inverse, first, second, third), (one, two), ranges, -1, 99,
    )
    return current


def post0(kept, coarse, out, one, two, tmp):
    field, source = kept.at[0], kept.at[1]
    parts = tuple(kept.at[number] for number in range(2, 7))
    member = position() % LAYER
    shape = Packed(ROWS0, 1, ROWS0, False)
    even = lanes_of(8) % 2 == 0
    for pair in range(5):
        value = coarse[7 + member + pair, 4:12, :]
        upper_rows = jnp.where(even, value, along(value, -1))
        lower_rows = jnp.where(even, along(value, 1), value)
        part = tmp.at[pair]
        for offset in range(4):
            part[pl.ds(offset, 8, stride=4), :] = upper_rows if offset < 2 else lower_rows
        for plane in (2 * pair, 2 * pair + 1):
            one[plane] = field[plane] + part[...]
    table = chebyshev_table(SWEEPS)
    ranges = [(1 + order, KEPT0 - 1 - order) for order in range(SWEEPS)]
    current, _ = sweep(
        shape, list(enumerate(table)), lambda plane: source[plane], parts, (one, two), ranges,
        -1, 99,
    )
    for plane in (4, 5):
        out[plane - 4] = current[plane][8:24, :]


def finish_kernel(
    packed, field1, region1, inverse1, first1, second1, third1, kept0, out,
    rows2, diag2, inverse2, first2, second2, third2, one2, two2, tall,
    one1, two1, wide1, tmp1, one0, two0, tmp0,
):
    parts2 = (diag2, inverse2, first2, second2, third2)
    whole = solve23(packed, rows2, parts2, one2, two2, tall)
    parts1 = (inverse1, first1, second1, third1)
    coarse = post1(field1, whole, region1, parts1, one1, two1, wide1, tmp1)
    post0(kept0, coarse, out, one0, two0, tmp0)


def f32(*shape):
    return jax.ShapeDtypeStruct(shape, jnp.float32)


def buffer(*shape):
    return pltpu.VMEM(shape, jnp.float32)


def call(kernel, out, scratch, name, *operands):
    return pl.pallas_call(
        kernel,
        out_shape=out,
        scratch_shapes=scratch,
        name=name,
        compiler_params=pltpu.CompilerParams(vmem_limit_bytes=VMEM),
    )(*operands)


def pre0(*pieces):
    plane = buffer(24, ROWS0, LANES)
    scratch = [plane] * 7 + [buffer(4, ROWS0, LANES)]
    out = (f32(7, KEPT0, ROWS0, LANES), f32(6, 3, 8, LANES), f32(4, 8, LANES))
    return call(pre0_kernel, out, scratch, "pre0", *pieces)


def pre1(*pieces):
    plane = f32(DEPTH1, ROWS1, LANES)
    scratch = [buffer(DEPTH1, ROWS1, LANES), buffer(6, ROWS1, LANES), buffer(8, LANES)]
    out = (f32(16, 2, LANES), plane, f32(3, DEPTH1, ROWS1, LANES)) + (plane,) * 4
    return call(pre1_kernel, out, scratch, "pre1", *pieces)


def finish(*pieces):
    plane2 = buffer(DEPTH2, ROWS2, LANES)
    plane1 = buffer(DEPTH1, ROWS1, LANES)
    plane0 = buffer(KEPT0, ROWS0, LANES)
    scratch = [buffer(3, DEPTH2, ROWS2, LANES)] + [plane2] * 7 + [buffer(3, 128, LANES)]
    scratch += [plane1] * 2 + [buffer(DEPTH2 + 6, 24, LANES), buffer(8, 32, LANES)]
    scratch += [plane0] * 2 + [buffer(5, ROWS0, LANES)]
    return call(finish_kernel, f32(2, 16, LANES), scratch, "finish", *pieces)


def layers_apart(value, steps):
    count = lax.axis_size("gx")
    ways = [(i, i + (LAYER * steps if i % 2 == 0 else -LAYER * steps)) for i in range(count)]
    return lax.ppermute(value, "gx", [(i, j) for i, j in ways if 0 <= j < count])


def columns_apart(value):
    count, wide = lax.axis_size("gx"), lax.axis_size("gy")
    ways = [
        (i * wide + j, i * wide + j + (1 if i % 2 == 0 else -1))
        for i in range(count)
        for j in range(wide)
        if 0 <= j + (1 if i % 2 == 0 else -1) < wide
    ]
    return lax.ppermute(value, ("gx", "gy"), ways)


def body(source, absorb, beta):
    members = lax.axis_size("gx")
    wide = lax.axis_size("gy")
    layers = members // LAYER
    near = [[LAYER * z + c for c in range(LAYER)] for z in range(layers)]
    chips = [[2 * chip, 2 * chip + 1] for chip in range(members // 2)]
    column = [[LAYER * z + c for z in range(layers)] for c in range(LAYER)]
    cores = [
        [(LAYER * z + 2 * chip + core) * wide + y for chip in range(2) for y in range(wide)]
        for z in range(layers)
        for core in range(2)
    ]
    first_core = lax.axis_index("gx") % 2 == 0

    def both(value):
        return lax.all_gather(value, "gx", axis_index_groups=chips)

    local = jnp.stack([source, absorb, beta])
    own = lax.all_gather(local, "gx", axis_index_groups=near)
    edges = jnp.where(first_core, own[..., 8:, :], own[..., :8, :])
    sides = both(columns_apart(edges))
    layer = jnp.concatenate([sides[0], own, sides[1]], axis=-2)
    kept0, tile, absorb1 = pre0(layer, both(layers_apart(layer, 1)))

    sides = both(columns_apart(tile))
    tall = jnp.concatenate([sides[0, ..., 0:6, :], tile[..., 2:6, :], sides[1, ..., 2:8, :]], axis=-2)
    tiles = [layers_apart(tall[1:5], 1), layers_apart(tall[..., 4:12, :], 2)]
    tiles = jnp.concatenate([x.reshape(-1, 8, LANES) for x in tiles])
    pay, *kept1 = pre1(tall, both(tiles), absorb1)

    rows = lax.all_to_all(pay, "gx", 0, 0, axis_index_groups=column)
    rows = jnp.broadcast_to(rows, (2 * wide,) + rows.shape)
    rows = lax.all_to_all(rows, ("gx", "gy"), 0, 0, axis_index_groups=cores)
    packed = both(rows).reshape(-1, LANES)
    return finish(packed, *kept1, kept0)


def solution(mesh):
    placed = (P("gx", "gy", None), P("gx", "gy", None), P("gx", "gy", None))
    return jax.shard_map(
        body, mesh=mesh, in_specs=placed, out_specs=P("gx", "gy", None), check_vma=False
    )
```

```python
import jax
import jax.numpy as jnp
from jax import lax
from jax.experimental import pallas as pl
from jax.experimental.pallas import tpu as pltpu
from jax.sharding import PartitionSpec as P

SWEEPS = 4
BOTTOM = 8
LANES = 128
VMEM = 24 * 1024 * 1024

LAYER = 4
PACK = (1, 2, 4, 8)


def face(level):
    return 0.5 * 0.25**level


def chebyshev_table(count):
    centre = 1.125
    half_width = 0.875
    ratio = centre / half_width
    factor = 1.0 / ratio
    table = [(0.0, 1.0 / centre)]
    for order in range(1, count):
        fresh_factor = 1.0 / (2.0 * ratio - factor)
        table.append((fresh_factor * factor, 2.0 * fresh_factor / half_width))
        factor = fresh_factor
    return table


def position():
    return lax.axis_index("gx")


def column_position():
    return lax.axis_index("gy")


def lanes_of(rows):
    return lax.broadcasted_iota(jnp.int32, (rows, LANES), 1)


def rows_of(rows):
    return lax.broadcasted_iota(jnp.int32, (rows, LANES), 0)


def along(value, steps):
    return pltpu.roll(value, (-steps) % LANES, value.ndim - 1)


def across(value, steps):
    rows = value.shape[-2]
    return pltpu.roll(value, (-steps) % rows, value.ndim - 2)


class Packed:
    def __init__(self, pack, period, whole):
        self.pack = pack
        self.period = period
        self.whole = whole
        self.kept = {}

    def masks(self, value):
        if value.shape not in self.kept:
            pack, dims = self.pack, value.ndim
            lane = lax.broadcasted_iota(jnp.int32, value.shape, dims - 1)
            row = lax.broadcasted_iota(jnp.int32, value.shape, dims - 2) & (self.period - 1)
            inner = lane & (pack - 1)
            self.kept[value.shape] = dict(
                up=inner < pack - 1,
                down=inner > 0,
                third_last=lane >= LANES - pack,
                third_first=lane < pack,
                second_last=(row == self.period - 1) & (inner == pack - 1),
                second_first=(row == 0) & (inner == 0),
            )
        return self.kept[value.shape]

    def second_up(self, value):
        if self.pack == 1:
            return across(value, 1)
        mask = self.masks(value)["up"]
        return jnp.where(mask, along(value, 1), across(along(value, 1 - self.pack), 1))

    def second_down(self, value):
        if self.pack == 1:
            return across(value, -1)
        mask = self.masks(value)["down"]
        return jnp.where(mask, along(value, -1), across(along(value, self.pack - 1), -1))

    def faces(self, beta, half):
        mask = self.masks(beta)
        up = self.second_up(beta)
        if self.whole:
            up = jnp.where(mask["second_last"], 0.0, up)
        second = half * (beta + up)
        down = self.second_down(beta)
        if self.whole:
            down = jnp.where(mask["second_first"], 0.0, down)
        share = half * (beta + down) + second
        if self.whole:
            second = jnp.where(mask["second_last"], 0.0, second)
        third_up = jnp.where(mask["third_last"], 0.0, along(beta, self.pack))
        third = half * (beta + third_up)
        third_down = jnp.where(mask["third_first"], 0.0, along(beta, -self.pack))
        share = share + half * (beta + third_down) + third
        return second, jnp.where(mask["third_last"], 0.0, third), share

    def coupled(self, value, second, third):
        total = second * self.second_up(value) + self.second_down(second * value)
        total = total + third * along(value, self.pack)
        return total + along(third * value, -self.pack)


def pair_sum(value, width):
    low = (lax.broadcasted_iota(jnp.int32, value.shape, value.ndim - 1) & width) == 0
    return value + jnp.where(low, along(value, width), along(value, -width))


def residual(shape, source, parts, field, start, stop):
    diag, _, first, second, third = parts
    here = field[start:stop]
    total = source(start, stop) - diag[start:stop] * here
    total = total + first[start:stop] * field[start + 1 : stop + 1]
    total = total + first[start - 1 : stop - 1] * field[start - 1 : stop - 1]
    return total + shape.coupled(here, second[start:stop], third[start:stop])


def sweep(shape, orders, source, parts, buffers, ranges, chunk):
    inverse = parts[1]
    current, previous = buffers
    for (order, (carry, push)), (low, high) in zip(orders, ranges):
        for start in range(low, high, chunk):
            stop = min(start + chunk, high)
            rest = residual(shape, source, parts, current, start, stop)
            here = current[start:stop]
            fresh = here + push * (inverse[start:stop] * rest)
            if order > 0:
                fresh = fresh + carry * (here - previous[start:stop])
            previous[start:stop] = fresh
        current, previous = previous, current
    return current, previous


def begin(table, inverse, source, buffers, low, high, chunk):
    for start in range(low, high, chunk):
        stop = min(start + chunk, high)
        fresh = table[0][1] * (inverse[start:stop] * source(start, stop))
        buffers[0][start:stop] = fresh
        buffers[1][start:stop] = jnp.zeros_like(fresh)


ROWS0 = 32


CHUNK0 = 2


def level0_parts(shape, beta, absorb, parts, low, high):
    diag, inverse, first, second, third = parts
    half = face(0)
    first[low - 1 : low] = half * (beta(low - 1, low) + beta(low, low + 1))
    for start in range(low, high, CHUNK0):
        stop = min(start + CHUNK0, high)
        here = beta(start, stop)
        first[start:stop] = half * (here + beta(start + 1, stop + 1))
        lower = half * (beta(start - 1, stop - 1) + here)
        second[start:stop], third[start:stop], share = shape.faces(here, half)
        total = absorb(start, stop) + lower + first[start:stop] + share
        diag[start:stop] = total
        inverse[start:stop] = jnp.where(here > 0.0, 1.0 / total, 0.0)


def pairs(value):
    return jnp.stack([value[at] + value[at + 1] for at in range(0, value.shape[0], 2)])


def coarse_rows(ref, value):
    count = value.shape[0]
    ref[0:count] = pair_sum(value, 1)
    take = lambda offset: jnp.stack([ref[at, pl.ds(offset, 8, stride=4), :] for at in range(count)])
    even = (lax.broadcasted_iota(jnp.int32, (count, 8, LANES), 2) & 1) == 0
    return 0.125 * jnp.where(even, take(0) + take(1), take(2) + take(3))


KEPT0 = 10


def pre0_kernel(
    own, outer, kept_out, tile_out, absorb_out,
    diag, inverse, first, second, third, one, two, tmp,
):
    def piece(kind):
        def planes(start, stop):
            found = []
            for plane in range(start, stop):
                part, member = plane // 8, plane % 8 // 2
                block = own.at[member] if part == 1 else outer.at[part // 2, member]
                found.append(block[kind, plane % 2])
            return jnp.stack(found)

        return planes

    source, absorb, beta = piece(0), piece(1), piece(2)
    shape = Packed(1, ROWS0, False)
    parts = (diag, inverse, first, second, third)
    level0_parts(shape, beta, absorb, parts, 1, 23)
    table = chebyshev_table(SWEEPS)
    begin(table, inverse, source, (one, two), 1, 23, CHUNK0)
    ranges = [(1 + order, 23 - order) for order in range(1, SWEEPS)]
    current, previous = sweep(
        shape, list(enumerate(table))[1:], source, parts, (one, two), ranges, CHUNK0
    )
    previous[4:20] = source(4, 20)
    base = 2 * (position() % LAYER) + 4
    for plane in range(KEPT0):
        for number, kept in enumerate((current, previous) + parts):
            kept_out[number, plane] = kept[base + plane]
    coarse = Packed(2, 8, False)
    half = face(1)
    betas = coarse_rows(tmp.at[0:8], pairs(beta(4, 20)))
    wide = coarse_rows(tmp.at[8:14], pairs(absorb(6, 18)))
    rest = [residual(shape, source, parts, current, p, p + 2) for p in range(6, 18, 2)]
    tile_out[:, 0] = coarse_rows(tmp.at[14:20], jnp.stack([x[0] + x[1] for x in rest]))
    here = betas[1:7]
    _, _, share = coarse.faces(here, half)
    tile_out[:, 1] = here
    tile_out[:, 2] = wide + half * (here + betas[0:6]) + half * (here + betas[2:8]) + share
    absorb_out[...] = wide[1:5]


DEPTH1 = 22
ROWS1 = 16


def gather_level1(region, own, outer):
    zero = jnp.zeros((4, LANES), jnp.float32)
    for plane in range(DEPTH1):
        for kind in range(3):
            if 5 <= plane < 17:
                part, index = divmod(plane - 5, 4)
                if part == 1:
                    region[kind, plane] = own[index + 1, kind]
                else:
                    at = 6 * index + 2 * kind
                    region[kind, plane, 0:8, :] = outer[part // 2, at]
                    region[kind, plane, 8:16, :] = outer[part // 2, at + 1]
            else:
                part, index = (0, plane) if plane < 5 else (1, plane - 16)
                region[kind, plane, 0:4, :] = zero
                region[kind, plane, 4:12, :] = outer[part, 24 + 3 * index + kind]
                region[kind, plane, 12:16, :] = zero


CHUNK1 = 4


def level1_parts(shape, region, inverse, first, second, third):
    half = face(1)
    beta = region.at[1]
    for start in range(0, DEPTH1, CHUNK1):
        stop = min(start + CHUNK1, DEPTH1)
        here = beta[start:stop]
        second[start:stop], third[start:stop], _ = shape.faces(here, half)
        inverse[start:stop] = jnp.where(here > 0.0, 1.0 / region[2, start:stop], 0.0)
        stop = min(stop, DEPTH1 - 1)
        first[start:stop] = half * (beta[start:stop] + beta[start + 1 : stop + 1])


def coarser_rows(ref, value, start):
    ref[...] = pair_sum(pair_sum(value, 1), 2)
    inner = lanes_of(1) & 3
    rows = []
    for at in range(value.shape[0]):
        row = ref[at, start : start + 1, :]
        for offset in range(1, 4):
            row = jnp.where(inner == offset, ref[at, start + offset : start + offset + 1, :], row)
        rows.append(0.125 * row)
    return rows


def pre1_kernel(
    own, outer, absorb, pay_out, field, region, inverse, first, second, third,
    two, tmp, small, tile,
):
    gather_level1(region, own, outer)
    shape = Packed(2, ROWS1, False)
    level1_parts(shape, region, inverse, first, second, third)
    source = lambda start, stop: region[0, start:stop]
    parts = (region.at[2], inverse, first, second, third)
    table = chebyshev_table(SWEEPS)
    begin(table, inverse, source, (two, field), 0, DEPTH1, CHUNK1)
    ranges = [(order, DEPTH1 - order) for order in range(1, SWEEPS)]
    current, _ = sweep(
        shape, list(enumerate(table))[1:], source, parts, (two, field), ranges, CHUNK1
    )
    rest = residual(shape, source, parts, current, 9, 13)
    rows = coarser_rows(tmp, jnp.concatenate([pairs(rest), pairs(region[1, 9:13])]), 6)
    rows += coarser_rows(small, pairs(absorb[...]), 2)
    for at in range(6):
        tile[at : at + 1, :] = rows[at]
    tile[6:8, :] = jnp.zeros((2, LANES), jnp.float32)
    kind = 2 * (position() % LAYER)
    for side in range(2):
        part = tile[pl.ds(kind + side, 1), :]
        pay_out[:, side * LANES : (side + 1) * LANES] = jnp.broadcast_to(part, (16, LANES))


DEPTH2 = 32
KIND_AT = (0, 2, 1)
ROWS2 = 8


CHUNK2 = 4


def level2_parts(shape, beta, absorb, parts):
    diag, inverse, first, second, third = parts
    half = face(2)
    first[0:1] = jnp.zeros((1, ROWS2, LANES), jnp.float32)
    for start in range(1, DEPTH2 + 1, CHUNK2):
        stop = start + CHUNK2
        here = beta[start:stop]
        upper = half * (here + beta[start + 1 : stop + 1])
        lower = half * (here + beta[start - 1 : stop - 1])
        second[start:stop], third[start:stop], share = shape.faces(here, half)
        total = absorb[start:stop] + lower + upper + share
        first[start:stop] = upper
        diag[start:stop] = total
        inverse[start:stop] = 1.0 / total


def bottom_rows(ref, planes):
    value = planes(1, DEPTH2 + 1)
    value = jnp.concatenate([value[at] + value[at + 1] for at in range(0, DEPTH2, 2)])
    ref[...] = pair_sum(pair_sum(value, 1), 4)
    inner = lanes_of(32) & 7
    total = None
    for offset in range(4):
        value = jnp.concatenate(
            [ref[pl.ds(32 * block + offset, 8, stride=4), :] for block in range(4)]
        )
        moved = along(value, 1 if offset % 2 == 0 else -1)
        same = 2 * offset + offset % 2
        value = jnp.where(inner == same, value, moved)
        total = value if total is None else jnp.where(inner >> 1 == offset, value, total)
    return 0.125 * total


def bottom_solve(source, absorb, beta):
    shape = Packed(8, 2, True)
    half = face(3)
    row = rows_of(32)
    last, initial = row >= 30, row < 2
    up = jnp.where(last, 0.0, across(beta, 2))
    down = jnp.where(initial, 0.0, across(beta, -2))
    second, third, share = shape.faces(beta, half)
    upper = half * (beta + up)
    diag = absorb + half * (beta + down) + upper + share
    first = jnp.where(last, 0.0, upper)
    inverse = 1.0 / diag
    table = chebyshev_table(BOTTOM)
    current = table[0][1] * (inverse * source)
    previous = jnp.zeros_like(current)
    for carry, push in table[1:]:
        rest = source - diag * current + first * across(current, 2) + across(first * current, -2)
        rest = rest + shape.coupled(current, second, third)
        fresh = current + carry * (current - previous) + push * (inverse * rest)
        current, previous = fresh, current
    return current


def bottom_prolong(ref, value):
    inner = lanes_of(32) & 7
    part = inner & 3
    back1, back2 = along(value, -1), along(value, -2)
    fore1, fore2 = along(value, 1), along(value, 2)
    low = jnp.where(part == 0, value, jnp.where(part == 3, back2, back1))
    high = jnp.where(part == 3, value, jnp.where(part == 0, fore2, fore1))
    left = inner < 4
    for offset in range(4):
        base = low if offset % 2 == 0 else high
        if offset < 2:
            moved = jnp.where(left, base, along(base, -4))
        else:
            moved = jnp.where(left, along(base, 4), base)
        for block in range(4):
            ref[pl.ds(32 * block + offset, 8, stride=4), :] = moved[8 * block : 8 * block + 8]


def solve23(packed, halves, rows2, parts2, one2, two2, tall):
    shape = Packed(4, ROWS2, True)
    zero = jnp.zeros((ROWS2, LANES), jnp.float32)
    for side in range(2):
        halves[side] = packed[:, side * LANES : (side + 1) * LANES]
    for number in range(3):
        for plane in range(DEPTH2):
            at = 128 * KIND_AT[number] + plane // 2
            rows2[number, plane + 1] = halves[plane % 2, pl.ds(at, 8, stride=16), :]
    for ref in (rows2.at[1], one2, two2):
        ref[0] = zero
        ref[DEPTH2 + 1] = zero

    source2 = lambda start, stop: rows2[0, start:stop]
    level2_parts(shape, rows2.at[1], rows2.at[2], parts2)
    table = chebyshev_table(SWEEPS)
    begin(table, parts2[1], source2, (one2, two2), 1, DEPTH2 + 1, CHUNK2)
    everywhere = [(1, DEPTH2 + 1)] * SWEEPS
    current, previous = sweep(
        shape, list(enumerate(table))[1:], source2, parts2, (one2, two2), everywhere, CHUNK2
    )
    source3 = bottom_rows(
        tall.at[0], lambda start, stop: residual(shape, source2, parts2, current, start, stop)
    )
    absorb3 = bottom_rows(tall.at[1], lambda start, stop: rows2[2, start:stop])
    beta3 = bottom_rows(tall.at[2], lambda start, stop: rows2[1, start:stop])
    bottom_prolong(tall.at[0], bottom_solve(source3, absorb3, beta3))
    for plane in range(DEPTH2):
        pair = plane // 2
        current[plane + 1] = current[plane + 1] + tall[0, 8 * pair : 8 * pair + 8, :]
    current, previous = sweep(
        shape, list(enumerate(table)), source2, parts2, (current, previous), everywhere, CHUNK2
    )
    return current


def post1(field, whole, region, parts, one, two, wide, tmp):
    inverse, first, second, third = parts
    shape = Packed(2, ROWS1, False)
    layer = position() // LAYER
    row = column_position() + 6
    zero = jnp.zeros((8, LANES), jnp.float32)
    for plane in range(DEPTH2 + 6):
        wide[plane, 0:8, :] = zero
        wide[plane, 16:24, :] = zero
        inside = 3 <= plane < DEPTH2 + 3
        wide[plane, 8:16, :] = whole[plane - 2] if inside else zero
    value = jnp.stack([wide[2 * layer + pair, pl.ds(row, 8), :] for pair in range(8)])
    inner = lax.broadcasted_iota(jnp.int32, value.shape, 2) & 3
    moved = {steps: along(value, steps) for steps in range(-3, 4) if steps}
    moved[0] = value
    for offset in range(4):
        picked = moved[offset]
        for lane in range(1, 4):
            picked = jnp.where(inner == lane, moved[offset - lane], picked)
        for pair in range(8):
            tmp[pair, pl.ds(offset, 8, stride=4), :] = picked[pair]
    for plane in range(3, 19):
        one[plane] = field[plane] + tmp[(plane - 3) // 2, 2:18, :]
    table = chebyshev_table(SWEEPS)
    ranges = [(3 + order, 19 - order) for order in range(1, SWEEPS + 1)]
    current, _ = sweep(
        shape, list(enumerate(table)), lambda start, stop: region[0, start:stop],
        (region.at[2], inverse, first, second, third), (one, two), ranges, CHUNK1,
    )
    return current


def post0(kept, coarse, out, one, two, tmp):
    field, source = kept.at[0], kept.at[1]
    parts = tuple(kept.at[number] for number in range(2, 7))
    member = position() % LAYER
    shape = Packed(1, ROWS0, False)
    value = jnp.stack([coarse[7 + member + pair, 4:12, :] for pair in range(5)])
    even = (lax.broadcasted_iota(jnp.int32, value.shape, 2) & 1) == 0
    upper_rows = jnp.where(even, value, along(value, -1))
    lower_rows = jnp.where(even, along(value, 1), value)
    for pair in range(5):
        for offset in range(4):
            rows = upper_rows if offset < 2 else lower_rows
            tmp[pair, pl.ds(offset, 8, stride=4), :] = rows[pair]
    for plane in range(KEPT0):
        one[plane] = field[plane] + tmp[plane // 2]
    table = chebyshev_table(SWEEPS)
    ranges = [(1 + order, KEPT0 - 1 - order) for order in range(SWEEPS)]
    current, _ = sweep(
        shape, list(enumerate(table)), lambda start, stop: source[start:stop], parts,
        (one, two), ranges, CHUNK0,
    )
    for plane in (4, 5):
        out[plane - 4] = current[plane][8:24, :]


def finish_kernel(
    packed, field1, region1, inverse1, first1, second1, third1, kept0, out,
    halves, rows2, diag2, inverse2, first2, second2, third2, one2, two2, tall,
    one1, two1, wide1, tmp1, one0, two0, tmp0,
):
    parts2 = (diag2, inverse2, first2, second2, third2)
    whole = solve23(packed, halves, rows2, parts2, one2, two2, tall)
    parts1 = (inverse1, first1, second1, third1)
    coarse = post1(field1, whole, region1, parts1, one1, two1, wide1, tmp1)
    post0(kept0, coarse, out, one0, two0, tmp0)


def f32(*shape):
    return jax.ShapeDtypeStruct(shape, jnp.float32)


def buffer(*shape):
    return pltpu.VMEM(shape, jnp.float32)


def call(kernel, out, scratch, name, *operands):
    return pl.pallas_call(
        kernel,
        out_shape=out,
        scratch_shapes=scratch,
        name=name,
        compiler_params=pltpu.CompilerParams(vmem_limit_bytes=VMEM),
    )(*operands)


def pre0(*pieces):
    plane = buffer(24, ROWS0, LANES)
    scratch = [plane] * 7 + [buffer(20, ROWS0, LANES)]
    out = (f32(7, KEPT0, ROWS0, LANES), f32(6, 3, 8, LANES), f32(4, 8, LANES))
    return call(pre0_kernel, out, scratch, "pre0", *pieces)


def pre1(*pieces):
    plane = f32(DEPTH1, ROWS1, LANES)
    scratch = [buffer(DEPTH1, ROWS1, LANES), buffer(4, ROWS1, LANES), buffer(2, 8, LANES)]
    scratch += [buffer(8, LANES)]
    out = (f32(16, 2 * LANES), plane, f32(3, DEPTH1, ROWS1, LANES)) + (plane,) * 4
    return call(pre1_kernel, out, scratch, "pre1", *pieces)


def finish(*pieces):
    plane2 = buffer(DEPTH2 + 2, ROWS2, LANES)
    plane1 = buffer(DEPTH1, ROWS1, LANES)
    plane0 = buffer(KEPT0, ROWS0, LANES)
    scratch = [buffer(2, 512, LANES), buffer(3, DEPTH2 + 2, ROWS2, LANES)] + [plane2] * 7 + [buffer(3, 128, LANES)]
    scratch += [plane1] * 2 + [buffer(DEPTH2 + 6, 24, LANES), buffer(8, 32, LANES)]
    scratch += [plane0] * 2 + [buffer(5, ROWS0, LANES)]
    return call(finish_kernel, f32(2, 16, LANES), scratch, "finish", *pieces)


def layers_apart(value, steps):
    count = lax.axis_size("gx")
    ways = [(i, i + (LAYER * steps if i % 2 == 0 else -LAYER * steps)) for i in range(count)]
    return lax.ppermute(value, "gx", [(i, j) for i, j in ways if 0 <= j < count])


def columns_apart(value):
    count, wide = lax.axis_size("gx"), lax.axis_size("gy")
    ways = [
        (i * wide + j, i * wide + j + (1 if i % 2 == 0 else -1))
        for i in range(count)
        for j in range(wide)
        if 0 <= j + (1 if i % 2 == 0 else -1) < wide
    ]
    return lax.ppermute(value, ("gx", "gy"), ways)


def body(source, absorb, beta):
    members = lax.axis_size("gx")
    wide = lax.axis_size("gy")
    layers = members // LAYER
    near = [[LAYER * z + c for c in range(LAYER)] for z in range(layers)]
    chips = [[2 * chip, 2 * chip + 1] for chip in range(members // 2)]
    column = [[LAYER * z + c for z in range(layers)] for c in range(LAYER)]
    cores = [
        [(LAYER * z + 2 * chip + core) * wide + y for chip in range(2) for y in range(wide)]
        for z in range(layers)
        for core in range(2)
    ]
    first_core = lax.axis_index("gx") % 2 == 0

    def both(value):
        return lax.all_gather(value, "gx", axis_index_groups=chips)

    local = jnp.stack([source, absorb, beta])
    own = lax.all_gather(local, "gx", axis_index_groups=near)
    edges = jnp.where(first_core, own[..., 8:, :], own[..., :8, :])
    sides = both(columns_apart(edges))
    layer = jnp.concatenate([sides[0], own, sides[1]], axis=-2)
    kept0, tile, absorb1 = pre0(layer, both(layers_apart(layer, 1)))

    sides = both(columns_apart(tile))
    tall = jnp.concatenate([sides[0, ..., 0:6, :], tile[..., 2:6, :], sides[1, ..., 2:8, :]], axis=-2)
    tiles = [layers_apart(tall[1:5], 1), layers_apart(tall[..., 4:12, :], 2)]
    tiles = jnp.concatenate([x.reshape(-1, 8, LANES) for x in tiles])
    pay, *kept1 = pre1(tall, both(tiles), absorb1)

    rows = lax.all_to_all(pay, "gx", 0, 0, axis_index_groups=column)
    rows = jnp.broadcast_to(rows, (2 * wide,) + rows.shape)
    rows = lax.all_to_all(rows, ("gx", "gy"), 0, 0, axis_index_groups=cores)
    packed = both(rows).reshape(-1, 2 * LANES)
    return finish(packed, *kept1, kept0)


def solution(mesh):
    placed = (P("gx", "gy", None), P("gx", "gy", None), P("gx", "gy", None))
    return jax.shard_map(
        body, mesh=mesh, in_specs=placed, out_specs=P("gx", "gy", None), check_vma=False
    )
```

```python
import jax
import jax.numpy as jnp
from jax import lax
from jax.experimental import pallas as pl
from jax.experimental.pallas import tpu as pltpu
from jax.sharding import PartitionSpec as P

SWEEPS = 4
BOTTOM = 8
LANES = 128
VMEM = 24 * 1024 * 1024

LAYER = 4
PACK = (1, 2, 4, 8)


def face(level):
    return 0.5 * 0.25**level


def chebyshev_table(count):
    centre = 1.125
    half_width = 0.875
    ratio = centre / half_width
    factor = 1.0 / ratio
    table = [(0.0, 1.0 / centre)]
    for order in range(1, count):
        fresh_factor = 1.0 / (2.0 * ratio - factor)
        table.append((fresh_factor * factor, 2.0 * fresh_factor / half_width))
        factor = fresh_factor
    return table


def position():
    return lax.axis_index("gx")


def column_position():
    return lax.axis_index("gy")


def lanes_of(rows):
    return lax.broadcasted_iota(jnp.int32, (rows, LANES), 1)


def rows_of(rows):
    return lax.broadcasted_iota(jnp.int32, (rows, LANES), 0)


def along(value, steps):
    return pltpu.roll(value, (-steps) % LANES, value.ndim - 1)


def across(value, steps):
    rows = value.shape[-2]
    return pltpu.roll(value, (-steps) % rows, value.ndim - 2)


class Packed:
    def __init__(self, pack, period, whole):
        self.pack = pack
        self.period = period
        self.whole = whole
        self.kept = {}

    def masks(self, value):
        if value.shape not in self.kept:
            pack, dims = self.pack, value.ndim
            lane = lax.broadcasted_iota(jnp.int32, value.shape, dims - 1)
            row = lax.broadcasted_iota(jnp.int32, value.shape, dims - 2) & (self.period - 1)
            inner = lane & (pack - 1)
            self.kept[value.shape] = dict(
                up=inner < pack - 1,
                down=inner > 0,
                third_last=lane >= LANES - pack,
                third_first=lane < pack,
                second_last=(row == self.period - 1) & (inner == pack - 1),
                second_first=(row == 0) & (inner == 0),
            )
        return self.kept[value.shape]

    def second_up(self, value):
        if self.pack == 1:
            return across(value, 1)
        mask = self.masks(value)["up"]
        return jnp.where(mask, along(value, 1), across(along(value, 1 - self.pack), 1))

    def second_down(self, value):
        if self.pack == 1:
            return across(value, -1)
        mask = self.masks(value)["down"]
        return jnp.where(mask, along(value, -1), across(along(value, self.pack - 1), -1))

    def faces(self, beta, half):
        mask = self.masks(beta)
        up = self.second_up(beta)
        if self.whole:
            up = jnp.where(mask["second_last"], 0.0, up)
        second = half * (beta + up)
        down = self.second_down(beta)
        if self.whole:
            down = jnp.where(mask["second_first"], 0.0, down)
        share = half * (beta + down) + second
        if self.whole:
            second = jnp.where(mask["second_last"], 0.0, second)
        third_up = jnp.where(mask["third_last"], 0.0, along(beta, self.pack))
        third = half * (beta + third_up)
        third_down = jnp.where(mask["third_first"], 0.0, along(beta, -self.pack))
        share = share + half * (beta + third_down) + third
        return second, jnp.where(mask["third_last"], 0.0, third), share

    def coupled(self, value, second, third):
        total = second * self.second_up(value) + self.second_down(second * value)
        total = total + third * along(value, self.pack)
        return total + along(third * value, -self.pack)


def pair_sum(value, width):
    low = (lax.broadcasted_iota(jnp.int32, value.shape, value.ndim - 1) & width) == 0
    return value + jnp.where(low, along(value, width), along(value, -width))


def residual(shape, source, parts, field, start, stop):
    diag, _, first, second, third = parts
    here = field[start:stop]
    total = source(start, stop) - diag[start:stop] * here
    total = total + first[start:stop] * field[start + 1 : stop + 1]
    total = total + first[start - 1 : stop - 1] * field[start - 1 : stop - 1]
    return total + shape.coupled(here, second[start:stop], third[start:stop])


def sweep(shape, orders, source, parts, buffers, ranges, chunk):
    inverse = parts[1]
    current, previous = buffers
    for (order, (carry, push)), (low, high) in zip(orders, ranges):
        for start in range(low, high, chunk):
            stop = min(start + chunk, high)
            rest = residual(shape, source, parts, current, start, stop)
            here = current[start:stop]
            fresh = here + push * (inverse[start:stop] * rest)
            if order > 0:
                fresh = fresh + carry * (here - previous[start:stop])
            previous[start:stop] = fresh
        current, previous = previous, current
    return current, previous


def begin(table, inverse, source, buffers, low, high, chunk):
    for start in range(low, high, chunk):
        stop = min(start + chunk, high)
        fresh = table[0][1] * (inverse[start:stop] * source(start, stop))
        buffers[0][start:stop] = fresh
        buffers[1][start:stop] = jnp.zeros_like(fresh)


ROWS0 = 48


CHUNK0 = 2


def level0_parts(shape, beta, absorb, parts, low, high):
    diag, inverse, first, second, third = parts
    half = face(0)
    first[low - 1 : low] = half * (beta(low - 1, low) + beta(low, low + 1))
    for start in range(low, high, CHUNK0):
        stop = min(start + CHUNK0, high)
        here = beta(start, stop)
        first[start:stop] = half * (here + beta(start + 1, stop + 1))
        lower = half * (beta(start - 1, stop - 1) + here)
        second[start:stop], third[start:stop], share = shape.faces(here, half)
        total = absorb(start, stop) + lower + first[start:stop] + share
        diag[start:stop] = total
        inverse[start:stop] = jnp.where(here > 0.0, 1.0 / total, 0.0)


def pairs(value):
    return jnp.stack([value[at] + value[at + 1] for at in range(0, value.shape[0], 2)])


def coarse_rows(ref, value):
    count = value.shape[0]
    zero = jnp.zeros((count, 8, LANES), jnp.float32)
    ref[0:count, 0:8, :] = zero
    ref[0:count, 8:56, :] = pair_sum(value, 1)
    ref[0:count, 56:64, :] = zero

    def take(offset):
        halves = [
            [ref[at, pl.ds(32 * half + offset, 8, stride=4), :] for half in range(2)]
            for at in range(count)
        ]
        return jnp.stack([jnp.concatenate(both) for both in halves])

    even = (lax.broadcasted_iota(jnp.int32, (count, ROWS1, LANES), 2) & 1) == 0
    return 0.125 * jnp.where(even, take(0) + take(1), take(2) + take(3))


KEPT0 = 10
KEPT_ROWS0 = 32


def pre0_kernel(
    own, outer, kept_out, tile_out, absorb_out,
    diag, inverse, first, second, third, one, two, tmp,
):
    def piece(kind):
        def planes(start, stop):
            found = []
            for plane in range(start, stop):
                part, member = plane // 8, plane % 8 // 2
                block = own.at[member] if part == 1 else outer.at[part // 2, member]
                found.append(block[kind, plane % 2])
            return jnp.stack(found)

        return planes

    source, absorb, beta = piece(0), piece(1), piece(2)
    shape = Packed(1, ROWS0, False)
    parts = (diag, inverse, first, second, third)
    level0_parts(shape, beta, absorb, parts, 1, 23)
    table = chebyshev_table(SWEEPS)
    begin(table, inverse, source, (one, two), 1, 23, CHUNK0)
    ranges = [(1 + order, 23 - order) for order in range(1, SWEEPS)]
    current, previous = sweep(
        shape, list(enumerate(table))[1:], source, parts, (one, two), ranges, CHUNK0
    )
    previous[4:20] = source(4, 20)
    base = 2 * (position() % LAYER) + 4
    for plane in range(KEPT0):
        for number, kept in enumerate((current, previous) + parts):
            kept_out[number, plane] = kept[base + plane, 8:40, :]
    coarse = Packed(2, ROWS1, False)
    half = face(1)
    betas = coarse_rows(tmp.at[0:8], pairs(beta(4, 20)))
    wide = coarse_rows(tmp.at[8:14], pairs(absorb(6, 18)))
    rest = [residual(shape, source, parts, current, p, p + 2) for p in range(6, 18, 2)]
    tile_out[:, 0] = coarse_rows(tmp.at[14:20], jnp.stack([x[0] + x[1] for x in rest]))
    here = betas[1:7]
    _, _, share = coarse.faces(here, half)
    tile_out[:, 1] = here
    tile_out[:, 2] = wide + half * (here + betas[0:6]) + half * (here + betas[2:8]) + share
    absorb_out[...] = wide[1:5]


DEPTH1 = 22
ROWS1 = 16


def gather_level1(region, own, outer):
    zero = jnp.zeros((4, LANES), jnp.float32)
    for plane in range(DEPTH1):
        for kind in range(3):
            if 5 <= plane < 17:
                part, index = divmod(plane - 5, 4)
                if part == 1:
                    region[kind, plane] = own[index + 1, kind]
                else:
                    at = 6 * index + 2 * kind
                    region[kind, plane, 0:8, :] = outer[part // 2, at]
                    region[kind, plane, 8:16, :] = outer[part // 2, at + 1]
            else:
                part, index = (0, plane) if plane < 5 else (1, plane - 16)
                region[kind, plane, 0:4, :] = zero
                region[kind, plane, 4:12, :] = outer[part, 24 + 3 * index + kind]
                region[kind, plane, 12:16, :] = zero


CHUNK1 = 4


def level1_parts(shape, region, inverse, first, second, third):
    half = face(1)
    beta = region.at[1]
    for start in range(0, DEPTH1, CHUNK1):
        stop = min(start + CHUNK1, DEPTH1)
        here = beta[start:stop]
        second[start:stop], third[start:stop], _ = shape.faces(here, half)
        inverse[start:stop] = jnp.where(here > 0.0, 1.0 / region[2, start:stop], 0.0)
        stop = min(stop, DEPTH1 - 1)
        first[start:stop] = half * (beta[start:stop] + beta[start + 1 : stop + 1])


def coarser_rows(ref, value, start):
    ref[...] = pair_sum(pair_sum(value, 1), 2)
    inner = lanes_of(1) & 3
    rows = []
    for at in range(value.shape[0]):
        row = ref[at, start : start + 1, :]
        for offset in range(1, 4):
            row = jnp.where(inner == offset, ref[at, start + offset : start + offset + 1, :], row)
        rows.append(0.125 * row)
    return rows


def pre1_kernel(
    own, outer, absorb, pay_out, rows_out, field, region, inverse, first, second, third,
    two, tmp, tile,
):
    gather_level1(region, own, outer)
    shape = Packed(2, ROWS1, False)
    level1_parts(shape, region, inverse, first, second, third)
    source = lambda start, stop: region[0, start:stop]
    parts = (region.at[2], inverse, first, second, third)
    table = chebyshev_table(SWEEPS)
    begin(table, inverse, source, (two, field), 0, DEPTH1, CHUNK1)
    ranges = [(order, DEPTH1 - order) for order in range(1, SWEEPS)]
    current, _ = sweep(
        shape, list(enumerate(table))[1:], source, parts, (two, field), ranges, CHUNK1
    )
    rest = residual(shape, source, parts, current, 9, 13)
    totals = [pairs(rest), pairs(region[1, 9:13]), pairs(absorb[...])]
    rows = coarser_rows(tmp, jnp.concatenate(totals), 6)
    for at in range(6):
        tile[at : at + 1, :] = rows[at]
    tile[6:8, :] = jnp.zeros((2, LANES), jnp.float32)
    kind = 2 * (position() % LAYER)
    for side in range(2):
        part = tile[pl.ds(kind + side, 1), :]
        pay_out[:, side * LANES : (side + 1) * LANES] = jnp.broadcast_to(part, (16, LANES))
    base = 3 + 4 * (position() % LAYER)
    for plane in range(4):
        row, lane = 4 * (plane % 2), plane // 2 * LANES
        rows_out[row : row + 4, lane : lane + LANES] = current[base + plane, 6:10, :]


DEPTH2 = 32
KIND_AT = (0, 2, 1)
ROWS2 = 8


CHUNK2 = 4


def level2_parts(shape, beta, absorb, parts):
    diag, inverse, first, second, third = parts
    half = face(2)
    first[0:1] = jnp.zeros((1, ROWS2, LANES), jnp.float32)
    for start in range(1, DEPTH2 + 1, CHUNK2):
        stop = start + CHUNK2
        here = beta[start:stop]
        upper = half * (here + beta[start + 1 : stop + 1])
        lower = half * (here + beta[start - 1 : stop - 1])
        second[start:stop], third[start:stop], share = shape.faces(here, half)
        total = absorb[start:stop] + lower + upper + share
        first[start:stop] = upper
        diag[start:stop] = total
        inverse[start:stop] = 1.0 / total


def bottom_rows(ref, planes):
    value = planes(1, DEPTH2 + 1)
    value = jnp.concatenate([value[at] + value[at + 1] for at in range(0, DEPTH2, 2)])
    ref[...] = pair_sum(pair_sum(value, 1), 4)
    inner = lanes_of(32) & 7
    total = None
    for offset in range(4):
        value = jnp.concatenate(
            [ref[pl.ds(32 * block + offset, 8, stride=4), :] for block in range(4)]
        )
        moved = along(value, 1 if offset % 2 == 0 else -1)
        same = 2 * offset + offset % 2
        value = jnp.where(inner == same, value, moved)
        total = value if total is None else jnp.where(inner >> 1 == offset, value, total)
    return 0.125 * total


def bottom_solve(source, absorb, beta):
    shape = Packed(8, 2, True)
    half = face(3)
    row = rows_of(32)
    last, initial = row >= 30, row < 2
    up = jnp.where(last, 0.0, across(beta, 2))
    down = jnp.where(initial, 0.0, across(beta, -2))
    second, third, share = shape.faces(beta, half)
    upper = half * (beta + up)
    diag = absorb + half * (beta + down) + upper + share
    first = jnp.where(last, 0.0, upper)
    inverse = 1.0 / diag
    table = chebyshev_table(BOTTOM)
    current = table[0][1] * (inverse * source)
    previous = jnp.zeros_like(current)
    for carry, push in table[1:]:
        rest = source - diag * current + first * across(current, 2) + across(first * current, -2)
        rest = rest + shape.coupled(current, second, third)
        fresh = current + carry * (current - previous) + push * (inverse * rest)
        current, previous = fresh, current
    return current


def bottom_prolong(ref, value):
    inner = lanes_of(32) & 7
    part = inner & 3
    back1, back2 = along(value, -1), along(value, -2)
    fore1, fore2 = along(value, 1), along(value, 2)
    low = jnp.where(part == 0, value, jnp.where(part == 3, back2, back1))
    high = jnp.where(part == 3, value, jnp.where(part == 0, fore2, fore1))
    left = inner < 4
    for offset in range(4):
        base = low if offset % 2 == 0 else high
        if offset < 2:
            moved = jnp.where(left, base, along(base, -4))
        else:
            moved = jnp.where(left, along(base, 4), base)
        for block in range(4):
            ref[pl.ds(32 * block + offset, 8, stride=4), :] = moved[8 * block : 8 * block + 8]


def solve23(packed, halves, rows2, parts2, one2, two2, tall):
    shape = Packed(4, ROWS2, True)
    zero = jnp.zeros((ROWS2, LANES), jnp.float32)
    for peer in range(32):
        for side in range(2):
            halves[side, 16 * peer : 16 * peer + 16, :] = packed[
                peer, 0:16, side * LANES : (side + 1) * LANES
            ]
    for number in range(3):
        for plane in range(DEPTH2):
            at = 128 * KIND_AT[number] + plane // 2
            rows2[number, plane + 1] = halves[plane % 2, pl.ds(at, 8, stride=16), :]
    for ref in (rows2.at[1], one2, two2):
        ref[0] = zero
        ref[DEPTH2 + 1] = zero

    source2 = lambda start, stop: rows2[0, start:stop]
    level2_parts(shape, rows2.at[1], rows2.at[2], parts2)
    table = chebyshev_table(SWEEPS)
    begin(table, parts2[1], source2, (one2, two2), 1, DEPTH2 + 1, CHUNK2)
    everywhere = [(1, DEPTH2 + 1)] * SWEEPS
    current, previous = sweep(
        shape, list(enumerate(table))[1:], source2, parts2, (one2, two2), everywhere, CHUNK2
    )
    source3 = bottom_rows(
        tall.at[0], lambda start, stop: residual(shape, source2, parts2, current, start, stop)
    )
    absorb3 = bottom_rows(tall.at[1], lambda start, stop: rows2[2, start:stop])
    beta3 = bottom_rows(tall.at[2], lambda start, stop: rows2[1, start:stop])
    bottom_prolong(tall.at[0], bottom_solve(source3, absorb3, beta3))
    for plane in range(DEPTH2):
        pair = plane // 2
        current[plane + 1] = current[plane + 1] + tall[0, 8 * pair : 8 * pair + 8, :]
    current, previous = sweep(
        shape, list(enumerate(table)), source2, parts2, (current, previous), everywhere, CHUNK2
    )
    return current


def post1(packed, field, whole, region, parts, one, two, wide, tmp):
    inverse, first, second, third = parts
    shape = Packed(2, ROWS1, False)
    layer = position() // LAYER
    row = column_position() + 6
    zero = jnp.zeros((8, LANES), jnp.float32)
    for plane in range(DEPTH2 + 6):
        wide[plane, 0:8, :] = zero
        wide[plane, 16:24, :] = zero
        inside = 3 <= plane < DEPTH2 + 3
        wide[plane, 8:16, :] = whole[plane - 2] if inside else zero
    value = jnp.stack([wide[2 * layer + pair, pl.ds(row, 8), :] for pair in range(8)])
    inner = lax.broadcasted_iota(jnp.int32, value.shape, 2) & 3
    moved = {steps: along(value, steps) for steps in range(-3, 4) if steps}
    moved[0] = value
    for offset in range(4):
        picked = moved[offset]
        for lane in range(1, 4):
            picked = jnp.where(inner == lane, moved[offset - lane], picked)
        for pair in range(8):
            tmp[pair, pl.ds(offset, 8, stride=4), :] = picked[pair]
    place = column_position()
    before, after = jnp.maximum(place - 1, 0), jnp.minimum(place + 1, 7)
    has_before = jnp.where(place > 0, 1.0, 0.0)
    has_after = jnp.where(place < 7, 1.0, 0.0)
    row = lax.broadcasted_iota(jnp.int32, (2, 8, LANES), 1)
    inside = (row >= 2) & (row < 6)

    def neighbour(start, who, there):
        member, half = divmod((start - 3) // 2, 2)
        at = 16 * (member % 2) + 8 * (member // 2)
        value = there * packed[at + who, 16:24, half * LANES : (half + 1) * LANES]
        return jnp.stack([across(value, -2), across(value, 2)])

    for start in range(3, 19, 2):
        here = field[start : start + 2]
        upper = jnp.where(inside, neighbour(start, before, has_before), here[:, 0:8])
        lower = jnp.where(inside, neighbour(start, after, has_after), here[:, 8:16])
        one[start : start + 2] = jnp.concatenate([upper, lower], 1) + tmp[(start - 3) // 2, 2:18, :]
    table = chebyshev_table(SWEEPS)
    ranges = [(3 + order, 19 - order) for order in range(1, SWEEPS + 1)]
    current, _ = sweep(
        shape, list(enumerate(table)), lambda start, stop: region[0, start:stop],
        (region.at[2], inverse, first, second, third), (one, two), ranges, CHUNK1,
    )
    return current


def post0(kept, coarse, out, one, two, tmp):
    field, source = kept.at[0], kept.at[1]
    parts = tuple(kept.at[number] for number in range(2, 7))
    member = position() % LAYER
    shape = Packed(1, ROWS0, False)
    value = jnp.stack([coarse[7 + member + pair, 4:12, :] for pair in range(5)])
    even = (lax.broadcasted_iota(jnp.int32, value.shape, 2) & 1) == 0
    upper_rows = jnp.where(even, value, along(value, -1))
    lower_rows = jnp.where(even, along(value, 1), value)
    for pair in range(5):
        for offset in range(4):
            rows = upper_rows if offset < 2 else lower_rows
            tmp[pair, pl.ds(offset, 8, stride=4), :] = rows[pair]
    for plane in range(KEPT0):
        one[plane] = field[plane] + tmp[plane // 2]
    table = chebyshev_table(SWEEPS)
    ranges = [(1 + order, KEPT0 - 1 - order) for order in range(SWEEPS)]
    current, _ = sweep(
        shape, list(enumerate(table)), lambda start, stop: source[start:stop], parts,
        (one, two), ranges, CHUNK0,
    )
    out[...] = current[4:6, 8:24, :]


def finish_kernel(
    packed, field1, region1, inverse1, first1, second1, third1, kept0, out,
    halves, rows2, diag2, inverse2, first2, second2, third2, one2, two2, tall,
    one1, two1, wide1, tmp1, one0, two0, tmp0,
):
    parts2 = (diag2, inverse2, first2, second2, third2)
    whole = solve23(packed, halves, rows2, parts2, one2, two2, tall)
    parts1 = (inverse1, first1, second1, third1)
    coarse = post1(packed, field1, whole, region1, parts1, one1, two1, wide1, tmp1)
    post0(kept0, coarse, out, one0, two0, tmp0)


def f32(*shape):
    return jax.ShapeDtypeStruct(shape, jnp.float32)


def buffer(*shape):
    return pltpu.VMEM(shape, jnp.float32)


def call(kernel, out, scratch, name, *operands):
    return pl.pallas_call(
        kernel,
        out_shape=out,
        scratch_shapes=scratch,
        name=name,
        compiler_params=pltpu.CompilerParams(vmem_limit_bytes=VMEM),
    )(*operands)


def pre0(*pieces):
    plane = buffer(24, ROWS0, LANES)
    scratch = [plane] * 7 + [buffer(20, 64, LANES)]
    out = (f32(7, KEPT0, KEPT_ROWS0, LANES), f32(6, 3, ROWS1, LANES), f32(4, ROWS1, LANES))
    return call(pre0_kernel, out, scratch, "pre0", *pieces)


def pre1(*pieces):
    plane = f32(DEPTH1, ROWS1, LANES)
    scratch = [buffer(DEPTH1, ROWS1, LANES), buffer(6, ROWS1, LANES), buffer(8, LANES)]
    out = (f32(16, 2 * LANES), f32(8, 2 * LANES), plane, f32(3, DEPTH1, ROWS1, LANES)) + (plane,) * 4
    return call(pre1_kernel, out, scratch, "pre1", *pieces)


def finish(*pieces):
    plane2 = buffer(DEPTH2 + 2, ROWS2, LANES)
    plane1 = buffer(DEPTH1, ROWS1, LANES)
    plane0 = buffer(KEPT0, KEPT_ROWS0, LANES)
    scratch = [buffer(2, 512, LANES), buffer(3, DEPTH2 + 2, ROWS2, LANES)] + [plane2] * 7 + [buffer(3, 128, LANES)]
    scratch += [plane1] * 2 + [buffer(DEPTH2 + 6, 24, LANES), buffer(8, 32, LANES)]
    scratch += [plane0] * 2 + [buffer(5, KEPT_ROWS0, LANES)]
    return call(finish_kernel, f32(2, 16, LANES), scratch, "finish", *pieces)


def layers_apart(value, steps):
    count = lax.axis_size("gx")
    ways = [(i, i + (LAYER * steps if i % 2 == 0 else -LAYER * steps)) for i in range(count)]
    return lax.ppermute(value, "gx", [(i, j) for i, j in ways if 0 <= j < count])


def columns_apart(value):
    count, wide = lax.axis_size("gx"), lax.axis_size("gy")
    ways = [
        (i * wide + j, i * wide + j + (1 if i % 2 == 0 else -1))
        for i in range(count)
        for j in range(wide)
        if 0 <= j + (1 if i % 2 == 0 else -1) < wide
    ]
    return lax.ppermute(value, ("gx", "gy"), ways)


def body(source, absorb, beta):
    members = lax.axis_size("gx")
    wide = lax.axis_size("gy")
    layers = members // LAYER
    near = [[LAYER * z + c for c in range(LAYER)] for z in range(layers)]
    chips = [[2 * chip, 2 * chip + 1] for chip in range(members // 2)]
    column = [[LAYER * z + c for z in range(layers)] for c in range(LAYER)]
    cores = [
        [(LAYER * z + 2 * chip + core) * wide + y for chip in range(2) for y in range(wide)]
        for z in range(layers)
        for core in range(2)
    ]
    def both(value):
        return lax.all_gather(value, "gx", axis_index_groups=chips)

    local = jnp.stack([source, absorb, beta])
    own = lax.all_gather(local, "gx", axis_index_groups=near)
    sides = both(columns_apart(own))
    layer = jnp.concatenate([sides[0], own, sides[1]], axis=-2)
    kept0, tile, absorb1 = pre0(layer, both(layers_apart(layer, 1)))

    tiles = [layers_apart(tile[1:5], 1), layers_apart(tile[..., 4:12, :], 2)]
    tiles = jnp.concatenate([x.reshape(-1, 8, LANES) for x in tiles])
    pay, rows1, *kept1 = pre1(tile, both(tiles), absorb1)

    rows = lax.all_to_all(pay, "gx", 0, 0, axis_index_groups=column)
    rows = jnp.concatenate([rows, rows1])
    rows = jnp.broadcast_to(rows, (2 * wide,) + rows.shape)
    rows = lax.all_to_all(rows, ("gx", "gy"), 0, 0, axis_index_groups=cores)
    packed = both(rows).reshape(-1, *rows.shape[1:])
    return finish(packed, *kept1, kept0)


def solution(mesh):
    placed = (P("gx", "gy", None), P("gx", "gy", None), P("gx", "gy", None))
    return jax.shard_map(
        body, mesh=mesh, in_specs=placed, out_specs=P("gx", "gy", None), check_vma=False
    )
```

```python
import jax
import jax.numpy as jnp
from jax import lax
from jax.experimental import pallas as pl
from jax.experimental.pallas import tpu as pltpu
from jax.sharding import PartitionSpec as P

SWEEPS = 4
BOTTOM = 8
LANES = 128
VMEM = 24 * 1024 * 1024

LAYER = 4
PACK = (1, 2, 4, 8)


def face(level):
    return 0.5 * 0.25**level


def chebyshev_table(count):
    centre = 1.125
    half_width = 0.875
    ratio = centre / half_width
    factor = 1.0 / ratio
    table = [(0.0, 1.0 / centre)]
    for order in range(1, count):
        fresh_factor = 1.0 / (2.0 * ratio - factor)
        table.append((fresh_factor * factor, 2.0 * fresh_factor / half_width))
        factor = fresh_factor
    return table


def position():
    return lax.axis_index("gx")


def column_position():
    return lax.axis_index("gy")


def lanes_of(rows):
    return lax.broadcasted_iota(jnp.int32, (rows, LANES), 1)


def rows_of(rows):
    return lax.broadcasted_iota(jnp.int32, (rows, LANES), 0)


def along(value, steps):
    return pltpu.roll(value, (-steps) % LANES, value.ndim - 1)


def across(value, steps):
    rows = value.shape[-2]
    return pltpu.roll(value, (-steps) % rows, value.ndim - 2)


class Packed:
    def __init__(self, pack, period, whole):
        self.pack = pack
        self.period = period
        self.whole = whole
        self.kept = {}

    def masks(self, value):
        if value.shape not in self.kept:
            pack, dims = self.pack, value.ndim
            lane = lax.broadcasted_iota(jnp.int32, value.shape, dims - 1)
            row = lax.broadcasted_iota(jnp.int32, value.shape, dims - 2) & (self.period - 1)
            inner = lane & (pack - 1)
            self.kept[value.shape] = dict(
                up=inner < pack - 1,
                down=inner > 0,
                third_last=lane >= LANES - pack,
                third_first=lane < pack,
                second_last=(row == self.period - 1) & (inner == pack - 1),
                second_first=(row == 0) & (inner == 0),
            )
        return self.kept[value.shape]

    def second_up(self, value):
        if self.pack == 1:
            return across(value, 1)
        mask = self.masks(value)["up"]
        return jnp.where(mask, along(value, 1), across(along(value, 1 - self.pack), 1))

    def second_down(self, value):
        if self.pack == 1:
            return across(value, -1)
        mask = self.masks(value)["down"]
        return jnp.where(mask, along(value, -1), across(along(value, self.pack - 1), -1))

    def faces(self, beta, half):
        mask = self.masks(beta)
        up = self.second_up(beta)
        if self.whole:
            up = jnp.where(mask["second_last"], 0.0, up)
        second = half * (beta + up)
        down = self.second_down(beta)
        if self.whole:
            down = jnp.where(mask["second_first"], 0.0, down)
        share = half * (beta + down) + second
        if self.whole:
            second = jnp.where(mask["second_last"], 0.0, second)
        third_up = jnp.where(mask["third_last"], 0.0, along(beta, self.pack))
        third = half * (beta + third_up)
        third_down = jnp.where(mask["third_first"], 0.0, along(beta, -self.pack))
        share = share + half * (beta + third_down) + third
        return second, jnp.where(mask["third_last"], 0.0, third), share

    def coupled(self, value, second, third):
        total = second * self.second_up(value) + self.second_down(second * value)
        total = total + third * along(value, self.pack)
        return total + along(third * value, -self.pack)


def pair_sum(value, width):
    low = (lax.broadcasted_iota(jnp.int32, value.shape, value.ndim - 1) & width) == 0
    return value + jnp.where(low, along(value, width), along(value, -width))


def residual(shape, source, parts, field, start, stop):
    diag, _, first, second, third = parts
    here = field[start:stop]
    total = source(start, stop) - diag[start:stop] * here
    total = total + first[start:stop] * field[start + 1 : stop + 1]
    total = total + first[start - 1 : stop - 1] * field[start - 1 : stop - 1]
    return total + shape.coupled(here, second[start:stop], third[start:stop])


def sweep(shape, orders, source, parts, buffers, ranges, chunk):
    inverse = parts[1]
    current, previous = buffers
    for (order, (carry, push)), (low, high) in zip(orders, ranges):
        for start in range(low, high, chunk):
            stop = min(start + chunk, high)
            rest = residual(shape, source, parts, current, start, stop)
            here = current[start:stop]
            fresh = here + push * (inverse[start:stop] * rest)
            if order > 0:
                fresh = fresh + carry * (here - previous[start:stop])
            previous[start:stop] = fresh
        current, previous = previous, current
    return current, previous


def begin(table, inverse, source, buffers, low, high, chunk):
    for start in range(low, high, chunk):
        stop = min(start + chunk, high)
        fresh = table[0][1] * (inverse[start:stop] * source(start, stop))
        buffers[0][start:stop] = fresh
        buffers[1][start:stop] = jnp.zeros_like(fresh)


ROWS0 = 48


CHUNK0 = 2


def level0_parts(shape, beta, absorb, parts, low, high):
    diag, inverse, first, second, third = parts
    half = face(0)
    first[low - 1 : low] = half * (beta(low - 1, low) + beta(low, low + 1))
    for start in range(low, high, CHUNK0):
        stop = min(start + CHUNK0, high)
        here = beta(start, stop)
        first[start:stop] = half * (here + beta(start + 1, stop + 1))
        lower = half * (beta(start - 1, stop - 1) + here)
        second[start:stop], third[start:stop], share = shape.faces(here, half)
        total = absorb(start, stop) + lower + first[start:stop] + share
        diag[start:stop] = total
        inverse[start:stop] = jnp.where(here > 0.0, 1.0 / total, 0.0)


def pairs(value):
    return jnp.stack([value[at] + value[at + 1] for at in range(0, value.shape[0], 2)])


def coarse_rows(ref, value):
    count = value.shape[0]
    zero = jnp.zeros((count, 8, LANES), jnp.float32)
    ref[0:count, 0:8, :] = zero
    ref[0:count, 8:56, :] = pair_sum(value, 1)
    ref[0:count, 56:64, :] = zero

    def take(offset):
        halves = [
            [ref[at, pl.ds(32 * half + offset, 8, stride=4), :] for half in range(2)]
            for at in range(count)
        ]
        return jnp.stack([jnp.concatenate(both) for both in halves])

    even = (lax.broadcasted_iota(jnp.int32, (count, ROWS1, LANES), 2) & 1) == 0
    return 0.125 * jnp.where(even, take(0) + take(1), take(2) + take(3))


KEPT0 = 10
KEPT_ROWS0 = 32


def pre0_kernel(
    own, outer, kept_out, tile_out, absorb_out,
    diag, inverse, first, second, third, one, two, tmp,
):
    zero = jnp.zeros((8, LANES), jnp.float32)

    def piece(kind):
        def planes(start, stop):
            found = []
            for plane in range(start, stop):
                part, member = plane // 8, plane % 8 // 2
                if part == 1:
                    found.append(own[member, kind, plane % 2])
                    continue
                side = part // 2
                at = 4 * (6 * member + 2 * kind + plane % 2)
                middle = [outer[side, at + tile] for tile in range(4)]
                reach = 3 if kind == 2 else 2
                near = member - (LAYER - reach) if side == 0 else member
                if 0 <= near < reach:
                    at = 96 + 2 * (2 * (2 * kind + near) + plane % 2)
                    ends = outer[side, at], outer[side, at + 1]
                else:
                    ends = zero, zero
                found.append(jnp.concatenate([ends[0], *middle, ends[1]]))
            return jnp.stack(found)

        return planes

    source, absorb, beta = piece(0), piece(1), piece(2)
    shape = Packed(1, ROWS0, False)
    parts = (diag, inverse, first, second, third)
    level0_parts(shape, beta, absorb, parts, 1, 23)
    table = chebyshev_table(SWEEPS)
    begin(table, inverse, source, (one, two), 1, 23, CHUNK0)
    ranges = [(1 + order, 23 - order) for order in range(1, SWEEPS)]
    current, previous = sweep(
        shape, list(enumerate(table))[1:], source, parts, (one, two), ranges, CHUNK0
    )
    previous[4:20] = source(4, 20)
    base = 2 * (position() % LAYER) + 4
    for plane in range(KEPT0):
        for number, kept in enumerate((current, previous) + parts):
            kept_out[number, plane] = kept[base + plane, 8:40, :]
    coarse = Packed(2, ROWS1, False)
    half = face(1)
    betas = coarse_rows(tmp.at[0:8], pairs(beta(4, 20)))
    wide = coarse_rows(tmp.at[8:14], pairs(absorb(6, 18)))
    rest = [residual(shape, source, parts, current, p, p + 2) for p in range(6, 18, 2)]
    tile_out[:, 0] = coarse_rows(tmp.at[14:20], jnp.stack([x[0] + x[1] for x in rest]))
    here = betas[1:7]
    _, _, share = coarse.faces(here, half)
    tile_out[:, 1] = here
    tile_out[:, 2] = wide + half * (here + betas[0:6]) + half * (here + betas[2:8]) + share
    absorb_out[...] = wide[1:5]


DEPTH1 = 22
ROWS1 = 16


def gather_level1(region, own, outer):
    zero = jnp.zeros((4, LANES), jnp.float32)
    for plane in range(DEPTH1):
        for kind in range(3):
            if 5 <= plane < 17:
                part, index = divmod(plane - 5, 4)
                if part == 1:
                    region[kind, plane] = own[index + 1, kind]
                else:
                    at = 6 * index + 2 * kind
                    region[kind, plane, 0:8, :] = outer[part // 2, at]
                    region[kind, plane, 8:16, :] = outer[part // 2, at + 1]
            else:
                part, index = (0, plane) if plane < 5 else (1, plane - 16)
                region[kind, plane, 0:4, :] = zero
                region[kind, plane, 4:12, :] = outer[part, 24 + 3 * index + kind]
                region[kind, plane, 12:16, :] = zero


CHUNK1 = 4


def level1_parts(shape, region, inverse, first, second, third):
    half = face(1)
    beta = region.at[1]
    for start in range(0, DEPTH1, CHUNK1):
        stop = min(start + CHUNK1, DEPTH1)
        here = beta[start:stop]
        second[start:stop], third[start:stop], _ = shape.faces(here, half)
        inverse[start:stop] = jnp.where(here > 0.0, 1.0 / region[2, start:stop], 0.0)
        stop = min(stop, DEPTH1 - 1)
        first[start:stop] = half * (beta[start:stop] + beta[start + 1 : stop + 1])


def coarser_rows(ref, value, start):
    ref[...] = pair_sum(pair_sum(value, 1), 2)
    inner = lanes_of(1) & 3
    rows = []
    for at in range(value.shape[0]):
        row = ref[at, start : start + 1, :]
        for offset in range(1, 4):
            row = jnp.where(inner == offset, ref[at, start + offset : start + offset + 1, :], row)
        rows.append(0.125 * row)
    return rows


def pre1_kernel(
    own, outer, absorb, pay_out, rows_out, field, region, inverse, first, second, third,
    two, tmp, tile,
):
    gather_level1(region, own, outer)
    shape = Packed(2, ROWS1, False)
    level1_parts(shape, region, inverse, first, second, third)
    source = lambda start, stop: region[0, start:stop]
    parts = (region.at[2], inverse, first, second, third)
    table = chebyshev_table(SWEEPS)
    begin(table, inverse, source, (two, field), 0, DEPTH1, CHUNK1)
    ranges = [(order, DEPTH1 - order) for order in range(1, SWEEPS)]
    current, _ = sweep(
        shape, list(enumerate(table))[1:], source, parts, (two, field), ranges, CHUNK1
    )
    rest = residual(shape, source, parts, current, 9, 13)
    totals = [pairs(rest), pairs(region[1, 9:13]), pairs(absorb[...])]
    rows = coarser_rows(tmp, jnp.concatenate(totals), 6)
    for at in range(6):
        tile[at : at + 1, :] = rows[at]
    tile[6:8, :] = jnp.zeros((2, LANES), jnp.float32)
    kind = 2 * (position() % LAYER)
    for side in range(2):
        part = tile[pl.ds(kind + side, 1), :]
        pay_out[:, side * LANES : (side + 1) * LANES] = jnp.broadcast_to(part, (16, LANES))
    base = 3 + 4 * (position() % LAYER)
    for plane in range(4):
        row, lane = 4 * (plane % 2), plane // 2 * LANES
        rows_out[row : row + 4, lane : lane + LANES] = current[base + plane, 6:10, :]


DEPTH2 = 32
KIND_AT = (0, 2, 1)
ROWS2 = 8


CHUNK2 = 4


def level2_parts(shape, beta, absorb, parts):
    diag, inverse, first, second, third = parts
    half = face(2)
    first[0:1] = jnp.zeros((1, ROWS2, LANES), jnp.float32)
    for start in range(1, DEPTH2 + 1, CHUNK2):
        stop = start + CHUNK2
        here = beta[start:stop]
        upper = half * (here + beta[start + 1 : stop + 1])
        lower = half * (here + beta[start - 1 : stop - 1])
        second[start:stop], third[start:stop], share = shape.faces(here, half)
        total = absorb[start:stop] + lower + upper + share
        first[start:stop] = upper
        diag[start:stop] = total
        inverse[start:stop] = 1.0 / total


def bottom_rows(ref, planes):
    value = planes(1, DEPTH2 + 1)
    value = jnp.concatenate([value[at] + value[at + 1] for at in range(0, DEPTH2, 2)])
    ref[...] = pair_sum(pair_sum(value, 1), 4)
    inner = lanes_of(32) & 7
    total = None
    for offset in range(4):
        value = jnp.concatenate(
            [ref[pl.ds(32 * block + offset, 8, stride=4), :] for block in range(4)]
        )
        moved = along(value, 1 if offset % 2 == 0 else -1)
        same = 2 * offset + offset % 2
        value = jnp.where(inner == same, value, moved)
        total = value if total is None else jnp.where(inner >> 1 == offset, value, total)
    return 0.125 * total


def bottom_solve(source, absorb, beta):
    shape = Packed(8, 2, True)
    half = face(3)
    row = rows_of(32)
    last, initial = row >= 30, row < 2
    up = jnp.where(last, 0.0, across(beta, 2))
    down = jnp.where(initial, 0.0, across(beta, -2))
    second, third, share = shape.faces(beta, half)
    upper = half * (beta + up)
    diag = absorb + half * (beta + down) + upper + share
    first = jnp.where(last, 0.0, upper)
    inverse = 1.0 / diag
    table = chebyshev_table(BOTTOM)
    current = table[0][1] * (inverse * source)
    previous = jnp.zeros_like(current)
    for carry, push in table[1:]:
        rest = source - diag * current + first * across(current, 2) + across(first * current, -2)
        rest = rest + shape.coupled(current, second, third)
        fresh = current + carry * (current - previous) + push * (inverse * rest)
        current, previous = fresh, current
    return current


def bottom_prolong(ref, value):
    inner = lanes_of(32) & 7
    part = inner & 3
    back1, back2 = along(value, -1), along(value, -2)
    fore1, fore2 = along(value, 1), along(value, 2)
    low = jnp.where(part == 0, value, jnp.where(part == 3, back2, back1))
    high = jnp.where(part == 3, value, jnp.where(part == 0, fore2, fore1))
    left = inner < 4
    for offset in range(4):
        base = low if offset % 2 == 0 else high
        if offset < 2:
            moved = jnp.where(left, base, along(base, -4))
        else:
            moved = jnp.where(left, along(base, 4), base)
        for block in range(4):
            ref[pl.ds(32 * block + offset, 8, stride=4), :] = moved[8 * block : 8 * block + 8]


def solve23(packed, halves, rows2, parts2, one2, two2, tall):
    shape = Packed(4, ROWS2, True)
    zero = jnp.zeros((ROWS2, LANES), jnp.float32)
    for peer in range(32):
        for side in range(2):
            halves[side, 16 * peer : 16 * peer + 16, :] = packed[
                peer, 0:16, side * LANES : (side + 1) * LANES
            ]
    for number in range(3):
        for plane in range(DEPTH2):
            at = 128 * KIND_AT[number] + plane // 2
            rows2[number, plane + 1] = halves[plane % 2, pl.ds(at, 8, stride=16), :]
    for ref in (rows2.at[1], one2, two2):
        ref[0] = zero
        ref[DEPTH2 + 1] = zero

    source2 = lambda start, stop: rows2[0, start:stop]
    level2_parts(shape, rows2.at[1], rows2.at[2], parts2)
    table = chebyshev_table(SWEEPS)
    begin(table, parts2[1], source2, (one2, two2), 1, DEPTH2 + 1, CHUNK2)
    everywhere = [(1, DEPTH2 + 1)] * SWEEPS
    current, previous = sweep(
        shape, list(enumerate(table))[1:], source2, parts2, (one2, two2), everywhere, CHUNK2
    )
    source3 = bottom_rows(
        tall.at[0], lambda start, stop: residual(shape, source2, parts2, current, start, stop)
    )
    absorb3 = bottom_rows(tall.at[1], lambda start, stop: rows2[2, start:stop])
    beta3 = bottom_rows(tall.at[2], lambda start, stop: rows2[1, start:stop])
    bottom_prolong(tall.at[0], bottom_solve(source3, absorb3, beta3))
    for plane in range(DEPTH2):
        pair = plane // 2
        current[plane + 1] = current[plane + 1] + tall[0, 8 * pair : 8 * pair + 8, :]
    current, previous = sweep(
        shape, list(enumerate(table)), source2, parts2, (current, previous), everywhere, CHUNK2
    )
    return current


def post1(packed, field, whole, region, parts, one, two, wide, tmp):
    inverse, first, second, third = parts
    shape = Packed(2, ROWS1, False)
    layer = position() // LAYER
    row = column_position() + 6
    zero = jnp.zeros((8, LANES), jnp.float32)
    for plane in range(DEPTH2 + 6):
        wide[plane, 0:8, :] = zero
        wide[plane, 16:24, :] = zero
        inside = 3 <= plane < DEPTH2 + 3
        wide[plane, 8:16, :] = whole[plane - 2] if inside else zero
    value = jnp.stack([wide[2 * layer + pair, pl.ds(row, 8), :] for pair in range(8)])
    inner = lax.broadcasted_iota(jnp.int32, value.shape, 2) & 3
    moved = {steps: along(value, steps) for steps in range(-3, 4) if steps}
    moved[0] = value
    for offset in range(4):
        picked = moved[offset]
        for lane in range(1, 4):
            picked = jnp.where(inner == lane, moved[offset - lane], picked)
        for pair in range(8):
            tmp[pair, pl.ds(offset, 8, stride=4), :] = picked[pair]
    place = column_position()
    before, after = jnp.maximum(place - 1, 0), jnp.minimum(place + 1, 7)
    has_before = jnp.where(place > 0, 1.0, 0.0)
    has_after = jnp.where(place < 7, 1.0, 0.0)
    row = lax.broadcasted_iota(jnp.int32, (2, 8, LANES), 1)
    inside = (row >= 2) & (row < 6)

    def neighbour(start, who, there):
        member, half = divmod((start - 3) // 2, 2)
        at = 16 * (member % 2) + 8 * (member // 2)
        value = there * packed[at + who, 16:24, half * LANES : (half + 1) * LANES]
        return jnp.stack([across(value, -2), across(value, 2)])

    for start in range(3, 19, 2):
        here = field[start : start + 2]
        upper = jnp.where(inside, neighbour(start, before, has_before), here[:, 0:8])
        lower = jnp.where(inside, neighbour(start, after, has_after), here[:, 8:16])
        one[start : start + 2] = jnp.concatenate([upper, lower], 1) + tmp[(start - 3) // 2, 2:18, :]
    table = chebyshev_table(SWEEPS)
    ranges = [(3 + order, 19 - order) for order in range(1, SWEEPS + 1)]
    current, _ = sweep(
        shape, list(enumerate(table)), lambda start, stop: region[0, start:stop],
        (region.at[2], inverse, first, second, third), (one, two), ranges, CHUNK1,
    )
    return current


def post0(kept, coarse, out, one, two, tmp):
    field, source = kept.at[0], kept.at[1]
    parts = tuple(kept.at[number] for number in range(2, 7))
    member = position() % LAYER
    shape = Packed(1, ROWS0, False)
    value = jnp.stack([coarse[7 + member + pair, 4:12, :] for pair in range(5)])
    even = (lax.broadcasted_iota(jnp.int32, value.shape, 2) & 1) == 0
    upper_rows = jnp.where(even, value, along(value, -1))
    lower_rows = jnp.where(even, along(value, 1), value)
    for pair in range(5):
        for offset in range(4):
            rows = upper_rows if offset < 2 else lower_rows
            tmp[pair, pl.ds(offset, 8, stride=4), :] = rows[pair]
    for plane in range(KEPT0):
        one[plane] = field[plane] + tmp[plane // 2]
    table = chebyshev_table(SWEEPS)
    ranges = [(1 + order, KEPT0 - 1 - order) for order in range(SWEEPS)]
    current, _ = sweep(
        shape, list(enumerate(table)), lambda start, stop: source[start:stop], parts,
        (one, two), ranges, CHUNK0,
    )
    out[...] = current[4:6, 8:24, :]


def finish_kernel(
    packed, field1, region1, inverse1, first1, second1, third1, kept0, out,
    halves, rows2, diag2, inverse2, first2, second2, third2, one2, two2, tall,
    one1, two1, wide1, tmp1, one0, two0, tmp0,
):
    parts2 = (diag2, inverse2, first2, second2, third2)
    whole = solve23(packed, halves, rows2, parts2, one2, two2, tall)
    parts1 = (inverse1, first1, second1, third1)
    coarse = post1(packed, field1, whole, region1, parts1, one1, two1, wide1, tmp1)
    post0(kept0, coarse, out, one0, two0, tmp0)


def f32(*shape):
    return jax.ShapeDtypeStruct(shape, jnp.float32)


def buffer(*shape):
    return pltpu.VMEM(shape, jnp.float32)


def call(kernel, out, scratch, name, *operands):
    return pl.pallas_call(
        kernel,
        out_shape=out,
        scratch_shapes=scratch,
        name=name,
        compiler_params=pltpu.CompilerParams(vmem_limit_bytes=VMEM),
    )(*operands)


def pre0(*pieces):
    plane = buffer(24, ROWS0, LANES)
    scratch = [plane] * 7 + [buffer(20, 64, LANES)]
    out = (f32(7, KEPT0, KEPT_ROWS0, LANES), f32(6, 3, ROWS1, LANES), f32(4, ROWS1, LANES))
    return call(pre0_kernel, out, scratch, "pre0", *pieces)


def pre1(*pieces):
    plane = f32(DEPTH1, ROWS1, LANES)
    scratch = [buffer(DEPTH1, ROWS1, LANES), buffer(6, ROWS1, LANES), buffer(8, LANES)]
    out = (f32(16, 2 * LANES), f32(8, 2 * LANES), plane, f32(3, DEPTH1, ROWS1, LANES)) + (plane,) * 4
    return call(pre1_kernel, out, scratch, "pre1", *pieces)


def finish(*pieces):
    plane2 = buffer(DEPTH2 + 2, ROWS2, LANES)
    plane1 = buffer(DEPTH1, ROWS1, LANES)
    plane0 = buffer(KEPT0, KEPT_ROWS0, LANES)
    scratch = [buffer(2, 512, LANES), buffer(3, DEPTH2 + 2, ROWS2, LANES)] + [plane2] * 7 + [buffer(3, 128, LANES)]
    scratch += [plane1] * 2 + [buffer(DEPTH2 + 6, 24, LANES), buffer(8, 32, LANES)]
    scratch += [plane0] * 2 + [buffer(5, KEPT_ROWS0, LANES)]
    return call(finish_kernel, f32(2, 16, LANES), scratch, "finish", *pieces)


def layers_apart(value, steps):
    count = lax.axis_size("gx")
    ways = [(i, i + (LAYER * steps if i % 2 == 0 else -LAYER * steps)) for i in range(count)]
    return lax.ppermute(value, "gx", [(i, j) for i, j in ways if 0 <= j < count])


def columns_apart(value):
    count, wide = lax.axis_size("gx"), lax.axis_size("gy")
    ways = [
        (i * wide + j, i * wide + j + (1 if i % 2 == 0 else -1))
        for i in range(count)
        for j in range(wide)
        if 0 <= j + (1 if i % 2 == 0 else -1) < wide
    ]
    return lax.ppermute(value, ("gx", "gy"), ways)


def body(source, absorb, beta):
    members = lax.axis_size("gx")
    wide = lax.axis_size("gy")
    layers = members // LAYER
    near = [[LAYER * z + c for c in range(LAYER)] for z in range(layers)]
    chips = [[2 * chip, 2 * chip + 1] for chip in range(members // 2)]
    column = [[LAYER * z + c for z in range(layers)] for c in range(LAYER)]
    cores = [
        [(LAYER * z + 2 * chip + core) * wide + y for chip in range(2) for y in range(wide)]
        for z in range(layers)
        for core in range(2)
    ]
    first_core = lax.axis_index("gx") % 2 == 0

    def both(value):
        return lax.all_gather(value, "gx", axis_index_groups=chips)

    local = jnp.stack([source, absorb, beta])
    own = lax.all_gather(local, "gx", axis_index_groups=near)
    sides = both(columns_apart(own))
    layer = jnp.concatenate([sides[0], own, sides[1]], axis=-2)
    ends = jnp.concatenate([sides[0, ..., :8, :], sides[1, ..., 8:, :]], axis=-2)
    near2 = jnp.where(first_core, ends[2:, :2], ends[:2, :2])
    near3 = jnp.where(first_core, ends[1:, 2], ends[:3, 2])
    sent = [layer[..., 8:40, :], near2[:, 0], near2[:, 1], near3]
    sent = jnp.concatenate([x.reshape(-1, 8, LANES) for x in sent])
    kept0, tile, absorb1 = pre0(layer, both(layers_apart(sent, 1)))

    tiles = [layers_apart(tile[1:5], 1), layers_apart(tile[..., 4:12, :], 2)]
    tiles = jnp.concatenate([x.reshape(-1, 8, LANES) for x in tiles])
    pay, rows1, *kept1 = pre1(tile, both(tiles), absorb1)

    rows = lax.all_to_all(pay, "gx", 0, 0, axis_index_groups=column)
    rows = jnp.concatenate([rows, rows1])
    rows = jnp.broadcast_to(rows, (2 * wide,) + rows.shape)
    rows = lax.all_to_all(rows, ("gx", "gy"), 0, 0, axis_index_groups=cores)
    packed = both(rows).reshape(-1, *rows.shape[1:])
    return finish(packed, *kept1, kept0)


def solution(mesh):
    placed = (P("gx", "gy", None), P("gx", "gy", None), P("gx", "gy", None))
    return jax.shard_map(
        body, mesh=mesh, in_specs=placed, out_specs=P("gx", "gy", None), check_vma=False
    )
```

```python
import jax
import jax.numpy as jnp
from jax import lax
from jax.experimental import pallas as pl
from jax.experimental.pallas import tpu as pltpu
from jax.sharding import PartitionSpec as P

SWEEPS = 4
BOTTOM = 8
LANES = 128
VMEM = 24 * 1024 * 1024

LAYER = 4
PACK = (1, 2, 4, 8)


def face(level):
    return 0.5 * 0.25**level


def chebyshev_table(count):
    centre = 1.125
    half_width = 0.875
    ratio = centre / half_width
    factor = 1.0 / ratio
    table = [(0.0, 1.0 / centre)]
    for order in range(1, count):
        fresh_factor = 1.0 / (2.0 * ratio - factor)
        table.append((fresh_factor * factor, 2.0 * fresh_factor / half_width))
        factor = fresh_factor
    return table


def position():
    return lax.axis_index("gx")


def column_position():
    return lax.axis_index("gy")


def lanes_of(rows):
    return lax.broadcasted_iota(jnp.int32, (rows, LANES), 1)


def rows_of(rows):
    return lax.broadcasted_iota(jnp.int32, (rows, LANES), 0)


def along(value, steps):
    return pltpu.roll(value, (-steps) % LANES, value.ndim - 1)


def across(value, steps):
    rows = value.shape[-2]
    return pltpu.roll(value, (-steps) % rows, value.ndim - 2)


class Packed:
    def __init__(self, pack, period, whole):
        self.pack = pack
        self.period = period
        self.whole = whole
        self.kept = {}

    def masks(self, value):
        if value.shape not in self.kept:
            pack, dims = self.pack, value.ndim
            lane = lax.broadcasted_iota(jnp.int32, value.shape, dims - 1)
            row = lax.broadcasted_iota(jnp.int32, value.shape, dims - 2) & (self.period - 1)
            inner = lane & (pack - 1)
            self.kept[value.shape] = dict(
                up=inner < pack - 1,
                down=inner > 0,
                third_last=lane >= LANES - pack,
                third_first=lane < pack,
                second_last=(row == self.period - 1) & (inner == pack - 1),
                second_first=(row == 0) & (inner == 0),
            )
        return self.kept[value.shape]

    def second_up(self, value):
        if self.pack == 1:
            return across(value, 1)
        mask = self.masks(value)["up"]
        return jnp.where(mask, along(value, 1), across(along(value, 1 - self.pack), 1))

    def second_down(self, value):
        if self.pack == 1:
            return across(value, -1)
        mask = self.masks(value)["down"]
        return jnp.where(mask, along(value, -1), across(along(value, self.pack - 1), -1))

    def faces(self, beta, half):
        mask = self.masks(beta)
        up = self.second_up(beta)
        if self.whole:
            up = jnp.where(mask["second_last"], 0.0, up)
        second = half * (beta + up)
        down = self.second_down(beta)
        if self.whole:
            down = jnp.where(mask["second_first"], 0.0, down)
        share = half * (beta + down) + second
        if self.whole:
            second = jnp.where(mask["second_last"], 0.0, second)
        third_up = jnp.where(mask["third_last"], 0.0, along(beta, self.pack))
        third = half * (beta + third_up)
        third_down = jnp.where(mask["third_first"], 0.0, along(beta, -self.pack))
        share = share + half * (beta + third_down) + third
        return second, jnp.where(mask["third_last"], 0.0, third), share

    def coupled(self, value, second, third):
        total = second * self.second_up(value) + self.second_down(second * value)
        total = total + third * along(value, self.pack)
        return total + along(third * value, -self.pack)


def pair_sum(value, width):
    low = (lax.broadcasted_iota(jnp.int32, value.shape, value.ndim - 1) & width) == 0
    return value + jnp.where(low, along(value, width), along(value, -width))


def residual(shape, source, parts, field, start, stop):
    diag, _, first, second, third = parts
    here = field[start:stop]
    total = source(start, stop) - diag[start:stop] * here
    total = total + first[start:stop] * field[start + 1 : stop + 1]
    total = total + first[start - 1 : stop - 1] * field[start - 1 : stop - 1]
    return total + shape.coupled(here, second[start:stop], third[start:stop])


def sweep(shape, orders, source, parts, buffers, ranges, chunk):
    inverse = parts[1]
    current, previous = buffers
    for (order, (carry, push)), (low, high) in zip(orders, ranges):
        for start in range(low, high, chunk):
            stop = min(start + chunk, high)
            rest = residual(shape, source, parts, current, start, stop)
            here = current[start:stop]
            fresh = here + push * (inverse[start:stop] * rest)
            if order > 0:
                fresh = fresh + carry * (here - previous[start:stop])
            previous[start:stop] = fresh
        current, previous = previous, current
    return current, previous


def begin(table, inverse, source, buffers, low, high, chunk):
    for start in range(low, high, chunk):
        stop = min(start + chunk, high)
        fresh = table[0][1] * (inverse[start:stop] * source(start, stop))
        buffers[0][start:stop] = fresh
        buffers[1][start:stop] = jnp.zeros_like(fresh)


ROWS0 = 48


CHUNK0 = 2


def level0_parts(shape, beta, absorb, parts, low, high):
    diag, inverse, first, second, third = parts
    half = face(0)
    first[low - 1 : low] = half * (beta(low - 1, low) + beta(low, low + 1))
    for start in range(low, high, CHUNK0):
        stop = min(start + CHUNK0, high)
        here = beta(start, stop)
        first[start:stop] = half * (here + beta(start + 1, stop + 1))
        lower = half * (beta(start - 1, stop - 1) + here)
        second[start:stop], third[start:stop], share = shape.faces(here, half)
        total = absorb(start, stop) + lower + first[start:stop] + share
        diag[start:stop] = total
        inverse[start:stop] = jnp.where(here > 0.0, 1.0 / total, 0.0)


def pairs(value):
    return jnp.stack([value[at] + value[at + 1] for at in range(0, value.shape[0], 2)])


def coarse_rows(ref, value):
    count = value.shape[0]
    zero = jnp.zeros((count, 8, LANES), jnp.float32)
    ref[0:count, 0:8, :] = zero
    ref[0:count, 8:56, :] = pair_sum(value, 1)
    ref[0:count, 56:64, :] = zero

    def take(offset):
        halves = [
            [ref[at, pl.ds(32 * half + offset, 8, stride=4), :] for half in range(2)]
            for at in range(count)
        ]
        return jnp.stack([jnp.concatenate(both) for both in halves])

    even = (lax.broadcasted_iota(jnp.int32, (count, ROWS1, LANES), 2) & 1) == 0
    return 0.125 * jnp.where(even, take(0) + take(1), take(2) + take(3))


KEPT0 = 10
KEPT_ROWS0 = 32


def pre0_kernel(
    own, outer, kept_out, tile_out, absorb_out,
    diag, inverse, first, second, third, one, two, tmp,
):
    zero = jnp.zeros((8, LANES), jnp.float32)

    def piece(kind):
        def planes(start, stop):
            found = []
            for plane in range(start, stop):
                part, member = plane // 8, plane % 8 // 2
                if part == 1:
                    found.append(own[member, kind, plane % 2])
                    continue
                side = part // 2
                at = 2 * (6 * member + 2 * kind + plane % 2)
                rows = [outer[side, at + tile] for tile in (48, 0, 1, 49)]
                reach = 3 if kind == 2 else 2
                near = member - (LAYER - reach) if side == 0 else member
                if 0 <= near < reach:
                    at = 96 + 2 * (2 * (2 * kind + near) + plane % 2)
                    ends = outer[side, at], outer[side, at + 1]
                else:
                    ends = zero, zero
                found.append(jnp.concatenate([ends[0], *rows, ends[1]]))
            return jnp.stack(found)

        return planes

    source, absorb, beta = piece(0), piece(1), piece(2)
    shape = Packed(1, ROWS0, False)
    parts = (diag, inverse, first, second, third)
    level0_parts(shape, beta, absorb, parts, 1, 23)
    table = chebyshev_table(SWEEPS)
    begin(table, inverse, source, (one, two), 1, 23, CHUNK0)
    ranges = [(1 + order, 23 - order) for order in range(1, SWEEPS)]
    current, previous = sweep(
        shape, list(enumerate(table))[1:], source, parts, (one, two), ranges, CHUNK0
    )
    previous[4:20] = source(4, 20)
    base = 2 * (position() % LAYER) + 4
    for plane in range(KEPT0):
        for number, kept in enumerate((current, previous) + parts):
            kept_out[number, plane] = kept[base + plane, 8:40, :]
    coarse = Packed(2, ROWS1, False)
    half = face(1)
    betas = coarse_rows(tmp.at[0:8], pairs(beta(4, 20)))
    wide = coarse_rows(tmp.at[8:14], pairs(absorb(6, 18)))
    rest = [residual(shape, source, parts, current, p, p + 2) for p in range(6, 18, 2)]
    tile_out[:, 0] = coarse_rows(tmp.at[14:20], jnp.stack([x[0] + x[1] for x in rest]))
    here = betas[1:7]
    _, _, share = coarse.faces(here, half)
    tile_out[:, 1] = here
    tile_out[:, 2] = wide + half * (here + betas[0:6]) + half * (here + betas[2:8]) + share
    absorb_out[...] = wide[1:5]


DEPTH1 = 22
ROWS1 = 16


def gather_level1(region, own, outer):
    zero = jnp.zeros((4, LANES), jnp.float32)
    for plane in range(DEPTH1):
        for kind in range(3):
            if 5 <= plane < 17:
                part, index = divmod(plane - 5, 4)
                if part == 1:
                    region[kind, plane] = own[index + 1, kind]
                else:
                    at = 6 * index + 2 * kind
                    region[kind, plane, 0:8, :] = outer[part // 2, at]
                    region[kind, plane, 8:16, :] = outer[part // 2, at + 1]
            else:
                part, index = (0, plane) if plane < 5 else (1, plane - 16)
                region[kind, plane, 0:4, :] = zero
                region[kind, plane, 4:12, :] = outer[part, 24 + 3 * index + kind]
                region[kind, plane, 12:16, :] = zero


CHUNK1 = 4


def level1_parts(shape, region, inverse, first, second, third):
    half = face(1)
    beta = region.at[1]
    for start in range(0, DEPTH1, CHUNK1):
        stop = min(start + CHUNK1, DEPTH1)
        here = beta[start:stop]
        second[start:stop], third[start:stop], _ = shape.faces(here, half)
        inverse[start:stop] = jnp.where(here > 0.0, 1.0 / region[2, start:stop], 0.0)
        stop = min(stop, DEPTH1 - 1)
        first[start:stop] = half * (beta[start:stop] + beta[start + 1 : stop + 1])


def coarser_rows(ref, value, start):
    ref[...] = pair_sum(pair_sum(value, 1), 2)
    inner = lanes_of(1) & 3
    rows = []
    for at in range(value.shape[0]):
        row = ref[at, start : start + 1, :]
        for offset in range(1, 4):
            row = jnp.where(inner == offset, ref[at, start + offset : start + offset + 1, :], row)
        rows.append(0.125 * row)
    return rows


def pre1_kernel(
    own, outer, absorb, pay_out, rows_out, field, region, inverse, first, second, third,
    two, tmp, tile,
):
    gather_level1(region, own, outer)
    shape = Packed(2, ROWS1, False)
    level1_parts(shape, region, inverse, first, second, third)
    source = lambda start, stop: region[0, start:stop]
    parts = (region.at[2], inverse, first, second, third)
    table = chebyshev_table(SWEEPS)
    begin(table, inverse, source, (two, field), 0, DEPTH1, CHUNK1)
    ranges = [(order, DEPTH1 - order) for order in range(1, SWEEPS)]
    current, _ = sweep(
        shape, list(enumerate(table))[1:], source, parts, (two, field), ranges, CHUNK1
    )
    rest = residual(shape, source, parts, current, 9, 13)
    totals = [pairs(rest), pairs(region[1, 9:13]), pairs(absorb[...])]
    rows = coarser_rows(tmp, jnp.concatenate(totals), 6)
    for at in range(6):
        tile[at : at + 1, :] = rows[at]
    tile[6:8, :] = jnp.zeros((2, LANES), jnp.float32)
    kind = 2 * (position() % LAYER)
    for side in range(2):
        part = tile[pl.ds(kind + side, 1), :]
        pay_out[:, side * LANES : (side + 1) * LANES] = jnp.broadcast_to(part, (16, LANES))
    base = 3 + 4 * (position() % LAYER)
    for plane in range(4):
        row, lane = 4 * (plane % 2), plane // 2 * LANES
        rows_out[row : row + 4, lane : lane + LANES] = current[base + plane, 6:10, :]


DEPTH2 = 32
KIND_AT = (0, 2, 1)
ROWS2 = 8


CHUNK2 = 4


def level2_parts(shape, beta, absorb, parts):
    diag, inverse, first, second, third = parts
    half = face(2)
    first[0:1] = jnp.zeros((1, ROWS2, LANES), jnp.float32)
    for start in range(1, DEPTH2 + 1, CHUNK2):
        stop = start + CHUNK2
        here = beta[start:stop]
        upper = half * (here + beta[start + 1 : stop + 1])
        lower = half * (here + beta[start - 1 : stop - 1])
        second[start:stop], third[start:stop], share = shape.faces(here, half)
        total = absorb[start:stop] + lower + upper + share
        first[start:stop] = upper
        diag[start:stop] = total
        inverse[start:stop] = 1.0 / total


def bottom_rows(ref, planes):
    value = planes(1, DEPTH2 + 1)
    value = jnp.concatenate([value[at] + value[at + 1] for at in range(0, DEPTH2, 2)])
    ref[...] = pair_sum(pair_sum(value, 1), 4)
    inner = lanes_of(32) & 7
    total = None
    for offset in range(4):
        value = jnp.concatenate(
            [ref[pl.ds(32 * block + offset, 8, stride=4), :] for block in range(4)]
        )
        moved = along(value, 1 if offset % 2 == 0 else -1)
        same = 2 * offset + offset % 2
        value = jnp.where(inner == same, value, moved)
        total = value if total is None else jnp.where(inner >> 1 == offset, value, total)
    return 0.125 * total


def bottom_solve(source, absorb, beta):
    shape = Packed(8, 2, True)
    half = face(3)
    row = rows_of(32)
    last, initial = row >= 30, row < 2
    up = jnp.where(last, 0.0, across(beta, 2))
    down = jnp.where(initial, 0.0, across(beta, -2))
    second, third, share = shape.faces(beta, half)
    upper = half * (beta + up)
    diag = absorb + half * (beta + down) + upper + share
    first = jnp.where(last, 0.0, upper)
    inverse = 1.0 / diag
    table = chebyshev_table(BOTTOM)
    current = table[0][1] * (inverse * source)
    previous = jnp.zeros_like(current)
    for carry, push in table[1:]:
        rest = source - diag * current + first * across(current, 2) + across(first * current, -2)
        rest = rest + shape.coupled(current, second, third)
        fresh = current + carry * (current - previous) + push * (inverse * rest)
        current, previous = fresh, current
    return current


def bottom_prolong(ref, value):
    inner = lanes_of(32) & 7
    part = inner & 3
    back1, back2 = along(value, -1), along(value, -2)
    fore1, fore2 = along(value, 1), along(value, 2)
    low = jnp.where(part == 0, value, jnp.where(part == 3, back2, back1))
    high = jnp.where(part == 3, value, jnp.where(part == 0, fore2, fore1))
    left = inner < 4
    for offset in range(4):
        base = low if offset % 2 == 0 else high
        if offset < 2:
            moved = jnp.where(left, base, along(base, -4))
        else:
            moved = jnp.where(left, along(base, 4), base)
        for block in range(4):
            ref[pl.ds(32 * block + offset, 8, stride=4), :] = moved[8 * block : 8 * block + 8]


def solve23(packed, halves, rows2, parts2, one2, two2, tall):
    shape = Packed(4, ROWS2, True)
    zero = jnp.zeros((ROWS2, LANES), jnp.float32)
    for peer in range(32):
        for side in range(2):
            halves[side, 16 * peer : 16 * peer + 16, :] = packed[
                peer, 0:16, side * LANES : (side + 1) * LANES
            ]
    for number in range(3):
        for plane in range(DEPTH2):
            at = 128 * KIND_AT[number] + plane // 2
            rows2[number, plane + 1] = halves[plane % 2, pl.ds(at, 8, stride=16), :]
    for ref in (rows2.at[1], one2, two2):
        ref[0] = zero
        ref[DEPTH2 + 1] = zero

    source2 = lambda start, stop: rows2[0, start:stop]
    level2_parts(shape, rows2.at[1], rows2.at[2], parts2)
    table = chebyshev_table(SWEEPS)
    begin(table, parts2[1], source2, (one2, two2), 1, DEPTH2 + 1, CHUNK2)
    everywhere = [(1, DEPTH2 + 1)] * SWEEPS
    current, previous = sweep(
        shape, list(enumerate(table))[1:], source2, parts2, (one2, two2), everywhere, CHUNK2
    )
    source3 = bottom_rows(
        tall.at[0], lambda start, stop: residual(shape, source2, parts2, current, start, stop)
    )
    absorb3 = bottom_rows(tall.at[1], lambda start, stop: rows2[2, start:stop])
    beta3 = bottom_rows(tall.at[2], lambda start, stop: rows2[1, start:stop])
    bottom_prolong(tall.at[0], bottom_solve(source3, absorb3, beta3))
    for plane in range(DEPTH2):
        pair = plane // 2
        current[plane + 1] = current[plane + 1] + tall[0, 8 * pair : 8 * pair + 8, :]
    current, previous = sweep(
        shape, list(enumerate(table)), source2, parts2, (current, previous), everywhere, CHUNK2
    )
    return current


def post1(packed, field, whole, region, parts, one, two, wide, tmp):
    inverse, first, second, third = parts
    shape = Packed(2, ROWS1, False)
    layer = position() // LAYER
    row = column_position() + 6
    zero = jnp.zeros((8, LANES), jnp.float32)
    for plane in range(DEPTH2 + 6):
        wide[plane, 0:8, :] = zero
        wide[plane, 16:24, :] = zero
        inside = 3 <= plane < DEPTH2 + 3
        wide[plane, 8:16, :] = whole[plane - 2] if inside else zero
    value = jnp.stack([wide[2 * layer + pair, pl.ds(row, 8), :] for pair in range(8)])
    inner = lax.broadcasted_iota(jnp.int32, value.shape, 2) & 3
    moved = {steps: along(value, steps) for steps in range(-3, 4) if steps}
    moved[0] = value
    for offset in range(4):
        picked = moved[offset]
        for lane in range(1, 4):
            picked = jnp.where(inner == lane, moved[offset - lane], picked)
        for pair in range(8):
            tmp[pair, pl.ds(offset, 8, stride=4), :] = picked[pair]
    place = column_position()
    before, after = jnp.maximum(place - 1, 0), jnp.minimum(place + 1, 7)
    has_before = jnp.where(place > 0, 1.0, 0.0)
    has_after = jnp.where(place < 7, 1.0, 0.0)
    row = lax.broadcasted_iota(jnp.int32, (2, 8, LANES), 1)
    inside = (row >= 2) & (row < 6)

    def neighbour(start, who, there):
        member, half = divmod((start - 3) // 2, 2)
        at = 16 * (member % 2) + 8 * (member // 2)
        value = there * packed[at + who, 16:24, half * LANES : (half + 1) * LANES]
        return jnp.stack([across(value, -2), across(value, 2)])

    for start in range(3, 19, 2):
        here = field[start : start + 2]
        upper = jnp.where(inside, neighbour(start, before, has_before), here[:, 0:8])
        lower = jnp.where(inside, neighbour(start, after, has_after), here[:, 8:16])
        one[start : start + 2] = jnp.concatenate([upper, lower], 1) + tmp[(start - 3) // 2, 2:18, :]
    table = chebyshev_table(SWEEPS)
    ranges = [(3 + order, 19 - order) for order in range(1, SWEEPS + 1)]
    current, _ = sweep(
        shape, list(enumerate(table)), lambda start, stop: region[0, start:stop],
        (region.at[2], inverse, first, second, third), (one, two), ranges, CHUNK1,
    )
    return current


def post0(kept, coarse, out, one, two, tmp):
    field, source = kept.at[0], kept.at[1]
    parts = tuple(kept.at[number] for number in range(2, 7))
    member = position() % LAYER
    shape = Packed(1, ROWS0, False)
    value = jnp.stack([coarse[7 + member + pair, 4:12, :] for pair in range(5)])
    even = (lax.broadcasted_iota(jnp.int32, value.shape, 2) & 1) == 0
    upper_rows = jnp.where(even, value, along(value, -1))
    lower_rows = jnp.where(even, along(value, 1), value)
    for pair in range(5):
        for offset in range(4):
            rows = upper_rows if offset < 2 else lower_rows
            tmp[pair, pl.ds(offset, 8, stride=4), :] = rows[pair]
    for plane in range(KEPT0):
        one[plane] = field[plane] + tmp[plane // 2]
    table = chebyshev_table(SWEEPS)
    ranges = [(1 + order, KEPT0 - 1 - order) for order in range(SWEEPS)]
    current, _ = sweep(
        shape, list(enumerate(table)), lambda start, stop: source[start:stop], parts,
        (one, two), ranges, CHUNK0,
    )
    out[...] = current[4:6, 8:24, :]


def finish_kernel(
    packed, field1, region1, inverse1, first1, second1, third1, kept0, out,
    halves, rows2, diag2, inverse2, first2, second2, third2, one2, two2, tall,
    one1, two1, wide1, tmp1, one0, two0, tmp0,
):
    parts2 = (diag2, inverse2, first2, second2, third2)
    whole = solve23(packed, halves, rows2, parts2, one2, two2, tall)
    parts1 = (inverse1, first1, second1, third1)
    coarse = post1(packed, field1, whole, region1, parts1, one1, two1, wide1, tmp1)
    post0(kept0, coarse, out, one0, two0, tmp0)


def f32(*shape):
    return jax.ShapeDtypeStruct(shape, jnp.float32)


def buffer(*shape):
    return pltpu.VMEM(shape, jnp.float32)


def call(kernel, out, scratch, name, *operands):
    return pl.pallas_call(
        kernel,
        out_shape=out,
        scratch_shapes=scratch,
        name=name,
        compiler_params=pltpu.CompilerParams(vmem_limit_bytes=VMEM),
    )(*operands)


def pre0(*pieces):
    plane = buffer(24, ROWS0, LANES)
    scratch = [plane] * 7 + [buffer(20, 64, LANES)]
    out = (f32(7, KEPT0, KEPT_ROWS0, LANES), f32(6, 3, ROWS1, LANES), f32(4, ROWS1, LANES))
    return call(pre0_kernel, out, scratch, "pre0", *pieces)


def pre1(*pieces):
    plane = f32(DEPTH1, ROWS1, LANES)
    scratch = [buffer(DEPTH1, ROWS1, LANES), buffer(6, ROWS1, LANES), buffer(8, LANES)]
    out = (f32(16, 2 * LANES), f32(8, 2 * LANES), plane, f32(3, DEPTH1, ROWS1, LANES)) + (plane,) * 4
    return call(pre1_kernel, out, scratch, "pre1", *pieces)


def finish(*pieces):
    plane2 = buffer(DEPTH2 + 2, ROWS2, LANES)
    plane1 = buffer(DEPTH1, ROWS1, LANES)
    plane0 = buffer(KEPT0, KEPT_ROWS0, LANES)
    scratch = [buffer(2, 512, LANES), buffer(3, DEPTH2 + 2, ROWS2, LANES)] + [plane2] * 7 + [buffer(3, 128, LANES)]
    scratch += [plane1] * 2 + [buffer(DEPTH2 + 6, 24, LANES), buffer(8, 32, LANES)]
    scratch += [plane0] * 2 + [buffer(5, KEPT_ROWS0, LANES)]
    return call(finish_kernel, f32(2, 16, LANES), scratch, "finish", *pieces)


def layers_apart(value, steps):
    count = lax.axis_size("gx")
    ways = [(i, i + (LAYER * steps if i % 2 == 0 else -LAYER * steps)) for i in range(count)]
    return lax.ppermute(value, "gx", [(i, j) for i, j in ways if 0 <= j < count])


def columns_apart(value):
    count, wide = lax.axis_size("gx"), lax.axis_size("gy")
    ways = [
        (i * wide + j, i * wide + j + (1 if i % 2 == 0 else -1))
        for i in range(count)
        for j in range(wide)
        if 0 <= j + (1 if i % 2 == 0 else -1) < wide
    ]
    return lax.ppermute(value, ("gx", "gy"), ways)


def body(source, absorb, beta):
    members = lax.axis_size("gx")
    wide = lax.axis_size("gy")
    layers = members // LAYER
    near = [[LAYER * z + c for c in range(LAYER)] for z in range(layers)]
    chips = [[2 * chip, 2 * chip + 1] for chip in range(members // 2)]
    column = [[LAYER * z + c for z in range(layers)] for c in range(LAYER)]
    cores = [
        [(LAYER * z + 2 * chip + core) * wide + y for chip in range(2) for y in range(wide)]
        for z in range(layers)
        for core in range(2)
    ]
    first_core = lax.axis_index("gx") % 2 == 0

    def both(value):
        return lax.all_gather(value, "gx", axis_index_groups=chips)

    local = jnp.stack([source, absorb, beta])
    own = lax.all_gather(local, "gx", axis_index_groups=near)
    def tiles_of(arrays):
        return jnp.concatenate([x.reshape(-1, 8, LANES) for x in arrays])

    sides = columns_apart(own)
    outer = layers_apart(own, 1)
    sides = both(sides)
    layer = jnp.concatenate([sides[0], own, sides[1]], axis=-2)
    rims = jnp.concatenate([sides[0, ..., 8:, :], sides[1, ..., :8, :]], axis=-2)
    ends = jnp.concatenate([sides[0, ..., :8, :], sides[1, ..., 8:, :]], axis=-2)
    near2 = jnp.where(first_core, ends[2:, :2], ends[:2, :2])
    near3 = jnp.where(first_core, ends[1:, 2], ends[:3, 2])
    rest = layers_apart(tiles_of([rims, near2[:, 0], near2[:, 1], near3]), 1)
    kept0, tile, absorb1 = pre0(layer, both(tiles_of([outer, rest])))

    tiles = tiles_of([layers_apart(tile[1:5], 1), layers_apart(tile[..., 4:12, :], 2)])
    pay, rows1, *kept1 = pre1(tile, both(tiles), absorb1)

    rows = lax.all_to_all(pay, "gx", 0, 0, axis_index_groups=column)
    rows = jnp.concatenate([rows, rows1])
    rows = jnp.broadcast_to(rows, (2 * wide,) + rows.shape)
    rows = lax.all_to_all(rows, ("gx", "gy"), 0, 0, axis_index_groups=cores)
    packed = both(rows).reshape(-1, *rows.shape[1:])
    return finish(packed, *kept1, kept0)


def solution(mesh):
    placed = (P("gx", "gy", None), P("gx", "gy", None), P("gx", "gy", None))
    return jax.shard_map(
        body, mesh=mesh, in_specs=placed, out_specs=P("gx", "gy", None), check_vma=False
    )
```

```python
import jax
import jax.numpy as jnp
from jax import lax
from jax.experimental import pallas as pl
from jax.experimental.pallas import tpu as pltpu
from jax.sharding import PartitionSpec as P

SWEEPS = 4
BOTTOM = 8
LANES = 128
VMEM = 24 * 1024 * 1024

LAYER = 4
PACK = (1, 2, 4, 8)


def face(level):
    return 0.5 * 0.25**level


def chebyshev_table(count):
    centre = 1.125
    half_width = 0.875
    ratio = centre / half_width
    factor = 1.0 / ratio
    table = [(0.0, 1.0 / centre)]
    for order in range(1, count):
        fresh_factor = 1.0 / (2.0 * ratio - factor)
        table.append((fresh_factor * factor, 2.0 * fresh_factor / half_width))
        factor = fresh_factor
    return table


def position():
    return lax.axis_index("gx")


def column_position():
    return lax.axis_index("gy")


def lanes_of(rows):
    return lax.broadcasted_iota(jnp.int32, (rows, LANES), 1)


def rows_of(rows):
    return lax.broadcasted_iota(jnp.int32, (rows, LANES), 0)


def along(value, steps):
    return pltpu.roll(value, (-steps) % LANES, value.ndim - 1)


def across(value, steps):
    rows = value.shape[-2]
    return pltpu.roll(value, (-steps) % rows, value.ndim - 2)


class Packed:
    def __init__(self, pack, period, whole):
        self.pack = pack
        self.period = period
        self.whole = whole
        self.kept = {}

    def masks(self, value):
        if value.shape not in self.kept:
            pack, dims = self.pack, value.ndim
            lane = lax.broadcasted_iota(jnp.int32, value.shape, dims - 1)
            row = lax.broadcasted_iota(jnp.int32, value.shape, dims - 2) & (self.period - 1)
            inner = lane & (pack - 1)
            self.kept[value.shape] = dict(
                up=inner < pack - 1,
                down=inner > 0,
                third_last=lane >= LANES - pack,
                third_first=lane < pack,
                second_last=(row == self.period - 1) & (inner == pack - 1),
                second_first=(row == 0) & (inner == 0),
            )
        return self.kept[value.shape]

    def second_up(self, value):
        if self.pack == 1:
            return across(value, 1)
        mask = self.masks(value)["up"]
        return jnp.where(mask, along(value, 1), across(along(value, 1 - self.pack), 1))

    def second_down(self, value):
        if self.pack == 1:
            return across(value, -1)
        mask = self.masks(value)["down"]
        return jnp.where(mask, along(value, -1), across(along(value, self.pack - 1), -1))

    def faces(self, beta, half):
        mask = self.masks(beta)
        up = self.second_up(beta)
        if self.whole:
            up = jnp.where(mask["second_last"], 0.0, up)
        second = half * (beta + up)
        down = self.second_down(beta)
        if self.whole:
            down = jnp.where(mask["second_first"], 0.0, down)
        share = half * (beta + down) + second
        if self.whole:
            second = jnp.where(mask["second_last"], 0.0, second)
        third_up = jnp.where(mask["third_last"], 0.0, along(beta, self.pack))
        third = half * (beta + third_up)
        third_down = jnp.where(mask["third_first"], 0.0, along(beta, -self.pack))
        share = share + half * (beta + third_down) + third
        return second, jnp.where(mask["third_last"], 0.0, third), share

    def coupled(self, value, second, third):
        total = second * self.second_up(value) + self.second_down(second * value)
        total = total + third * along(value, self.pack)
        return total + along(third * value, -self.pack)


def pair_sum(value, width):
    low = (lax.broadcasted_iota(jnp.int32, value.shape, value.ndim - 1) & width) == 0
    return value + jnp.where(low, along(value, width), along(value, -width))


def residual(shape, source, parts, field, start, stop):
    diag, _, first, second, third = parts
    here = field[start:stop]
    total = source(start, stop) - diag[start:stop] * here
    total = total + first[start:stop] * field[start + 1 : stop + 1]
    total = total + first[start - 1 : stop - 1] * field[start - 1 : stop - 1]
    return total + shape.coupled(here, second[start:stop], third[start:stop])


def sweep(shape, orders, source, parts, buffers, ranges, chunk):
    inverse = parts[1]
    current, previous = buffers
    for (order, (carry, push)), (low, high) in zip(orders, ranges):
        for start in range(low, high, chunk):
            stop = min(start + chunk, high)
            rest = residual(shape, source, parts, current, start, stop)
            here = current[start:stop]
            fresh = here + push * (inverse[start:stop] * rest)
            if order > 0:
                fresh = fresh + carry * (here - previous[start:stop])
            previous[start:stop] = fresh
        current, previous = previous, current
    return current, previous


def begin(table, inverse, source, buffers, low, high, chunk):
    for start in range(low, high, chunk):
        stop = min(start + chunk, high)
        fresh = table[0][1] * (inverse[start:stop] * source(start, stop))
        buffers[0][start:stop] = fresh
        buffers[1][start:stop] = jnp.zeros_like(fresh)


ROWS0 = 48


CHUNK0 = 2


def level0_parts(shape, beta, absorb, parts, low, high):
    diag, inverse, first, second, third = parts
    half = face(0)
    first[low - 1 : low] = half * (beta(low - 1, low) + beta(low, low + 1))
    for start in range(low, high, CHUNK0):
        stop = min(start + CHUNK0, high)
        here = beta(start, stop)
        first[start:stop] = half * (here + beta(start + 1, stop + 1))
        lower = half * (beta(start - 1, stop - 1) + here)
        second[start:stop], third[start:stop], share = shape.faces(here, half)
        total = absorb(start, stop) + lower + first[start:stop] + share
        diag[start:stop] = total
        inverse[start:stop] = jnp.where(here > 0.0, 1.0 / total, 0.0)


def pairs(value):
    return jnp.stack([value[at] + value[at + 1] for at in range(0, value.shape[0], 2)])


def coarse_rows(ref, value):
    count = value.shape[0]
    zero = jnp.zeros((count, 8, LANES), jnp.float32)
    ref[0:count, 0:8, :] = zero
    ref[0:count, 8:56, :] = pair_sum(value, 1)
    ref[0:count, 56:64, :] = zero

    def take(offset):
        halves = [
            [ref[at, pl.ds(32 * half + offset, 8, stride=4), :] for half in range(2)]
            for at in range(count)
        ]
        return jnp.stack([jnp.concatenate(both) for both in halves])

    even = (lax.broadcasted_iota(jnp.int32, (count, ROWS1, LANES), 2) & 1) == 0
    return 0.125 * jnp.where(even, take(0) + take(1), take(2) + take(3))


KEPT0 = 10
KEPT_ROWS0 = 32


def pre0_kernel(
    own, outer, kept_out, rest_out, beta_out, diag_out, absorb_out,
    diag, inverse, first, second, third, one, two, tmp,
):
    zero = jnp.zeros((8, LANES), jnp.float32)

    def piece(kind):
        def planes(start, stop):
            found = []
            for plane in range(start, stop):
                part, member = plane // 8, plane % 8 // 2
                if part == 1:
                    found.append(own[member, kind, plane % 2])
                    continue
                side = part // 2
                at = 2 * (6 * member + 2 * kind + plane % 2)
                rows = [outer[side, at + tile] for tile in (48, 0, 1, 49)]
                reach = 3 if kind == 2 else 2
                near = member - (LAYER - reach) if side == 0 else member
                if 0 <= near < reach:
                    at = 96 + 2 * (2 * (2 * kind + near) + plane % 2)
                    ends = outer[side, at], outer[side, at + 1]
                else:
                    ends = zero, zero
                found.append(jnp.concatenate([ends[0], *rows, ends[1]]))
            return jnp.stack(found)

        return planes

    source, absorb, beta = piece(0), piece(1), piece(2)
    shape = Packed(1, ROWS0, False)
    parts = (diag, inverse, first, second, third)
    level0_parts(shape, beta, absorb, parts, 1, 23)
    table = chebyshev_table(SWEEPS)
    begin(table, inverse, source, (one, two), 1, 23, CHUNK0)
    ranges = [(1 + order, 23 - order) for order in range(1, SWEEPS)]
    current, previous = sweep(
        shape, list(enumerate(table))[1:], source, parts, (one, two), ranges, CHUNK0
    )
    previous[4:20] = source(4, 20)
    base = 2 * (position() % LAYER) + 4
    for plane in range(KEPT0):
        for number, kept in enumerate((current, previous) + parts):
            kept_out[number, plane] = kept[base + plane, 8:40, :]
    coarse = Packed(2, ROWS1, False)
    half = face(1)
    betas = coarse_rows(tmp.at[0:8], pairs(beta(4, 20)))
    wide = coarse_rows(tmp.at[8:14], pairs(absorb(6, 18)))
    rest = [residual(shape, source, parts, current, p, p + 2) for p in range(6, 18, 2)]
    rest_out[...] = coarse_rows(tmp.at[14:20], jnp.stack([x[0] + x[1] for x in rest]))
    here = betas[1:7]
    _, _, share = coarse.faces(here, half)
    beta_out[...] = betas
    diag_out[...] = wide + half * (here + betas[0:6]) + half * (here + betas[2:8]) + share
    absorb_out[...] = wide[1:5]


DEPTH1 = 16
ROWS1 = 16


def gather_level1(region, rest, beta, diag, outer):
    region[0, 1:6] = outer[0, 0:5]
    region[0, 6:10] = rest[1:5]
    region[0, 10:15] = outer[1, 0:5]
    region[1, 0:6] = outer[0, 5:11]
    region[1, 6:10] = beta[2:6]
    region[1, 10:16] = outer[1, 5:11]
    region[2, 1:6] = outer[0, 11:16]
    region[2, 6:10] = diag[1:5]
    region[2, 10:15] = outer[1, 11:16]


CHUNK1 = 4


def level1_parts(shape, region, inverse, first, second, third):
    half = face(1)
    beta = region.at[1]
    first[0:1] = half * (beta[0:1] + beta[1:2])
    for start in range(1, DEPTH1 - 1, CHUNK1):
        stop = min(start + CHUNK1, DEPTH1 - 1)
        here = beta[start:stop]
        second[start:stop], third[start:stop], _ = shape.faces(here, half)
        inverse[start:stop] = jnp.where(here > 0.0, 1.0 / region[2, start:stop], 0.0)
        first[start:stop] = half * (here + beta[start + 1 : stop + 1])


def coarser_rows(ref, value, start):
    ref[...] = pair_sum(pair_sum(value, 1), 2)
    inner = lanes_of(1) & 3
    rows = []
    for at in range(value.shape[0]):
        row = ref[at, start : start + 1, :]
        for offset in range(1, 4):
            row = jnp.where(inner == offset, ref[at, start + offset : start + offset + 1, :], row)
        rows.append(0.125 * row)
    return rows


def pre1_kernel(
    rest1, beta1, diag1, outer, absorb, pay_out, region, inverse, first, second, third,
    one, two, tmp, tile,
):
    gather_level1(region, rest1, beta1, diag1, outer)
    shape = Packed(2, ROWS1, False)
    level1_parts(shape, region, inverse, first, second, third)
    source = lambda start, stop: region[0, start:stop]
    parts = (region.at[2], inverse, first, second, third)
    table = chebyshev_table(SWEEPS)
    begin(table, inverse, source, (one, two), 2, 14, CHUNK1)
    ranges = [(2 + order, 14 - order) for order in range(1, SWEEPS)]
    current, _ = sweep(
        shape, list(enumerate(table))[1:], source, parts, (one, two), ranges, CHUNK1
    )
    rest = residual(shape, source, parts, current, 6, 10)
    totals = [pairs(rest), pairs(region[1, 6:10]), pairs(absorb[...])]
    rows = coarser_rows(tmp, jnp.concatenate(totals), 6)
    for at in range(6):
        tile[at : at + 1, :] = rows[at]
    tile[6:8, :] = jnp.zeros((2, LANES), jnp.float32)
    member = position() % LAYER
    tile[8:10, :] = tile[pl.ds(2 * member, 2), :]
    tile[10:12, :] = jnp.zeros((2, LANES), jnp.float32)
    tile[12:16, :] = current[6 + member, 6:10, :]
    whole = tile[8:16, :]
    for slot in range(16):
        pay_out[slot] = whole


DEPTH2 = 32
SLOT = 48
KIND_AT = (0, 2, 1)
ROWS2 = 8


CHUNK2 = 4


def level2_parts(shape, beta, absorb, parts):
    diag, inverse, first, second, third = parts
    half = face(2)
    first[0:1] = jnp.zeros((1, ROWS2, LANES), jnp.float32)
    for start in range(1, DEPTH2 + 1, CHUNK2):
        stop = start + CHUNK2
        here = beta[start:stop]
        upper = half * (here + beta[start + 1 : stop + 1])
        lower = half * (here + beta[start - 1 : stop - 1])
        second[start:stop], third[start:stop], share = shape.faces(here, half)
        total = absorb[start:stop] + lower + upper + share
        first[start:stop] = upper
        diag[start:stop] = total
        inverse[start:stop] = 1.0 / total


def bottom_rows(ref, planes):
    value = planes(1, DEPTH2 + 1)
    value = jnp.concatenate([value[at] + value[at + 1] for at in range(0, DEPTH2, 2)])
    ref[...] = pair_sum(pair_sum(value, 1), 4)
    inner = lanes_of(32) & 7
    total = None
    for offset in range(4):
        value = jnp.concatenate(
            [ref[pl.ds(32 * block + offset, 8, stride=4), :] for block in range(4)]
        )
        moved = along(value, 1 if offset % 2 == 0 else -1)
        same = 2 * offset + offset % 2
        value = jnp.where(inner == same, value, moved)
        total = value if total is None else jnp.where(inner >> 1 == offset, value, total)
    return 0.125 * total


def bottom_solve(source, absorb, beta):
    shape = Packed(8, 2, True)
    half = face(3)
    row = rows_of(32)
    last, initial = row >= 30, row < 2
    up = jnp.where(last, 0.0, across(beta, 2))
    down = jnp.where(initial, 0.0, across(beta, -2))
    second, third, share = shape.faces(beta, half)
    upper = half * (beta + up)
    diag = absorb + half * (beta + down) + upper + share
    first = jnp.where(last, 0.0, upper)
    inverse = 1.0 / diag
    table = chebyshev_table(BOTTOM)
    current = table[0][1] * (inverse * source)
    previous = jnp.zeros_like(current)
    for carry, push in table[1:]:
        rest = source - diag * current + first * across(current, 2) + across(first * current, -2)
        rest = rest + shape.coupled(current, second, third)
        fresh = current + carry * (current - previous) + push * (inverse * rest)
        current, previous = fresh, current
    return current


def bottom_prolong(ref, value):
    inner = lanes_of(32) & 7
    part = inner & 3
    back1, back2 = along(value, -1), along(value, -2)
    fore1, fore2 = along(value, 1), along(value, 2)
    low = jnp.where(part == 0, value, jnp.where(part == 3, back2, back1))
    high = jnp.where(part == 3, value, jnp.where(part == 0, fore2, fore1))
    left = inner < 4
    for offset in range(4):
        base = low if offset % 2 == 0 else high
        if offset < 2:
            moved = jnp.where(left, base, along(base, -4))
        else:
            moved = jnp.where(left, along(base, 4), base)
        for block in range(4):
            ref[pl.ds(32 * block + offset, 8, stride=4), :] = moved[8 * block : 8 * block + 8]


def solve23(gathered, rows2, parts2, one2, two2, tall):
    shape = Packed(4, ROWS2, True)
    zero = jnp.zeros((ROWS2, LANES), jnp.float32)
    for number in range(3):
        for plane in range(DEPTH2):
            at = SLOT * 8 * KIND_AT[number] + plane
            rows2[number, plane + 1] = gathered[pl.ds(at, 8, stride=SLOT), :]
    for ref in (rows2.at[1], one2, two2):
        ref[0] = zero
        ref[DEPTH2 + 1] = zero

    source2 = lambda start, stop: rows2[0, start:stop]
    level2_parts(shape, rows2.at[1], rows2.at[2], parts2)
    table = chebyshev_table(SWEEPS)
    begin(table, parts2[1], source2, (one2, two2), 1, DEPTH2 + 1, CHUNK2)
    everywhere = [(1, DEPTH2 + 1)] * SWEEPS
    current, previous = sweep(
        shape, list(enumerate(table))[1:], source2, parts2, (one2, two2), everywhere, CHUNK2
    )
    source3 = bottom_rows(
        tall.at[0], lambda start, stop: residual(shape, source2, parts2, current, start, stop)
    )
    absorb3 = bottom_rows(tall.at[1], lambda start, stop: rows2[2, start:stop])
    beta3 = bottom_rows(tall.at[2], lambda start, stop: rows2[1, start:stop])
    bottom_prolong(tall.at[0], bottom_solve(source3, absorb3, beta3))
    for plane in range(DEPTH2):
        pair = plane // 2
        current[plane + 1] = current[plane + 1] + tall[0, 8 * pair : 8 * pair + 8, :]
    current, previous = sweep(
        shape, list(enumerate(table)), source2, parts2, (current, previous), everywhere, CHUNK2
    )
    return current


def post1(packed, whole, region, parts, one, two, wide, tmp):
    inverse, first, second, third = parts
    shape = Packed(2, ROWS1, False)
    layer = position() // LAYER
    row = column_position() + 6
    zero = jnp.zeros((8, LANES), jnp.float32)
    for plane in range(DEPTH2 + 6):
        wide[plane, 0:8, :] = zero
        wide[plane, 16:24, :] = zero
        inside = 3 <= plane < DEPTH2 + 3
        wide[plane, 8:16, :] = whole[plane - 2] if inside else zero
    value = jnp.stack([wide[2 * layer + pair, pl.ds(row, 8), :] for pair in range(8)])
    inner = lax.broadcasted_iota(jnp.int32, value.shape, 2) & 3
    moved = {steps: along(value, steps) for steps in range(-3, 4) if steps}
    moved[0] = value
    for offset in range(4):
        picked = moved[offset]
        for lane in range(1, 4):
            picked = jnp.where(inner == lane, moved[offset - lane], picked)
        for pair in range(8):
            tmp[pair, pl.ds(offset, 8, stride=4), :] = picked[pair]
    place = column_position()
    columns = (
        (jnp.maximum(place - 1, 0), jnp.where(place > 0, 1.0, 0.0)),
        (place, 1.0),
        (jnp.minimum(place + 1, 7), jnp.where(place < 7, 1.0, 0.0)),
    )
    blank = jnp.zeros((2, LANES), jnp.float32)
    for plane in range(DEPTH1):
        member = (plane - 6) % LAYER
        at = 16 * (member % 2) + 8 * (member // 2)
        row = 32 + 4 * (plane // LAYER)
        one[plane, 0:2, :] = blank
        for number, (who, there) in enumerate(columns):
            start = 2 + 4 * number
            one[plane, start : start + 4, :] = there * packed[at + who, row : row + 4, :]
        one[plane, 14:16, :] = blank
    for plane in range(DEPTH1):
        one[plane] = one[plane] + tmp[plane // 2, 2:18, :]
    table = chebyshev_table(SWEEPS)
    ranges = [(order, DEPTH1 - order) for order in range(1, SWEEPS + 1)]
    current, _ = sweep(
        shape, list(enumerate(table)), lambda start, stop: region[0, start:stop],
        (region.at[2], inverse, first, second, third), (one, two), ranges, CHUNK1,
    )
    return current


def post0(kept, coarse, out, one, two, tmp):
    field, source = kept.at[0], kept.at[1]
    parts = tuple(kept.at[number] for number in range(2, 7))
    member = position() % LAYER
    shape = Packed(1, ROWS0, False)
    value = jnp.stack([coarse[4 + member + pair, 4:12, :] for pair in range(5)])
    even = (lax.broadcasted_iota(jnp.int32, value.shape, 2) & 1) == 0
    upper_rows = jnp.where(even, value, along(value, -1))
    lower_rows = jnp.where(even, along(value, 1), value)
    for pair in range(5):
        for offset in range(4):
            rows = upper_rows if offset < 2 else lower_rows
            tmp[pair, pl.ds(offset, 8, stride=4), :] = rows[pair]
    for plane in range(KEPT0):
        one[plane] = field[plane] + tmp[plane // 2]
    table = chebyshev_table(SWEEPS)
    ranges = [(1 + order, KEPT0 - 1 - order) for order in range(SWEEPS)]
    current, _ = sweep(
        shape, list(enumerate(table)), lambda start, stop: source[start:stop], parts,
        (one, two), ranges, CHUNK0,
    )
    out[...] = current[4:6, 8:24, :]


def finish_kernel(
    gathered, packed, region1, inverse1, first1, second1, third1, kept0, out,
    rows2, diag2, inverse2, first2, second2, third2, one2, two2, tall,
    one1, two1, wide1, tmp1, one0, two0, tmp0,
):
    parts2 = (diag2, inverse2, first2, second2, third2)
    whole = solve23(gathered, rows2, parts2, one2, two2, tall)
    parts1 = (inverse1, first1, second1, third1)
    coarse = post1(packed, whole, region1, parts1, one1, two1, wide1, tmp1)
    post0(kept0, coarse, out, one0, two0, tmp0)


def f32(*shape):
    return jax.ShapeDtypeStruct(shape, jnp.float32)


def buffer(*shape):
    return pltpu.VMEM(shape, jnp.float32)


def call(kernel, out, scratch, name, *operands):
    return pl.pallas_call(
        kernel,
        out_shape=out,
        scratch_shapes=scratch,
        name=name,
        compiler_params=pltpu.CompilerParams(vmem_limit_bytes=VMEM),
    )(*operands)


def pre0(*pieces):
    plane = buffer(24, ROWS0, LANES)
    scratch = [plane] * 7 + [buffer(20, 64, LANES)]
    coarse = lambda count: f32(count, ROWS1, LANES)
    out = (f32(7, KEPT0, KEPT_ROWS0, LANES), coarse(6), coarse(8), coarse(6), coarse(4))
    return call(pre0_kernel, out, scratch, "pre0", *pieces)


def pre1(*pieces):
    plane, work = f32(DEPTH1, ROWS1, LANES), buffer(DEPTH1, ROWS1, LANES)
    scratch = [work, work, buffer(6, ROWS1, LANES), buffer(16, LANES)]
    out = (f32(16, 8, LANES), f32(3, DEPTH1, ROWS1, LANES)) + (plane,) * 4
    return call(pre1_kernel, out, scratch, "pre1", *pieces)


def finish(*pieces):
    plane2 = buffer(DEPTH2 + 2, ROWS2, LANES)
    plane1 = buffer(DEPTH1, ROWS1, LANES)
    plane0 = buffer(KEPT0, KEPT_ROWS0, LANES)
    scratch = [buffer(3, DEPTH2 + 2, ROWS2, LANES)] + [plane2] * 7 + [buffer(3, 128, LANES)]
    scratch += [plane1] * 2 + [buffer(DEPTH2 + 6, 24, LANES), buffer(8, 32, LANES)]
    scratch += [plane0] * 2 + [buffer(5, KEPT_ROWS0, LANES)]
    return call(finish_kernel, f32(2, 16, LANES), scratch, "finish", *pieces)


def layers_apart(value, steps):
    count = lax.axis_size("gx")
    ways = [(i, i + (LAYER * steps if i % 2 == 0 else -LAYER * steps)) for i in range(count)]
    return lax.ppermute(value, "gx", [(i, j) for i, j in ways if 0 <= j < count])


def columns_apart(value):
    count, wide = lax.axis_size("gx"), lax.axis_size("gy")
    ways = [
        (i * wide + j, i * wide + j + (1 if i % 2 == 0 else -1))
        for i in range(count)
        for j in range(wide)
        if 0 <= j + (1 if i % 2 == 0 else -1) < wide
    ]
    return lax.ppermute(value, ("gx", "gy"), ways)


def body(source, absorb, beta):
    members = lax.axis_size("gx")
    wide = lax.axis_size("gy")
    layers = members // LAYER
    near = [[LAYER * z + c for c in range(LAYER)] for z in range(layers)]
    chips = [[2 * chip, 2 * chip + 1] for chip in range(members // 2)]
    column = [[LAYER * z + c for z in range(layers)] for c in range(LAYER)]
    cores = [
        [(LAYER * z + 2 * chip + core) * wide + y for chip in range(2) for y in range(wide)]
        for z in range(layers)
        for core in range(2)
    ]
    first_core = lax.axis_index("gx") % 2 == 0

    def both(value):
        return lax.all_gather(value, "gx", axis_index_groups=chips)

    local = jnp.stack([source, absorb, beta])
    own = lax.all_gather(local, "gx", axis_index_groups=near)
    def tiles_of(arrays):
        return jnp.concatenate([x.reshape(-1, 8, LANES) for x in arrays])

    sides = columns_apart(own)
    outer = layers_apart(own, 1)
    sides = both(sides)
    layer = jnp.concatenate([sides[0], own, sides[1]], axis=-2)
    rims = jnp.concatenate([sides[0, ..., 8:, :], sides[1, ..., :8, :]], axis=-2)
    ends = jnp.concatenate([sides[0, ..., :8, :], sides[1, ..., 8:, :]], axis=-2)
    near2 = jnp.where(first_core, ends[2:, :2], ends[:2, :2])
    near3 = jnp.where(first_core, ends[1:, 2], ends[:3, 2])
    rest = layers_apart(tiles_of([rims, near2[:, 0], near2[:, 1], near3]), 1)
    kept0, rest1, beta1, diag1, absorb1 = pre0(layer, both(tiles_of([outer, rest])))

    upwards = jnp.concatenate([rest1[0:5], beta1[0:6], diag1[0:5]])
    downwards = jnp.concatenate([rest1[1:6], beta1[2:8], diag1[1:6]])
    outer = both(layers_apart(jnp.where(first_core, upwards, downwards), 1))
    pay, *kept1 = pre1(rest1, beta1, diag1, outer, absorb1)

    rows = lax.all_to_all(pay, "gx", 0, 0, axis_index_groups=column)
    place = lax.axis_index("gx")
    start = place // LAYER + jnp.where(place % LAYER < 2, 1, 0)
    fields = jnp.pad(rows[:, 4:8], ((2, 2), (0, 0), (0, 0)))
    fields = lax.dynamic_slice_in_dim(fields, start, 4)
    rows = jnp.concatenate([rows[:, 0:2].reshape(-1, LANES), fields.reshape(-1, LANES)])
    rows = jnp.broadcast_to(rows, (2 * wide,) + rows.shape)
    rows = lax.all_to_all(rows, ("gx", "gy"), 0, 0, axis_index_groups=cores)
    packed = both(rows).reshape(-1, SLOT, LANES)
    return finish(packed.reshape(-1, LANES), packed, *kept1, kept0)


def solution(mesh):
    placed = (P("gx", "gy", None), P("gx", "gy", None), P("gx", "gy", None))
    return jax.shard_map(
        body, mesh=mesh, in_specs=placed, out_specs=P("gx", "gy", None), check_vma=False
    )
```

```python
import jax
import jax.numpy as jnp
from jax import lax
from jax.experimental import pallas as pl
from jax.experimental.pallas import tpu as pltpu
from jax.sharding import PartitionSpec as P

SWEEPS = 4
BOTTOM = 8
LANES = 128
VMEM = 24 * 1024 * 1024

LAYER = 4
PACK = (1, 2, 4, 8)


def face(level):
    return 0.5 * 0.25**level


def chebyshev_table(count):
    centre = 1.125
    half_width = 0.875
    ratio = centre / half_width
    factor = 1.0 / ratio
    table = [(0.0, 1.0 / centre)]
    for order in range(1, count):
        fresh_factor = 1.0 / (2.0 * ratio - factor)
        table.append((fresh_factor * factor, 2.0 * fresh_factor / half_width))
        factor = fresh_factor
    return table


def position():
    return lax.axis_index("gx")


def column_position():
    return lax.axis_index("gy")


def lanes_of(rows):
    return lax.broadcasted_iota(jnp.int32, (rows, LANES), 1)


def rows_of(rows):
    return lax.broadcasted_iota(jnp.int32, (rows, LANES), 0)


def along(value, steps):
    return pltpu.roll(value, (-steps) % LANES, value.ndim - 1)


def across(value, steps):
    rows = value.shape[-2]
    return pltpu.roll(value, (-steps) % rows, value.ndim - 2)


class Packed:
    def __init__(self, pack, period, whole):
        self.pack = pack
        self.period = period
        self.whole = whole
        self.kept = {}

    def masks(self, value):
        if value.shape not in self.kept:
            pack, dims = self.pack, value.ndim
            lane = lax.broadcasted_iota(jnp.int32, value.shape, dims - 1)
            row = lax.broadcasted_iota(jnp.int32, value.shape, dims - 2) & (self.period - 1)
            inner = lane & (pack - 1)
            self.kept[value.shape] = dict(
                up=inner < pack - 1,
                down=inner > 0,
                third_last=lane >= LANES - pack,
                third_first=lane < pack,
                second_last=(row == self.period - 1) & (inner == pack - 1),
                second_first=(row == 0) & (inner == 0),
            )
        return self.kept[value.shape]

    def second_up(self, value):
        if self.pack == 1:
            return across(value, 1)
        mask = self.masks(value)["up"]
        return jnp.where(mask, along(value, 1), across(along(value, 1 - self.pack), 1))

    def second_down(self, value):
        if self.pack == 1:
            return across(value, -1)
        mask = self.masks(value)["down"]
        return jnp.where(mask, along(value, -1), across(along(value, self.pack - 1), -1))

    def faces(self, beta, half):
        mask = self.masks(beta)
        up = self.second_up(beta)
        if self.whole:
            up = jnp.where(mask["second_last"], 0.0, up)
        second = half * (beta + up)
        down = self.second_down(beta)
        if self.whole:
            down = jnp.where(mask["second_first"], 0.0, down)
        share = half * (beta + down) + second
        if self.whole:
            second = jnp.where(mask["second_last"], 0.0, second)
        third_up = jnp.where(mask["third_last"], 0.0, along(beta, self.pack))
        third = half * (beta + third_up)
        third_down = jnp.where(mask["third_first"], 0.0, along(beta, -self.pack))
        share = share + half * (beta + third_down) + third
        return second, jnp.where(mask["third_last"], 0.0, third), share

    def coupled(self, value, second, third):
        total = second * self.second_up(value) + self.second_down(second * value)
        total = total + third * along(value, self.pack)
        return total + along(third * value, -self.pack)


def pair_sum(value, width):
    low = (lax.broadcasted_iota(jnp.int32, value.shape, value.ndim - 1) & width) == 0
    return value + jnp.where(low, along(value, width), along(value, -width))


def residual(shape, source, parts, field, start, stop):
    diag, _, first, second, third = parts
    here = field[start:stop]
    total = source(start, stop) - diag[start:stop] * here
    total = total + first[start:stop] * field[start + 1 : stop + 1]
    total = total + first[start - 1 : stop - 1] * field[start - 1 : stop - 1]
    return total + shape.coupled(here, second[start:stop], third[start:stop])


def sweep(shape, orders, source, parts, buffers, ranges, chunk):
    inverse = parts[1]
    current, previous = buffers
    for (order, (carry, push)), (low, high) in zip(orders, ranges):
        for start in range(low, high, chunk):
            stop = min(start + chunk, high)
            rest = residual(shape, source, parts, current, start, stop)
            here = current[start:stop]
            fresh = here + push * (inverse[start:stop] * rest)
            if order > 0:
                fresh = fresh + carry * (here - previous[start:stop])
            previous[start:stop] = fresh
        current, previous = previous, current
    return current, previous


def begin(table, inverse, source, buffers, low, high, chunk):
    for start in range(low, high, chunk):
        stop = min(start + chunk, high)
        fresh = table[0][1] * (inverse[start:stop] * source(start, stop))
        buffers[0][start:stop] = fresh
        buffers[1][start:stop] = jnp.zeros_like(fresh)


ROWS0 = 48


CHUNK0 = 2


def level0_parts(shape, beta, absorb, parts, low, high):
    diag, inverse, first, second, third = parts
    half = face(0)
    first[low - 1 : low] = half * (beta(low - 1, low) + beta(low, low + 1))
    for start in range(low, high, CHUNK0):
        stop = min(start + CHUNK0, high)
        here = beta(start, stop)
        first[start:stop] = half * (here + beta(start + 1, stop + 1))
        lower = half * (beta(start - 1, stop - 1) + here)
        second[start:stop], third[start:stop], share = shape.faces(here, half)
        total = absorb(start, stop) + lower + first[start:stop] + share
        diag[start:stop] = total
        inverse[start:stop] = jnp.where(here > 0.0, 1.0 / total, 0.0)


def pairs(value):
    return jnp.stack([value[at] + value[at + 1] for at in range(0, value.shape[0], 2)])


def coarse_rows(ref, value):
    count = value.shape[0]
    zero = jnp.zeros((count, 8, LANES), jnp.float32)
    ref[0:count, 0:8, :] = zero
    ref[0:count, 8:56, :] = pair_sum(value, 1)
    ref[0:count, 56:64, :] = zero

    def take(offset):
        halves = [
            [ref[at, pl.ds(32 * half + offset, 8, stride=4), :] for half in range(2)]
            for at in range(count)
        ]
        return jnp.stack([jnp.concatenate(both) for both in halves])

    even = (lax.broadcasted_iota(jnp.int32, (count, ROWS1, LANES), 2) & 1) == 0
    return 0.125 * jnp.where(even, take(0) + take(1), take(2) + take(3))


KEPT0 = 10
KEPT_ROWS0 = 32


def pre0_kernel(
    own, outer, kept_out, rest_out, beta_out, diag_out, absorb_out,
    diag, inverse, first, second, third, one, two, tmp,
):
    zero = jnp.zeros((8, LANES), jnp.float32)

    def piece(kind):
        def planes(start, stop):
            found = []
            for plane in range(start, stop):
                part, member = plane // 8, plane % 8 // 2
                if part == 1:
                    found.append(own[member, kind, plane % 2])
                    continue
                side = part // 2
                at = 2 * (6 * member + 2 * kind + plane % 2)
                rows = [outer[side, at + tile] for tile in (48, 0, 1, 49)]
                reach = 3 if kind == 2 else 2
                near = member - (LAYER - reach) if side == 0 else member
                if 0 <= near < reach:
                    at = 96 + 2 * (2 * (2 * kind + near) + plane % 2)
                    ends = outer[side, at], outer[side, at + 1]
                else:
                    ends = zero, zero
                found.append(jnp.concatenate([ends[0], *rows, ends[1]]))
            return jnp.stack(found)

        return planes

    source, absorb, beta = piece(0), piece(1), piece(2)
    shape = Packed(1, ROWS0, False)
    parts = (diag, inverse, first, second, third)
    level0_parts(shape, beta, absorb, parts, 1, 23)
    table = chebyshev_table(SWEEPS)
    begin(table, inverse, source, (one, two), 1, 23, CHUNK0)
    ranges = [(1 + order, 23 - order) for order in range(1, SWEEPS)]
    current, previous = sweep(
        shape, list(enumerate(table))[1:], source, parts, (one, two), ranges, CHUNK0
    )
    previous[4:20] = source(4, 20)
    base = 2 * (position() % LAYER) + 4
    for plane in range(KEPT0):
        for number, kept in enumerate((current, previous) + parts):
            kept_out[number, plane] = kept[base + plane, 8:40, :]
    coarse = Packed(2, ROWS1, False)
    half = face(1)
    betas = coarse_rows(tmp.at[0:8], pairs(beta(4, 20)))
    wide = coarse_rows(tmp.at[8:14], pairs(absorb(6, 18)))
    rest = [residual(shape, source, parts, current, p, p + 2) for p in range(6, 18, 2)]
    rest_out[...] = coarse_rows(tmp.at[14:20], jnp.stack([x[0] + x[1] for x in rest]))
    here = betas[1:7]
    _, _, share = coarse.faces(here, half)
    beta_out[...] = betas
    diag_out[...] = wide + half * (here + betas[0:6]) + half * (here + betas[2:8]) + share
    absorb_out[...] = wide[1:5]


DEPTH1 = 16
ROWS1 = 16


def gather_level1(region, rest, beta, diag, outer):
    region[0, 1:6] = outer[0, 0:5]
    region[0, 6:10] = rest[1:5]
    region[0, 10:15] = outer[1, 0:5]
    region[1, 0:6] = outer[0, 5:11]
    region[1, 6:10] = beta[2:6]
    region[1, 10:16] = outer[1, 5:11]
    region[2, 1:6] = outer[0, 11:16]
    region[2, 6:10] = diag[1:5]
    region[2, 10:15] = outer[1, 11:16]


CHUNK1 = 4


def level1_parts(shape, region, inverse, first, second, third):
    half = face(1)
    beta = region.at[1]
    first[0:1] = half * (beta[0:1] + beta[1:2])
    for start in range(1, DEPTH1 - 1, CHUNK1):
        stop = min(start + CHUNK1, DEPTH1 - 1)
        here = beta[start:stop]
        second[start:stop], third[start:stop], _ = shape.faces(here, half)
        inverse[start:stop] = jnp.where(here > 0.0, 1.0 / region[2, start:stop], 0.0)
        first[start:stop] = half * (here + beta[start + 1 : stop + 1])


def coarser_rows(ref, value, start):
    ref[...] = pair_sum(pair_sum(value, 1), 2)
    inner = lanes_of(1) & 3
    rows = []
    for at in range(value.shape[0]):
        row = ref[at, start : start + 1, :]
        for offset in range(1, 4):
            row = jnp.where(inner == offset, ref[at, start + offset : start + offset + 1, :], row)
        rows.append(0.125 * row)
    return rows


def pre1_kernel(
    rest1, beta1, diag1, outer, absorb, pay_out, region, inverse, first, second, third,
    one, two, tmp, tile,
):
    gather_level1(region, rest1, beta1, diag1, outer)
    shape = Packed(2, ROWS1, False)
    level1_parts(shape, region, inverse, first, second, third)
    source = lambda start, stop: region[0, start:stop]
    parts = (region.at[2], inverse, first, second, third)
    table = chebyshev_table(SWEEPS)
    begin(table, inverse, source, (one, two), 2, 14, CHUNK1)
    ranges = [(2 + order, 14 - order) for order in range(1, SWEEPS)]
    current, _ = sweep(
        shape, list(enumerate(table))[1:], source, parts, (one, two), ranges, CHUNK1
    )
    rest = residual(shape, source, parts, current, 6, 10)
    totals = [pairs(rest), pairs(region[1, 6:10]), pairs(absorb[...])]
    rows = coarser_rows(tmp, jnp.concatenate(totals), 6)
    for at in range(6):
        tile[at : at + 1, :] = rows[at]
    tile[6:8, :] = jnp.zeros((2, LANES), jnp.float32)
    member = position() % LAYER
    tile[8:10, :] = tile[pl.ds(2 * member, 2), :]
    tile[10:14, :] = current[6 + member, 6:10, :]
    for at in range(6):
        row = jnp.broadcast_to(tile[8 + at : 9 + at, :], (16, LANES))
        pay_out[:, at * LANES : (at + 1) * LANES] = row


DEPTH2 = 32
SLOT = 48
KIND_AT = (0, 2, 1)
ROWS2 = 8


CHUNK2 = 4


def level2_parts(shape, beta, absorb, parts):
    diag, inverse, first, second, third = parts
    half = face(2)
    first[0:1] = jnp.zeros((1, ROWS2, LANES), jnp.float32)
    for start in range(1, DEPTH2 + 1, CHUNK2):
        stop = start + CHUNK2
        here = beta[start:stop]
        upper = half * (here + beta[start + 1 : stop + 1])
        lower = half * (here + beta[start - 1 : stop - 1])
        second[start:stop], third[start:stop], share = shape.faces(here, half)
        total = absorb[start:stop] + lower + upper + share
        first[start:stop] = upper
        diag[start:stop] = total
        inverse[start:stop] = 1.0 / total


def bottom_rows(ref, planes):
    value = planes(1, DEPTH2 + 1)
    value = jnp.concatenate([value[at] + value[at + 1] for at in range(0, DEPTH2, 2)])
    ref[...] = pair_sum(pair_sum(value, 1), 4)
    inner = lanes_of(32) & 7
    total = None
    for offset in range(4):
        value = jnp.concatenate(
            [ref[pl.ds(32 * block + offset, 8, stride=4), :] for block in range(4)]
        )
        moved = along(value, 1 if offset % 2 == 0 else -1)
        same = 2 * offset + offset % 2
        value = jnp.where(inner == same, value, moved)
        total = value if total is None else jnp.where(inner >> 1 == offset, value, total)
    return 0.125 * total


def bottom_solve(source, absorb, beta):
    shape = Packed(8, 2, True)
    half = face(3)
    row = rows_of(32)
    last, initial = row >= 30, row < 2
    up = jnp.where(last, 0.0, across(beta, 2))
    down = jnp.where(initial, 0.0, across(beta, -2))
    second, third, share = shape.faces(beta, half)
    upper = half * (beta + up)
    diag = absorb + half * (beta + down) + upper + share
    first = jnp.where(last, 0.0, upper)
    inverse = 1.0 / diag
    table = chebyshev_table(BOTTOM)
    current = table[0][1] * (inverse * source)
    previous = jnp.zeros_like(current)
    for carry, push in table[1:]:
        rest = source - diag * current + first * across(current, 2) + across(first * current, -2)
        rest = rest + shape.coupled(current, second, third)
        fresh = current + carry * (current - previous) + push * (inverse * rest)
        current, previous = fresh, current
    return current


def bottom_prolong(ref, value):
    inner = lanes_of(32) & 7
    part = inner & 3
    back1, back2 = along(value, -1), along(value, -2)
    fore1, fore2 = along(value, 1), along(value, 2)
    low = jnp.where(part == 0, value, jnp.where(part == 3, back2, back1))
    high = jnp.where(part == 3, value, jnp.where(part == 0, fore2, fore1))
    left = inner < 4
    for offset in range(4):
        base = low if offset % 2 == 0 else high
        if offset < 2:
            moved = jnp.where(left, base, along(base, -4))
        else:
            moved = jnp.where(left, along(base, 4), base)
        for block in range(4):
            ref[pl.ds(32 * block + offset, 8, stride=4), :] = moved[8 * block : 8 * block + 8]


def solve23(gathered, rows2, parts2, one2, two2, tall):
    shape = Packed(4, ROWS2, True)
    zero = jnp.zeros((ROWS2, LANES), jnp.float32)
    for number in range(3):
        for plane in range(DEPTH2):
            at = SLOT * 8 * KIND_AT[number] + plane
            rows2[number, plane + 1] = gathered[pl.ds(at, 8, stride=SLOT), :]
    for ref in (rows2.at[1], one2, two2):
        ref[0] = zero
        ref[DEPTH2 + 1] = zero

    source2 = lambda start, stop: rows2[0, start:stop]
    level2_parts(shape, rows2.at[1], rows2.at[2], parts2)
    table = chebyshev_table(SWEEPS)
    begin(table, parts2[1], source2, (one2, two2), 1, DEPTH2 + 1, CHUNK2)
    everywhere = [(1, DEPTH2 + 1)] * SWEEPS
    current, previous = sweep(
        shape, list(enumerate(table))[1:], source2, parts2, (one2, two2), everywhere, CHUNK2
    )
    source3 = bottom_rows(
        tall.at[0], lambda start, stop: residual(shape, source2, parts2, current, start, stop)
    )
    absorb3 = bottom_rows(tall.at[1], lambda start, stop: rows2[2, start:stop])
    beta3 = bottom_rows(tall.at[2], lambda start, stop: rows2[1, start:stop])
    bottom_prolong(tall.at[0], bottom_solve(source3, absorb3, beta3))
    for plane in range(DEPTH2):
        pair = plane // 2
        current[plane + 1] = current[plane + 1] + tall[0, 8 * pair : 8 * pair + 8, :]
    current, previous = sweep(
        shape, list(enumerate(table)), source2, parts2, (current, previous), everywhere, CHUNK2
    )
    return current


def post1(packed, whole, region, parts, one, two, wide, tmp):
    inverse, first, second, third = parts
    shape = Packed(2, ROWS1, False)
    layer = position() // LAYER
    row = column_position() + 6
    zero = jnp.zeros((8, LANES), jnp.float32)
    for plane in range(DEPTH2 + 6):
        wide[plane, 0:8, :] = zero
        wide[plane, 16:24, :] = zero
        inside = 3 <= plane < DEPTH2 + 3
        wide[plane, 8:16, :] = whole[plane - 2] if inside else zero
    value = jnp.stack([wide[2 * layer + pair, pl.ds(row, 8), :] for pair in range(8)])
    inner = lax.broadcasted_iota(jnp.int32, value.shape, 2) & 3
    moved = {steps: along(value, steps) for steps in range(-3, 4) if steps}
    moved[0] = value
    for offset in range(4):
        picked = moved[offset]
        for lane in range(1, 4):
            picked = jnp.where(inner == lane, moved[offset - lane], picked)
        for pair in range(8):
            tmp[pair, pl.ds(offset, 8, stride=4), :] = picked[pair]
    place = column_position()
    columns = (
        (jnp.maximum(place - 1, 0), jnp.where(place > 0, 1.0, 0.0)),
        (place, 1.0),
        (jnp.minimum(place + 1, 7), jnp.where(place < 7, 1.0, 0.0)),
    )
    blank = jnp.zeros((2, LANES), jnp.float32)
    for plane in range(DEPTH1):
        member = (plane - 6) % LAYER
        at = 16 * (member % 2) + 8 * (member // 2)
        row = 32 + 4 * (plane // LAYER)
        one[plane, 0:2, :] = blank
        for number, (who, there) in enumerate(columns):
            start = 2 + 4 * number
            one[plane, start : start + 4, :] = there * packed[at + who, row : row + 4, :]
        one[plane, 14:16, :] = blank
    for plane in range(DEPTH1):
        one[plane] = one[plane] + tmp[plane // 2, 2:18, :]
    table = chebyshev_table(SWEEPS)
    ranges = [(order, DEPTH1 - order) for order in range(1, SWEEPS + 1)]
    current, _ = sweep(
        shape, list(enumerate(table)), lambda start, stop: region[0, start:stop],
        (region.at[2], inverse, first, second, third), (one, two), ranges, CHUNK1,
    )
    return current


def post0(kept, coarse, out, one, two, tmp):
    field, source = kept.at[0], kept.at[1]
    parts = tuple(kept.at[number] for number in range(2, 7))
    member = position() % LAYER
    shape = Packed(1, ROWS0, False)
    value = jnp.stack([coarse[4 + member + pair, 4:12, :] for pair in range(5)])
    even = (lax.broadcasted_iota(jnp.int32, value.shape, 2) & 1) == 0
    upper_rows = jnp.where(even, value, along(value, -1))
    lower_rows = jnp.where(even, along(value, 1), value)
    for pair in range(5):
        for offset in range(4):
            rows = upper_rows if offset < 2 else lower_rows
            tmp[pair, pl.ds(offset, 8, stride=4), :] = rows[pair]
    for plane in range(KEPT0):
        one[plane] = field[plane] + tmp[plane // 2]
    table = chebyshev_table(SWEEPS)
    ranges = [(1 + order, KEPT0 - 1 - order) for order in range(SWEEPS)]
    current, _ = sweep(
        shape, list(enumerate(table)), lambda start, stop: source[start:stop], parts,
        (one, two), ranges, CHUNK0,
    )
    out[...] = current[4:6, 8:24, :]


def finish_kernel(
    gathered, packed, region1, inverse1, first1, second1, third1, kept0, out,
    rows2, diag2, inverse2, first2, second2, third2, one2, two2, tall,
    one1, two1, wide1, tmp1, one0, two0, tmp0,
):
    parts2 = (diag2, inverse2, first2, second2, third2)
    whole = solve23(gathered, rows2, parts2, one2, two2, tall)
    parts1 = (inverse1, first1, second1, third1)
    coarse = post1(packed, whole, region1, parts1, one1, two1, wide1, tmp1)
    post0(kept0, coarse, out, one0, two0, tmp0)


def f32(*shape):
    return jax.ShapeDtypeStruct(shape, jnp.float32)


def buffer(*shape):
    return pltpu.VMEM(shape, jnp.float32)


def call(kernel, out, scratch, name, *operands):
    return pl.pallas_call(
        kernel,
        out_shape=out,
        scratch_shapes=scratch,
        name=name,
        compiler_params=pltpu.CompilerParams(vmem_limit_bytes=VMEM),
    )(*operands)


def pre0(*pieces):
    plane = buffer(24, ROWS0, LANES)
    scratch = [plane] * 7 + [buffer(20, 64, LANES)]
    coarse = lambda count: f32(count, ROWS1, LANES)
    out = (f32(7, KEPT0, KEPT_ROWS0, LANES), coarse(6), coarse(8), coarse(6), coarse(4))
    return call(pre0_kernel, out, scratch, "pre0", *pieces)


def pre1(*pieces):
    plane, work = f32(DEPTH1, ROWS1, LANES), buffer(DEPTH1, ROWS1, LANES)
    scratch = [work, work, buffer(6, ROWS1, LANES), buffer(16, LANES)]
    out = (f32(16, 6 * LANES), f32(3, DEPTH1, ROWS1, LANES)) + (plane,) * 4
    return call(pre1_kernel, out, scratch, "pre1", *pieces)


def finish(*pieces):
    plane2 = buffer(DEPTH2 + 2, ROWS2, LANES)
    plane1 = buffer(DEPTH1, ROWS1, LANES)
    plane0 = buffer(KEPT0, KEPT_ROWS0, LANES)
    scratch = [buffer(3, DEPTH2 + 2, ROWS2, LANES)] + [plane2] * 7 + [buffer(3, 128, LANES)]
    scratch += [plane1] * 2 + [buffer(DEPTH2 + 6, 24, LANES), buffer(8, 32, LANES)]
    scratch += [plane0] * 2 + [buffer(5, KEPT_ROWS0, LANES)]
    return call(finish_kernel, f32(2, 16, LANES), scratch, "finish", *pieces)


def layers_apart(value, steps):
    count = lax.axis_size("gx")
    ways = [(i, i + (LAYER * steps if i % 2 == 0 else -LAYER * steps)) for i in range(count)]
    return lax.ppermute(value, "gx", [(i, j) for i, j in ways if 0 <= j < count])


def columns_apart(value):
    count, wide = lax.axis_size("gx"), lax.axis_size("gy")
    ways = [
        (i * wide + j, i * wide + j + (1 if i % 2 == 0 else -1))
        for i in range(count)
        for j in range(wide)
        if 0 <= j + (1 if i % 2 == 0 else -1) < wide
    ]
    return lax.ppermute(value, ("gx", "gy"), ways)


def body(source, absorb, beta):
    members = lax.axis_size("gx")
    wide = lax.axis_size("gy")
    layers = members // LAYER
    near = [[LAYER * z + c for c in range(LAYER)] for z in range(layers)]
    chips = [[2 * chip, 2 * chip + 1] for chip in range(members // 2)]
    column = [[LAYER * z + c for z in range(layers)] for c in range(LAYER)]
    cores = [
        [(LAYER * z + 2 * chip + core) * wide + y for chip in range(2) for y in range(wide)]
        for z in range(layers)
        for core in range(2)
    ]
    first_core = lax.axis_index("gx") % 2 == 0

    def both(value):
        return lax.all_gather(value, "gx", axis_index_groups=chips)

    local = jnp.stack([source, absorb, beta])
    own = lax.all_gather(local, "gx", axis_index_groups=near)
    def tiles_of(arrays):
        return jnp.concatenate([x.reshape(-1, 8, LANES) for x in arrays])

    sides = columns_apart(own)
    outer = layers_apart(own, 1)
    sides = both(sides)
    layer = jnp.concatenate([sides[0], own, sides[1]], axis=-2)
    rims = jnp.concatenate([sides[0, ..., 8:, :], sides[1, ..., :8, :]], axis=-2)
    ends = jnp.concatenate([sides[0, ..., :8, :], sides[1, ..., 8:, :]], axis=-2)
    near2 = jnp.where(first_core, ends[2:, :2], ends[:2, :2])
    near3 = jnp.where(first_core, ends[1:, 2], ends[:3, 2])
    rest = layers_apart(tiles_of([rims, near2[:, 0], near2[:, 1], near3]), 1)
    kept0, rest1, beta1, diag1, absorb1 = pre0(layer, both(tiles_of([outer, rest])))

    upwards = jnp.concatenate([rest1[0:5], beta1[0:6], diag1[0:5]])
    downwards = jnp.concatenate([rest1[1:6], beta1[2:8], diag1[1:6]])
    outer = both(layers_apart(jnp.where(first_core, upwards, downwards), 1))
    pay, *kept1 = pre1(rest1, beta1, diag1, outer, absorb1)

    place = lax.axis_index("gx")
    start = (place >> 2) + (((place & 3) ^ 3) >> 1)
    pay, start = lax.optimization_barrier((pay, start))
    rows = lax.all_to_all(pay, "gx", 0, 0, axis_index_groups=column)
    rows, start = lax.optimization_barrier((rows, start))
    fields = jnp.pad(rows[:, 2 * LANES :], ((2, 2), (0, 0)))
    fields = lax.dynamic_slice_in_dim(fields, start, 4)
    rows = jnp.concatenate([x.reshape(-1, LANES) for x in (rows[:, : 2 * LANES], fields)])
    rows = jnp.broadcast_to(rows, (2 * wide,) + rows.shape)
    rows = lax.all_to_all(rows, ("gx", "gy"), 0, 0, axis_index_groups=cores)
    packed = both(rows).reshape(-1, SLOT, LANES)
    return finish(packed.reshape(-1, LANES), packed, *kept1, kept0)


def solution(mesh):
    placed = (P("gx", "gy", None), P("gx", "gy", None), P("gx", "gy", None))
    return jax.shard_map(
        body, mesh=mesh, in_specs=placed, out_specs=P("gx", "gy", None), check_vma=False
    )
```

```python
import jax
import jax.numpy as jnp
from jax import lax
from jax.experimental import pallas as pl
from jax.experimental.pallas import tpu as pltpu
from jax.sharding import PartitionSpec as P

SWEEPS = 4
BOTTOM = 8
LANES = 128
VMEM = 24 * 1024 * 1024

LAYER = 4
PACK = (1, 2, 4, 8)


def face(level):
    return 0.5 * 0.25**level


def chebyshev_table(count):
    centre = 1.125
    half_width = 0.875
    ratio = centre / half_width
    factor = 1.0 / ratio
    table = [(0.0, 1.0 / centre)]
    for order in range(1, count):
        fresh_factor = 1.0 / (2.0 * ratio - factor)
        table.append((fresh_factor * factor, 2.0 * fresh_factor / half_width))
        factor = fresh_factor
    return table


def position():
    return lax.axis_index("gx")


def column_position():
    return lax.axis_index("gy")


def lanes_of(rows):
    return lax.broadcasted_iota(jnp.int32, (rows, LANES), 1)


def rows_of(rows):
    return lax.broadcasted_iota(jnp.int32, (rows, LANES), 0)


def along(value, steps):
    return pltpu.roll(value, (-steps) % LANES, value.ndim - 1)


def across(value, steps):
    rows = value.shape[-2]
    return pltpu.roll(value, (-steps) % rows, value.ndim - 2)


class Packed:
    def __init__(self, pack, period, whole):
        self.pack = pack
        self.period = period
        self.whole = whole
        self.kept = {}

    def masks(self, value):
        if value.shape not in self.kept:
            pack, dims = self.pack, value.ndim
            lane = lax.broadcasted_iota(jnp.int32, value.shape, dims - 1)
            row = lax.broadcasted_iota(jnp.int32, value.shape, dims - 2) & (self.period - 1)
            inner = lane & (pack - 1)
            self.kept[value.shape] = dict(
                up=inner < pack - 1,
                down=inner > 0,
                third_last=lane >= LANES - pack,
                third_first=lane < pack,
                second_last=(row == self.period - 1) & (inner == pack - 1),
                second_first=(row == 0) & (inner == 0),
            )
        return self.kept[value.shape]

    def second_up(self, value):
        if self.pack == 1:
            return across(value, 1)
        mask = self.masks(value)["up"]
        return jnp.where(mask, along(value, 1), across(along(value, 1 - self.pack), 1))

    def second_down(self, value):
        if self.pack == 1:
            return across(value, -1)
        mask = self.masks(value)["down"]
        return jnp.where(mask, along(value, -1), across(along(value, self.pack - 1), -1))

    def faces(self, beta, half):
        mask = self.masks(beta)
        up = self.second_up(beta)
        if self.whole:
            up = jnp.where(mask["second_last"], 0.0, up)
        second = half * (beta + up)
        down = self.second_down(beta)
        if self.whole:
            down = jnp.where(mask["second_first"], 0.0, down)
        share = half * (beta + down) + second
        if self.whole:
            second = jnp.where(mask["second_last"], 0.0, second)
        third_up = jnp.where(mask["third_last"], 0.0, along(beta, self.pack))
        third = half * (beta + third_up)
        third_down = jnp.where(mask["third_first"], 0.0, along(beta, -self.pack))
        share = share + half * (beta + third_down) + third
        return second, jnp.where(mask["third_last"], 0.0, third), share

    def coupled(self, value, second, third):
        total = second * self.second_up(value) + self.second_down(second * value)
        total = total + third * along(value, self.pack)
        return total + along(third * value, -self.pack)


def pair_sum(value, width):
    low = (lax.broadcasted_iota(jnp.int32, value.shape, value.ndim - 1) & width) == 0
    return value + jnp.where(low, along(value, width), along(value, -width))


def residual(shape, source, parts, field, start, stop):
    diag, _, first, second, third = parts
    here = field[start:stop]
    total = source(start, stop) - diag[start:stop] * here
    total = total + first[start:stop] * field[start + 1 : stop + 1]
    total = total + first[start - 1 : stop - 1] * field[start - 1 : stop - 1]
    return total + shape.coupled(here, second[start:stop], third[start:stop])


def sweep(shape, orders, source, parts, buffers, ranges, chunk):
    inverse = parts[1]
    current, previous = buffers
    for (order, (carry, push)), (low, high) in zip(orders, ranges):
        for start in range(low, high, chunk):
            stop = min(start + chunk, high)
            rest = residual(shape, source, parts, current, start, stop)
            here = current[start:stop]
            fresh = here + push * (inverse[start:stop] * rest)
            if order > 0:
                fresh = fresh + carry * (here - previous[start:stop])
            previous[start:stop] = fresh
        current, previous = previous, current
    return current, previous


def begin(table, inverse, source, buffers, low, high, chunk):
    for start in range(low, high, chunk):
        stop = min(start + chunk, high)
        fresh = table[0][1] * (inverse[start:stop] * source(start, stop))
        buffers[0][start:stop] = fresh
        buffers[1][start:stop] = jnp.zeros_like(fresh)


ROWS0 = 48


CHUNK0 = 2


def level0_parts(shape, beta, absorb, parts, low, high):
    diag, inverse, first, second, third = parts
    half = face(0)
    first[low - 1 : low] = half * (beta(low - 1, low) + beta(low, low + 1))
    for start in range(low, high, CHUNK0):
        stop = min(start + CHUNK0, high)
        here = beta(start, stop)
        first[start:stop] = half * (here + beta(start + 1, stop + 1))
        lower = half * (beta(start - 1, stop - 1) + here)
        second[start:stop], third[start:stop], share = shape.faces(here, half)
        total = absorb(start, stop) + lower + first[start:stop] + share
        diag[start:stop] = total
        inverse[start:stop] = jnp.where(here > 0.0, 1.0 / total, 0.0)


def pairs(value):
    return jnp.stack([value[at] + value[at + 1] for at in range(0, value.shape[0], 2)])


def coarse_rows(ref, value):
    count = value.shape[0]
    zero = jnp.zeros((count, 8, LANES), jnp.float32)
    ref[0:count, 0:8, :] = zero
    ref[0:count, 8:56, :] = pair_sum(value, 1)
    ref[0:count, 56:64, :] = zero

    def take(offset):
        halves = [
            [ref[at, pl.ds(32 * half + offset, 8, stride=4), :] for half in range(2)]
            for at in range(count)
        ]
        return jnp.stack([jnp.concatenate(both) for both in halves])

    even = (lax.broadcasted_iota(jnp.int32, (count, ROWS1, LANES), 2) & 1) == 0
    return 0.125 * jnp.where(even, take(0) + take(1), take(2) + take(3))


KEPT0 = 10
KEPT_ROWS0 = 32


def pre0_kernel(
    own, outer, kept_out, rest_out, beta_out, diag_out, absorb_out,
    diag, inverse, first, second, third, one, two, tmp,
):
    zero = jnp.zeros((8, LANES), jnp.float32)

    def piece(kind):
        def planes(start, stop):
            found = []
            for plane in range(start, stop):
                part, member = plane // 8, plane % 8 // 2
                if part == 1:
                    found.append(own[member, kind, plane % 2])
                    continue
                side = part // 2
                at = 2 * (6 * member + 2 * kind + plane % 2)
                rows = [outer[side, at + tile] for tile in (48, 0, 1, 49)]
                reach = 3 if kind == 2 else 2
                near = member - (LAYER - reach) if side == 0 else member
                if 0 <= near < reach:
                    at = 96 + 2 * (2 * (2 * kind + near) + plane % 2)
                    ends = outer[side, at], outer[side, at + 1]
                else:
                    ends = zero, zero
                found.append(jnp.concatenate([ends[0], *rows, ends[1]]))
            return jnp.stack(found)

        return planes

    source, absorb, beta = piece(0), piece(1), piece(2)
    shape = Packed(1, ROWS0, False)
    parts = (diag, inverse, first, second, third)
    level0_parts(shape, beta, absorb, parts, 1, 23)
    table = chebyshev_table(SWEEPS)
    begin(table, inverse, source, (one, two), 1, 23, CHUNK0)
    ranges = [(1 + order, 23 - order) for order in range(1, SWEEPS)]
    current, previous = sweep(
        shape, list(enumerate(table))[1:], source, parts, (one, two), ranges, CHUNK0
    )
    previous[4:20] = source(4, 20)
    base = 2 * (position() % LAYER) + 4
    for plane in range(KEPT0):
        for number, kept in enumerate((current, previous) + parts):
            kept_out[number, plane] = kept[base + plane, 8:40, :]
    coarse = Packed(2, ROWS1, False)
    half = face(1)
    betas = coarse_rows(tmp.at[0:8], pairs(beta(4, 20)))
    wide = coarse_rows(tmp.at[8:14], pairs(absorb(6, 18)))
    rest = [residual(shape, source, parts, current, p, p + 2) for p in range(6, 18, 2)]
    rest_out[...] = coarse_rows(tmp.at[14:20], jnp.stack([x[0] + x[1] for x in rest]))
    here = betas[1:7]
    _, _, share = coarse.faces(here, half)
    beta_out[...] = betas
    diag_out[...] = wide + half * (here + betas[0:6]) + half * (here + betas[2:8]) + share
    absorb_out[...] = wide[1:5]


DEPTH1 = 16
ROWS1 = 16


def gather_level1(region, rest, beta, diag, below, above):
    region[0, 1:6] = below[0:5]
    region[0, 6:10] = rest[1:5]
    region[0, 10:15] = above[0:5]
    region[1, 0:6] = below[5:11]
    region[1, 6:10] = beta[2:6]
    region[1, 10:16] = above[5:11]
    region[2, 1:6] = below[11:16]
    region[2, 6:10] = diag[1:5]
    region[2, 10:15] = above[11:16]


CHUNK1 = 4


def level1_parts(shape, region, inverse, first, second, third):
    half = face(1)
    beta = region.at[1]
    first[0:1] = half * (beta[0:1] + beta[1:2])
    for start in range(1, DEPTH1 - 1, CHUNK1):
        stop = min(start + CHUNK1, DEPTH1 - 1)
        here = beta[start:stop]
        second[start:stop], third[start:stop], _ = shape.faces(here, half)
        inverse[start:stop] = jnp.where(here > 0.0, 1.0 / region[2, start:stop], 0.0)
        first[start:stop] = half * (here + beta[start + 1 : stop + 1])


def coarser_rows(ref, value, start):
    ref[...] = pair_sum(pair_sum(value, 1), 2)
    inner = lanes_of(1) & 3
    rows = []
    for at in range(value.shape[0]):
        row = ref[at, start : start + 1, :]
        for offset in range(1, 4):
            row = jnp.where(inner == offset, ref[at, start + offset : start + offset + 1, :], row)
        rows.append(0.125 * row)
    return rows


def pre1_kernel(
    rest1, beta1, diag1, below, above, absorb, pay_out, region, inverse, first, second, third,
    one, two, tmp, tile,
):
    gather_level1(region, rest1, beta1, diag1, below, above)
    shape = Packed(2, ROWS1, False)
    level1_parts(shape, region, inverse, first, second, third)
    source = lambda start, stop: region[0, start:stop]
    parts = (region.at[2], inverse, first, second, third)
    table = chebyshev_table(SWEEPS)
    begin(table, inverse, source, (one, two), 2, 14, CHUNK1)
    ranges = [(2 + order, 14 - order) for order in range(1, SWEEPS)]
    current, _ = sweep(
        shape, list(enumerate(table))[1:], source, parts, (one, two), ranges, CHUNK1
    )
    rest = residual(shape, source, parts, current, 6, 10)
    totals = [pairs(rest), pairs(region[1, 6:10]), pairs(absorb[...])]
    rows = coarser_rows(tmp, jnp.concatenate(totals), 6)
    for at in range(6):
        tile[at : at + 1, :] = rows[at]
    tile[6:8, :] = jnp.zeros((2, LANES), jnp.float32)
    member = position() % LAYER
    tile[8:10, :] = tile[pl.ds(2 * member, 2), :]
    tile[10:14, :] = current[6 + member, 6:10, :]
    for at in range(6):
        row = jnp.broadcast_to(tile[8 + at : 9 + at, :], (16, LANES))
        pay_out[:, at * LANES : (at + 1) * LANES] = row


DEPTH2 = 32
SLOT = 48
KIND_AT = (0, 2, 1)
ROWS2 = 8


CHUNK2 = 4


def level2_parts(shape, beta, absorb, parts):
    diag, inverse, first, second, third = parts
    half = face(2)
    first[0:1] = jnp.zeros((1, ROWS2, LANES), jnp.float32)
    for start in range(1, DEPTH2 + 1, CHUNK2):
        stop = start + CHUNK2
        here = beta[start:stop]
        upper = half * (here + beta[start + 1 : stop + 1])
        lower = half * (here + beta[start - 1 : stop - 1])
        second[start:stop], third[start:stop], share = shape.faces(here, half)
        total = absorb[start:stop] + lower + upper + share
        first[start:stop] = upper
        diag[start:stop] = total
        inverse[start:stop] = 1.0 / total


def bottom_rows(ref, planes):
    value = planes(1, DEPTH2 + 1)
    value = jnp.concatenate([value[at] + value[at + 1] for at in range(0, DEPTH2, 2)])
    ref[...] = pair_sum(pair_sum(value, 1), 4)
    inner = lanes_of(32) & 7
    total = None
    for offset in range(4):
        value = jnp.concatenate(
            [ref[pl.ds(32 * block + offset, 8, stride=4), :] for block in range(4)]
        )
        moved = along(value, 1 if offset % 2 == 0 else -1)
        same = 2 * offset + offset % 2
        value = jnp.where(inner == same, value, moved)
        total = value if total is None else jnp.where(inner >> 1 == offset, value, total)
    return 0.125 * total


def bottom_solve(source, absorb, beta):
    shape = Packed(8, 2, True)
    half = face(3)
    row = rows_of(32)
    last, initial = row >= 30, row < 2
    up = jnp.where(last, 0.0, across(beta, 2))
    down = jnp.where(initial, 0.0, across(beta, -2))
    second, third, share = shape.faces(beta, half)
    upper = half * (beta + up)
    diag = absorb + half * (beta + down) + upper + share
    first = jnp.where(last, 0.0, upper)
    inverse = 1.0 / diag
    table = chebyshev_table(BOTTOM)
    current = table[0][1] * (inverse * source)
    previous = jnp.zeros_like(current)
    for carry, push in table[1:]:
        rest = source - diag * current + first * across(current, 2) + across(first * current, -2)
        rest = rest + shape.coupled(current, second, third)
        fresh = current + carry * (current - previous) + push * (inverse * rest)
        current, previous = fresh, current
    return current


def bottom_prolong(ref, value):
    inner = lanes_of(32) & 7
    part = inner & 3
    back1, back2 = along(value, -1), along(value, -2)
    fore1, fore2 = along(value, 1), along(value, 2)
    low = jnp.where(part == 0, value, jnp.where(part == 3, back2, back1))
    high = jnp.where(part == 3, value, jnp.where(part == 0, fore2, fore1))
    left = inner < 4
    for offset in range(4):
        base = low if offset % 2 == 0 else high
        if offset < 2:
            moved = jnp.where(left, base, along(base, -4))
        else:
            moved = jnp.where(left, along(base, 4), base)
        for block in range(4):
            ref[pl.ds(32 * block + offset, 8, stride=4), :] = moved[8 * block : 8 * block + 8]


def solve23(gathered, rows2, parts2, one2, two2, tall):
    shape = Packed(4, ROWS2, True)
    zero = jnp.zeros((ROWS2, LANES), jnp.float32)
    for number in range(3):
        for plane in range(DEPTH2):
            at = SLOT * 8 * KIND_AT[number] + plane
            rows2[number, plane + 1] = gathered[pl.ds(at, 8, stride=SLOT), :]
    for ref in (rows2.at[1], one2, two2):
        ref[0] = zero
        ref[DEPTH2 + 1] = zero

    source2 = lambda start, stop: rows2[0, start:stop]
    level2_parts(shape, rows2.at[1], rows2.at[2], parts2)
    table = chebyshev_table(SWEEPS)
    begin(table, parts2[1], source2, (one2, two2), 1, DEPTH2 + 1, CHUNK2)
    everywhere = [(1, DEPTH2 + 1)] * SWEEPS
    current, previous = sweep(
        shape, list(enumerate(table))[1:], source2, parts2, (one2, two2), everywhere, CHUNK2
    )
    source3 = bottom_rows(
        tall.at[0], lambda start, stop: residual(shape, source2, parts2, current, start, stop)
    )
    absorb3 = bottom_rows(tall.at[1], lambda start, stop: rows2[2, start:stop])
    beta3 = bottom_rows(tall.at[2], lambda start, stop: rows2[1, start:stop])
    bottom_prolong(tall.at[0], bottom_solve(source3, absorb3, beta3))
    for plane in range(DEPTH2):
        pair = plane // 2
        current[plane + 1] = current[plane + 1] + tall[0, 8 * pair : 8 * pair + 8, :]
    current, previous = sweep(
        shape, list(enumerate(table)), source2, parts2, (current, previous), everywhere, CHUNK2
    )
    return current


def post1(packed, whole, region, parts, one, two, wide, tmp):
    inverse, first, second, third = parts
    shape = Packed(2, ROWS1, False)
    layer = position() // LAYER
    row = column_position() + 6
    zero = jnp.zeros((8, LANES), jnp.float32)
    for plane in range(DEPTH2 + 6):
        wide[plane, 0:8, :] = zero
        wide[plane, 16:24, :] = zero
        inside = 3 <= plane < DEPTH2 + 3
        wide[plane, 8:16, :] = whole[plane - 2] if inside else zero
    value = jnp.stack([wide[2 * layer + pair, pl.ds(row, 8), :] for pair in range(8)])
    inner = lax.broadcasted_iota(jnp.int32, value.shape, 2) & 3
    moved = {steps: along(value, steps) for steps in range(-3, 4) if steps}
    moved[0] = value
    for offset in range(4):
        picked = moved[offset]
        for lane in range(1, 4):
            picked = jnp.where(inner == lane, moved[offset - lane], picked)
        for pair in range(8):
            tmp[pair, pl.ds(offset, 8, stride=4), :] = picked[pair]
    place = column_position()
    columns = (
        (jnp.maximum(place - 1, 0), jnp.where(place > 0, 1.0, 0.0)),
        (place, 1.0),
        (jnp.minimum(place + 1, 7), jnp.where(place < 7, 1.0, 0.0)),
    )
    blank = jnp.zeros((2, LANES), jnp.float32)
    for plane in range(DEPTH1):
        member = (plane - 6) % LAYER
        at = 16 * (member % 2) + 8 * (member // 2)
        row = 32 + 4 * (plane // LAYER)
        one[plane, 0:2, :] = blank
        for number, (who, there) in enumerate(columns):
            start = 2 + 4 * number
            one[plane, start : start + 4, :] = there * packed[at + who, row : row + 4, :]
        one[plane, 14:16, :] = blank
    for plane in range(DEPTH1):
        one[plane] = one[plane] + tmp[plane // 2, 2:18, :]
    table = chebyshev_table(SWEEPS)
    ranges = [(order, DEPTH1 - order) for order in range(1, SWEEPS + 1)]
    current, _ = sweep(
        shape, list(enumerate(table)), lambda start, stop: region[0, start:stop],
        (region.at[2], inverse, first, second, third), (one, two), ranges, CHUNK1,
    )
    return current


def post0(kept, coarse, out, one, two, tmp):
    field, source = kept.at[0], kept.at[1]
    parts = tuple(kept.at[number] for number in range(2, 7))
    member = position() % LAYER
    shape = Packed(1, ROWS0, False)
    value = jnp.stack([coarse[4 + member + pair, 4:12, :] for pair in range(5)])
    even = (lax.broadcasted_iota(jnp.int32, value.shape, 2) & 1) == 0
    upper_rows = jnp.where(even, value, along(value, -1))
    lower_rows = jnp.where(even, along(value, 1), value)
    for pair in range(5):
        for offset in range(4):
            rows = upper_rows if offset < 2 else lower_rows
            tmp[pair, pl.ds(offset, 8, stride=4), :] = rows[pair]
    for plane in range(KEPT0):
        one[plane] = field[plane] + tmp[plane // 2]
    table = chebyshev_table(SWEEPS)
    ranges = [(1 + order, KEPT0 - 1 - order) for order in range(SWEEPS)]
    current, _ = sweep(
        shape, list(enumerate(table)), lambda start, stop: source[start:stop], parts,
        (one, two), ranges, CHUNK0,
    )
    out[...] = current[4:6, 8:24, :]


def finish_kernel(
    gathered, packed, region1, inverse1, first1, second1, third1, kept0, out,
    rows2, diag2, inverse2, first2, second2, third2, one2, two2, tall,
    one1, two1, wide1, tmp1, one0, two0, tmp0,
):
    parts2 = (diag2, inverse2, first2, second2, third2)
    whole = solve23(gathered, rows2, parts2, one2, two2, tall)
    parts1 = (inverse1, first1, second1, third1)
    coarse = post1(packed, whole, region1, parts1, one1, two1, wide1, tmp1)
    post0(kept0, coarse, out, one0, two0, tmp0)


def f32(*shape):
    return jax.ShapeDtypeStruct(shape, jnp.float32)


def buffer(*shape):
    return pltpu.VMEM(shape, jnp.float32)


def call(kernel, out, scratch, name, *operands):
    return pl.pallas_call(
        kernel,
        out_shape=out,
        scratch_shapes=scratch,
        name=name,
        compiler_params=pltpu.CompilerParams(vmem_limit_bytes=VMEM),
    )(*operands)


def pre0(*pieces):
    plane = buffer(24, ROWS0, LANES)
    scratch = [plane] * 7 + [buffer(20, 64, LANES)]
    coarse = lambda count: f32(count, ROWS1, LANES)
    out = (f32(7, KEPT0, KEPT_ROWS0, LANES), coarse(6), coarse(8), coarse(6), coarse(4))
    return call(pre0_kernel, out, scratch, "pre0", *pieces)


def pre1(*pieces):
    plane, work = f32(DEPTH1, ROWS1, LANES), buffer(DEPTH1, ROWS1, LANES)
    scratch = [work, work, buffer(6, ROWS1, LANES), buffer(16, LANES)]
    out = (f32(16, 6 * LANES), f32(3, DEPTH1, ROWS1, LANES)) + (plane,) * 4
    return call(pre1_kernel, out, scratch, "pre1", *pieces)


def finish(*pieces):
    plane2 = buffer(DEPTH2 + 2, ROWS2, LANES)
    plane1 = buffer(DEPTH1, ROWS1, LANES)
    plane0 = buffer(KEPT0, KEPT_ROWS0, LANES)
    scratch = [buffer(3, DEPTH2 + 2, ROWS2, LANES)] + [plane2] * 7 + [buffer(3, 128, LANES)]
    scratch += [plane1] * 2 + [buffer(DEPTH2 + 6, 24, LANES), buffer(8, 32, LANES)]
    scratch += [plane0] * 2 + [buffer(5, KEPT_ROWS0, LANES)]
    return call(finish_kernel, f32(2, 16, LANES), scratch, "finish", *pieces)


def layers_apart(value, steps):
    count = lax.axis_size("gx")
    ways = [(i, i + (LAYER * steps if i % 2 == 0 else -LAYER * steps)) for i in range(count)]
    return lax.ppermute(value, "gx", [(i, j) for i, j in ways if 0 <= j < count])


def shifted(value, steps):
    count = lax.axis_size("gx")
    pairs = [(i, i + steps) for i in range(count) if 0 <= i + steps < count]
    return lax.ppermute(value, "gx", pairs)


def columns_apart(value):
    count, wide = lax.axis_size("gx"), lax.axis_size("gy")
    ways = [
        (i * wide + j, i * wide + j + (1 if i % 2 == 0 else -1))
        for i in range(count)
        for j in range(wide)
        if 0 <= j + (1 if i % 2 == 0 else -1) < wide
    ]
    return lax.ppermute(value, ("gx", "gy"), ways)


def body(source, absorb, beta):
    members = lax.axis_size("gx")
    wide = lax.axis_size("gy")
    layers = members // LAYER
    near = [[LAYER * z + c for c in range(LAYER)] for z in range(layers)]
    chips = [[2 * chip, 2 * chip + 1] for chip in range(members // 2)]
    column = [[LAYER * z + c for z in range(layers)] for c in range(LAYER)]
    cores = [
        [(LAYER * z + 2 * chip + core) * wide + y for chip in range(2) for y in range(wide)]
        for z in range(layers)
        for core in range(2)
    ]
    first_core = lax.axis_index("gx") % 2 == 0

    def both(value):
        return lax.all_gather(value, "gx", axis_index_groups=chips)

    local = jnp.stack([source, absorb, beta])
    own = lax.all_gather(local, "gx", axis_index_groups=near)
    def tiles_of(arrays):
        return jnp.concatenate([x.reshape(-1, 8, LANES) for x in arrays])

    sides = columns_apart(own)
    outer = layers_apart(own, 1)
    sides = both(sides)
    layer = jnp.concatenate([sides[0], own, sides[1]], axis=-2)
    rims = jnp.concatenate([sides[0, ..., 8:, :], sides[1, ..., :8, :]], axis=-2)
    ends = jnp.concatenate([sides[0, ..., :8, :], sides[1, ..., 8:, :]], axis=-2)
    near2 = jnp.where(first_core, ends[2:, :2], ends[:2, :2])
    near3 = jnp.where(first_core, ends[1:, 2], ends[:3, 2])
    rest = layers_apart(tiles_of([rims, near2[:, 0], near2[:, 1], near3]), 1)
    kept0, rest1, beta1, diag1, absorb1 = pre0(layer, both(tiles_of([outer, rest])))

    upwards = jnp.concatenate([rest1[0:5], beta1[0:6], diag1[0:5]])
    downwards = jnp.concatenate([rest1[1:6], beta1[2:8], diag1[1:6]])
    below, above = shifted(upwards, LAYER), shifted(downwards, -LAYER)
    pay, *kept1 = pre1(rest1, beta1, diag1, below, above, absorb1)

    place = lax.axis_index("gx")
    start = (place >> 2) + (((place & 3) ^ 3) >> 1)
    pay, start = lax.optimization_barrier((pay, start))
    rows = lax.all_to_all(pay, "gx", 0, 0, axis_index_groups=column)
    rows, start = lax.optimization_barrier((rows, start))
    fields = jnp.pad(rows[:, 2 * LANES :], ((2, 2), (0, 0)))
    fields = lax.dynamic_slice_in_dim(fields, start, 4)
    rows = jnp.concatenate([x.reshape(-1, LANES) for x in (rows[:, : 2 * LANES], fields)])
    rows = jnp.broadcast_to(rows, (2 * wide,) + rows.shape)
    rows = lax.all_to_all(rows, ("gx", "gy"), 0, 0, axis_index_groups=cores)
    packed = both(rows).reshape(-1, SLOT, LANES)
    return finish(packed.reshape(-1, LANES), packed, *kept1, kept0)


def solution(mesh):
    placed = (P("gx", "gy", None), P("gx", "gy", None), P("gx", "gy", None))
    return jax.shard_map(
        body, mesh=mesh, in_specs=placed, out_specs=P("gx", "gy", None), check_vma=False
    )
```

```python
import jax
import jax.numpy as jnp
from jax import lax
from jax.experimental import pallas as pl
from jax.experimental.pallas import tpu as pltpu
from jax.sharding import PartitionSpec as P

SWEEPS = 4
BOTTOM = 8
LANES = 128
VMEM = 24 * 1024 * 1024

LAYER = 4
PACK = (1, 2, 4, 8)


def face(level):
    return 0.5 * 0.25**level


def chebyshev_table(count):
    centre = 1.125
    half_width = 0.875
    ratio = centre / half_width
    factor = 1.0 / ratio
    table = [(0.0, 1.0 / centre)]
    for order in range(1, count):
        fresh_factor = 1.0 / (2.0 * ratio - factor)
        table.append((fresh_factor * factor, 2.0 * fresh_factor / half_width))
        factor = fresh_factor
    return table


def position():
    return lax.axis_index("gx")


def column_position():
    return lax.axis_index("gy")


def lanes_of(rows):
    return lax.broadcasted_iota(jnp.int32, (rows, LANES), 1)


def rows_of(rows):
    return lax.broadcasted_iota(jnp.int32, (rows, LANES), 0)


def along(value, steps):
    return pltpu.roll(value, (-steps) % LANES, value.ndim - 1)


def across(value, steps):
    rows = value.shape[-2]
    return pltpu.roll(value, (-steps) % rows, value.ndim - 2)


class Packed:
    def __init__(self, pack, period, whole):
        self.pack = pack
        self.period = period
        self.whole = whole
        self.kept = {}

    def masks(self, value):
        if value.shape not in self.kept:
            pack, dims = self.pack, value.ndim
            lane = lax.broadcasted_iota(jnp.int32, value.shape, dims - 1)
            row = lax.broadcasted_iota(jnp.int32, value.shape, dims - 2) & (self.period - 1)
            inner = lane & (pack - 1)
            self.kept[value.shape] = dict(
                up=inner < pack - 1,
                down=inner > 0,
                third_last=lane >= LANES - pack,
                third_first=lane < pack,
                second_last=(row == self.period - 1) & (inner == pack - 1),
                second_first=(row == 0) & (inner == 0),
            )
        return self.kept[value.shape]

    def second_up(self, value):
        if self.pack == 1:
            return across(value, 1)
        mask = self.masks(value)["up"]
        return jnp.where(mask, along(value, 1), across(along(value, 1 - self.pack), 1))

    def second_down(self, value):
        if self.pack == 1:
            return across(value, -1)
        mask = self.masks(value)["down"]
        return jnp.where(mask, along(value, -1), across(along(value, self.pack - 1), -1))

    def faces(self, beta, half):
        mask = self.masks(beta)
        up = self.second_up(beta)
        if self.whole:
            up = jnp.where(mask["second_last"], 0.0, up)
        second = half * (beta + up)
        down = self.second_down(beta)
        if self.whole:
            down = jnp.where(mask["second_first"], 0.0, down)
        share = half * (beta + down) + second
        if self.whole:
            second = jnp.where(mask["second_last"], 0.0, second)
        third_up = jnp.where(mask["third_last"], 0.0, along(beta, self.pack))
        third = half * (beta + third_up)
        third_down = jnp.where(mask["third_first"], 0.0, along(beta, -self.pack))
        share = share + half * (beta + third_down) + third
        return second, jnp.where(mask["third_last"], 0.0, third), share

    def coupled(self, value, second, third):
        total = second * self.second_up(value) + self.second_down(second * value)
        total = total + third * along(value, self.pack)
        return total + along(third * value, -self.pack)


def pair_sum(value, width):
    low = (lax.broadcasted_iota(jnp.int32, value.shape, value.ndim - 1) & width) == 0
    return value + jnp.where(low, along(value, width), along(value, -width))


def residual(shape, source, parts, field, start, stop):
    diag, _, first, second, third = parts
    here = field[start:stop]
    total = source(start, stop) - diag[start:stop] * here
    total = total + first[start:stop] * field[start + 1 : stop + 1]
    total = total + first[start - 1 : stop - 1] * field[start - 1 : stop - 1]
    return total + shape.coupled(here, second[start:stop], third[start:stop])


def sweep(shape, orders, source, parts, buffers, ranges, chunk):
    inverse = parts[1]
    current, previous = buffers
    for (order, (carry, push)), (low, high) in zip(orders, ranges):
        for start in range(low, high, chunk):
            stop = min(start + chunk, high)
            rest = residual(shape, source, parts, current, start, stop)
            here = current[start:stop]
            fresh = here + push * (inverse[start:stop] * rest)
            if order > 0:
                fresh = fresh + carry * (here - previous[start:stop])
            previous[start:stop] = fresh
        current, previous = previous, current
    return current, previous


def begin(table, inverse, source, buffers, low, high, chunk):
    for start in range(low, high, chunk):
        stop = min(start + chunk, high)
        fresh = table[0][1] * (inverse[start:stop] * source(start, stop))
        buffers[0][start:stop] = fresh
        buffers[1][start:stop] = jnp.zeros_like(fresh)


ROWS0 = 48


CHUNK0 = 2


def level0_parts(shape, beta, absorb, parts, low, high):
    diag, inverse, first, second, third = parts
    half = face(0)
    first[low - 1 : low] = half * (beta(low - 1, low) + beta(low, low + 1))
    for start in range(low, high, CHUNK0):
        stop = min(start + CHUNK0, high)
        here = beta(start, stop)
        first[start:stop] = half * (here + beta(start + 1, stop + 1))
        lower = half * (beta(start - 1, stop - 1) + here)
        second[start:stop], third[start:stop], share = shape.faces(here, half)
        total = absorb(start, stop) + lower + first[start:stop] + share
        diag[start:stop] = total
        inverse[start:stop] = jnp.where(here > 0.0, 1.0 / total, 0.0)


def pairs(value):
    return jnp.stack([value[at] + value[at + 1] for at in range(0, value.shape[0], 2)])


def coarse_rows(ref, value):
    count = value.shape[0]
    zero = jnp.zeros((count, 8, LANES), jnp.float32)
    ref[0:count, 0:8, :] = zero
    ref[0:count, 8:56, :] = pair_sum(value, 1)
    ref[0:count, 56:64, :] = zero

    def take(offset):
        halves = [
            [ref[at, pl.ds(32 * half + offset, 8, stride=4), :] for half in range(2)]
            for at in range(count)
        ]
        return jnp.stack([jnp.concatenate(both) for both in halves])

    even = (lax.broadcasted_iota(jnp.int32, (count, ROWS1, LANES), 2) & 1) == 0
    return 0.125 * jnp.where(even, take(0) + take(1), take(2) + take(3))


RIM_REACH = (3, 3, 4)
END_REACH = (2, 2, 3)
RIMS = (0, 12, 24)
ENDS = (40, 48, 56)
KEPT0 = 10
KEPT_ROWS0 = 32


def pre0_kernel(
    own, outer, rims, kept_out, rest_out, beta_out, diag_out, absorb_out,
    diag, inverse, first, second, third, one, two, tmp,
):
    zero = jnp.zeros((8, LANES), jnp.float32)

    def piece(kind):
        def planes(start, stop):
            found = []
            for plane in range(start, stop):
                part, member = plane // 8, plane % 8 // 2
                if part == 1:
                    found.append(own[member, kind, plane % 2])
                    continue
                side = part // 2
                at = 2 * (6 * member + 2 * kind + plane % 2)
                own_rows = [outer[side, at], outer[side, at + 1]]
                outward = LAYER - 1 - member if side == 0 else member
                found_tiles = []
                for first_tile, reach in ((RIMS[kind], RIM_REACH[kind]), (ENDS[kind], END_REACH[kind])):
                    if outward < reach:
                        index = reach - 1 - outward if side == 0 else outward
                        at = first_tile + 2 * (2 * index + plane % 2)
                        found_tiles.append((rims[side, at], rims[side, at + 1]))
                    else:
                        found_tiles.append((zero, zero))
                rim, ends = found_tiles
                rows = [rim[0], *own_rows, rim[1]]
                found.append(jnp.concatenate([ends[0], *rows, ends[1]]))
            return jnp.stack(found)

        return planes

    source, absorb, beta = piece(0), piece(1), piece(2)
    shape = Packed(1, ROWS0, False)
    parts = (diag, inverse, first, second, third)
    level0_parts(shape, beta, absorb, parts, 1, 23)
    table = chebyshev_table(SWEEPS)
    begin(table, inverse, source, (one, two), 1, 23, CHUNK0)
    ranges = [(1 + order, 23 - order) for order in range(1, SWEEPS)]
    current, previous = sweep(
        shape, list(enumerate(table))[1:], source, parts, (one, two), ranges, CHUNK0
    )
    previous[4:20] = source(4, 20)
    base = 2 * (position() % LAYER) + 4
    for plane in range(KEPT0):
        for number, kept in enumerate((current, previous) + parts):
            kept_out[number, plane] = kept[base + plane, 8:40, :]
    coarse = Packed(2, ROWS1, False)
    half = face(1)
    betas = coarse_rows(tmp.at[0:8], pairs(beta(4, 20)))
    wide = coarse_rows(tmp.at[8:14], pairs(absorb(6, 18)))
    rest = [residual(shape, source, parts, current, p, p + 2) for p in range(6, 18, 2)]
    rest_out[...] = coarse_rows(tmp.at[14:20], jnp.stack([x[0] + x[1] for x in rest]))
    here = betas[1:7]
    _, _, share = coarse.faces(here, half)
    beta_out[...] = betas
    diag_out[...] = wide + half * (here + betas[0:6]) + half * (here + betas[2:8]) + share
    absorb_out[...] = wide[1:5]


DEPTH1 = 16
ROWS1 = 16


def gather_level1(region, rest, beta, diag, outer):
    region[0, 1:6] = outer[0, 0:5]
    region[0, 6:10] = rest[1:5]
    region[0, 10:15] = outer[1, 0:5]
    region[1, 0:6] = outer[0, 5:11]
    region[1, 6:10] = beta[2:6]
    region[1, 10:16] = outer[1, 5:11]
    region[2, 1:6] = outer[0, 11:16]
    region[2, 6:10] = diag[1:5]
    region[2, 10:15] = outer[1, 11:16]


CHUNK1 = 4


def level1_parts(shape, region, inverse, first, second, third):
    half = face(1)
    beta = region.at[1]
    first[0:1] = half * (beta[0:1] + beta[1:2])
    for start in range(1, DEPTH1 - 1, CHUNK1):
        stop = min(start + CHUNK1, DEPTH1 - 1)
        here = beta[start:stop]
        second[start:stop], third[start:stop], _ = shape.faces(here, half)
        inverse[start:stop] = jnp.where(here > 0.0, 1.0 / region[2, start:stop], 0.0)
        first[start:stop] = half * (here + beta[start + 1 : stop + 1])


def coarser_rows(ref, value, start):
    ref[...] = pair_sum(pair_sum(value, 1), 2)
    inner = lanes_of(1) & 3
    rows = []
    for at in range(value.shape[0]):
        row = ref[at, start : start + 1, :]
        for offset in range(1, 4):
            row = jnp.where(inner == offset, ref[at, start + offset : start + offset + 1, :], row)
        rows.append(0.125 * row)
    return rows


def pre1_kernel(
    rest1, beta1, diag1, outer, absorb, pay_out, region, inverse, first, second, third,
    one, two, tmp, tile,
):
    gather_level1(region, rest1, beta1, diag1, outer)
    shape = Packed(2, ROWS1, False)
    level1_parts(shape, region, inverse, first, second, third)
    source = lambda start, stop: region[0, start:stop]
    parts = (region.at[2], inverse, first, second, third)
    table = chebyshev_table(SWEEPS)
    begin(table, inverse, source, (one, two), 2, 14, CHUNK1)
    ranges = [(2 + order, 14 - order) for order in range(1, SWEEPS)]
    current, _ = sweep(
        shape, list(enumerate(table))[1:], source, parts, (one, two), ranges, CHUNK1
    )
    rest = residual(shape, source, parts, current, 6, 10)
    totals = [pairs(rest), pairs(region[1, 6:10]), pairs(absorb[...])]
    rows = coarser_rows(tmp, jnp.concatenate(totals), 6)
    for at in range(6):
        tile[at : at + 1, :] = rows[at]
    tile[6:8, :] = jnp.zeros((2, LANES), jnp.float32)
    member = position() % LAYER
    tile[8:10, :] = tile[pl.ds(2 * member, 2), :]
    tile[10:14, :] = current[6 + member, 6:10, :]
    for at in range(6):
        row = jnp.broadcast_to(tile[8 + at : 9 + at, :], (16, LANES))
        pay_out[:, at * LANES : (at + 1) * LANES] = row


DEPTH2 = 32
SLOT = 48
KIND_AT = (0, 2, 1)
ROWS2 = 8


CHUNK2 = 4


def level2_parts(shape, beta, absorb, parts):
    diag, inverse, first, second, third = parts
    half = face(2)
    first[0:1] = jnp.zeros((1, ROWS2, LANES), jnp.float32)
    for start in range(1, DEPTH2 + 1, CHUNK2):
        stop = start + CHUNK2
        here = beta[start:stop]
        upper = half * (here + beta[start + 1 : stop + 1])
        lower = half * (here + beta[start - 1 : stop - 1])
        second[start:stop], third[start:stop], share = shape.faces(here, half)
        total = absorb[start:stop] + lower + upper + share
        first[start:stop] = upper
        diag[start:stop] = total
        inverse[start:stop] = 1.0 / total


def bottom_rows(ref, planes):
    value = planes(1, DEPTH2 + 1)
    value = jnp.concatenate([value[at] + value[at + 1] for at in range(0, DEPTH2, 2)])
    ref[...] = pair_sum(pair_sum(value, 1), 4)
    inner = lanes_of(32) & 7
    total = None
    for offset in range(4):
        value = jnp.concatenate(
            [ref[pl.ds(32 * block + offset, 8, stride=4), :] for block in range(4)]
        )
        moved = along(value, 1 if offset % 2 == 0 else -1)
        same = 2 * offset + offset % 2
        value = jnp.where(inner == same, value, moved)
        total = value if total is None else jnp.where(inner >> 1 == offset, value, total)
    return 0.125 * total


def bottom_solve(source, absorb, beta):
    shape = Packed(8, 2, True)
    half = face(3)
    row = rows_of(32)
    last, initial = row >= 30, row < 2
    up = jnp.where(last, 0.0, across(beta, 2))
    down = jnp.where(initial, 0.0, across(beta, -2))
    second, third, share = shape.faces(beta, half)
    upper = half * (beta + up)
    diag = absorb + half * (beta + down) + upper + share
    first = jnp.where(last, 0.0, upper)
    inverse = 1.0 / diag
    table = chebyshev_table(BOTTOM)
    current = table[0][1] * (inverse * source)
    previous = jnp.zeros_like(current)
    for carry, push in table[1:]:
        rest = source - diag * current + first * across(current, 2) + across(first * current, -2)
        rest = rest + shape.coupled(current, second, third)
        fresh = current + carry * (current - previous) + push * (inverse * rest)
        current, previous = fresh, current
    return current


def bottom_prolong(ref, value):
    inner = lanes_of(32) & 7
    part = inner & 3
    back1, back2 = along(value, -1), along(value, -2)
    fore1, fore2 = along(value, 1), along(value, 2)
    low = jnp.where(part == 0, value, jnp.where(part == 3, back2, back1))
    high = jnp.where(part == 3, value, jnp.where(part == 0, fore2, fore1))
    left = inner < 4
    for offset in range(4):
        base = low if offset % 2 == 0 else high
        if offset < 2:
            moved = jnp.where(left, base, along(base, -4))
        else:
            moved = jnp.where(left, along(base, 4), base)
        for block in range(4):
            ref[pl.ds(32 * block + offset, 8, stride=4), :] = moved[8 * block : 8 * block + 8]


def solve23(gathered, rows2, parts2, one2, two2, tall):
    shape = Packed(4, ROWS2, True)
    zero = jnp.zeros((ROWS2, LANES), jnp.float32)
    for number in range(3):
        for plane in range(DEPTH2):
            at = SLOT * 8 * KIND_AT[number] + plane
            rows2[number, plane + 1] = gathered[pl.ds(at, 8, stride=SLOT), :]
    for ref in (rows2.at[1], one2, two2):
        ref[0] = zero
        ref[DEPTH2 + 1] = zero

    source2 = lambda start, stop: rows2[0, start:stop]
    level2_parts(shape, rows2.at[1], rows2.at[2], parts2)
    table = chebyshev_table(SWEEPS)
    begin(table, parts2[1], source2, (one2, two2), 1, DEPTH2 + 1, CHUNK2)
    everywhere = [(1, DEPTH2 + 1)] * SWEEPS
    current, previous = sweep(
        shape, list(enumerate(table))[1:], source2, parts2, (one2, two2), everywhere, CHUNK2
    )
    source3 = bottom_rows(
        tall.at[0], lambda start, stop: residual(shape, source2, parts2, current, start, stop)
    )
    absorb3 = bottom_rows(tall.at[1], lambda start, stop: rows2[2, start:stop])
    beta3 = bottom_rows(tall.at[2], lambda start, stop: rows2[1, start:stop])
    bottom_prolong(tall.at[0], bottom_solve(source3, absorb3, beta3))
    for plane in range(DEPTH2):
        pair = plane // 2
        current[plane + 1] = current[plane + 1] + tall[0, 8 * pair : 8 * pair + 8, :]
    current, previous = sweep(
        shape, list(enumerate(table)), source2, parts2, (current, previous), everywhere, CHUNK2
    )
    return current


def post1(packed, whole, region, parts, one, two, wide, tmp):
    inverse, first, second, third = parts
    shape = Packed(2, ROWS1, False)
    layer = position() // LAYER
    row = column_position() + 6
    zero = jnp.zeros((8, LANES), jnp.float32)
    for plane in range(DEPTH2 + 6):
        wide[plane, 0:8, :] = zero
        wide[plane, 16:24, :] = zero
        inside = 3 <= plane < DEPTH2 + 3
        wide[plane, 8:16, :] = whole[plane - 2] if inside else zero
    value = jnp.stack([wide[2 * layer + pair, pl.ds(row, 8), :] for pair in range(8)])
    inner = lax.broadcasted_iota(jnp.int32, value.shape, 2) & 3
    moved = {steps: along(value, steps) for steps in range(-3, 4) if steps}
    moved[0] = value
    for offset in range(4):
        picked = moved[offset]
        for lane in range(1, 4):
            picked = jnp.where(inner == lane, moved[offset - lane], picked)
        for pair in range(8):
            tmp[pair, pl.ds(offset, 8, stride=4), :] = picked[pair]
    place = column_position()
    columns = (
        (jnp.maximum(place - 1, 0), jnp.where(place > 0, 1.0, 0.0)),
        (place, 1.0),
        (jnp.minimum(place + 1, 7), jnp.where(place < 7, 1.0, 0.0)),
    )
    blank = jnp.zeros((2, LANES), jnp.float32)
    for plane in range(DEPTH1):
        member = (plane - 6) % LAYER
        at = 16 * (member % 2) + 8 * (member // 2)
        row = 32 + 4 * (plane // LAYER)
        one[plane, 0:2, :] = blank
        for number, (who, there) in enumerate(columns):
            start = 2 + 4 * number
            one[plane, start : start + 4, :] = there * packed[at + who, row : row + 4, :]
        one[plane, 14:16, :] = blank
    for plane in range(DEPTH1):
        one[plane] = one[plane] + tmp[plane // 2, 2:18, :]
    table = chebyshev_table(SWEEPS)
    ranges = [(order, DEPTH1 - order) for order in range(1, SWEEPS + 1)]
    current, _ = sweep(
        shape, list(enumerate(table)), lambda start, stop: region[0, start:stop],
        (region.at[2], inverse, first, second, third), (one, two), ranges, CHUNK1,
    )
    return current


def post0(kept, coarse, out, one, two, tmp):
    field, source = kept.at[0], kept.at[1]
    parts = tuple(kept.at[number] for number in range(2, 7))
    member = position() % LAYER
    shape = Packed(1, ROWS0, False)
    value = jnp.stack([coarse[4 + member + pair, 4:12, :] for pair in range(5)])
    even = (lax.broadcasted_iota(jnp.int32, value.shape, 2) & 1) == 0
    upper_rows = jnp.where(even, value, along(value, -1))
    lower_rows = jnp.where(even, along(value, 1), value)
    for pair in range(5):
        for offset in range(4):
            rows = upper_rows if offset < 2 else lower_rows
            tmp[pair, pl.ds(offset, 8, stride=4), :] = rows[pair]
    for plane in range(KEPT0):
        one[plane] = field[plane] + tmp[plane // 2]
    table = chebyshev_table(SWEEPS)
    ranges = [(1 + order, KEPT0 - 1 - order) for order in range(SWEEPS)]
    current, _ = sweep(
        shape, list(enumerate(table)), lambda start, stop: source[start:stop], parts,
        (one, two), ranges, CHUNK0,
    )
    out[...] = current[4:6, 8:24, :]


def finish_kernel(
    gathered, packed, region1, inverse1, first1, second1, third1, kept0, out,
    rows2, diag2, inverse2, first2, second2, third2, one2, two2, tall,
    one1, two1, wide1, tmp1, one0, two0, tmp0,
):
    parts2 = (diag2, inverse2, first2, second2, third2)
    whole = solve23(gathered, rows2, parts2, one2, two2, tall)
    parts1 = (inverse1, first1, second1, third1)
    coarse = post1(packed, whole, region1, parts1, one1, two1, wide1, tmp1)
    post0(kept0, coarse, out, one0, two0, tmp0)


def f32(*shape):
    return jax.ShapeDtypeStruct(shape, jnp.float32)


def buffer(*shape):
    return pltpu.VMEM(shape, jnp.float32)


def call(kernel, out, scratch, name, *operands):
    return pl.pallas_call(
        kernel,
        out_shape=out,
        scratch_shapes=scratch,
        name=name,
        compiler_params=pltpu.CompilerParams(vmem_limit_bytes=VMEM),
    )(*operands)


def pre0(*pieces):
    plane = buffer(24, ROWS0, LANES)
    scratch = [plane] * 7 + [buffer(20, 64, LANES)]
    coarse = lambda count: f32(count, ROWS1, LANES)
    out = (f32(7, KEPT0, KEPT_ROWS0, LANES), coarse(6), coarse(8), coarse(6), coarse(4))
    return call(pre0_kernel, out, scratch, "pre0", *pieces)


def pre1(*pieces):
    plane, work = f32(DEPTH1, ROWS1, LANES), buffer(DEPTH1, ROWS1, LANES)
    scratch = [work, work, buffer(6, ROWS1, LANES), buffer(16, LANES)]
    out = (f32(16, 6 * LANES), f32(3, DEPTH1, ROWS1, LANES)) + (plane,) * 4
    return call(pre1_kernel, out, scratch, "pre1", *pieces)


def finish(*pieces):
    plane2 = buffer(DEPTH2 + 2, ROWS2, LANES)
    plane1 = buffer(DEPTH1, ROWS1, LANES)
    plane0 = buffer(KEPT0, KEPT_ROWS0, LANES)
    scratch = [buffer(3, DEPTH2 + 2, ROWS2, LANES)] + [plane2] * 7 + [buffer(3, 128, LANES)]
    scratch += [plane1] * 2 + [buffer(DEPTH2 + 6, 24, LANES), buffer(8, 32, LANES)]
    scratch += [plane0] * 2 + [buffer(5, KEPT_ROWS0, LANES)]
    return call(finish_kernel, f32(2, 16, LANES), scratch, "finish", *pieces)


def layers_apart(value, steps):
    count = lax.axis_size("gx")
    ways = [(i, i + (LAYER * steps if i % 2 == 0 else -LAYER * steps)) for i in range(count)]
    return lax.ppermute(value, "gx", [(i, j) for i, j in ways if 0 <= j < count])


def columns_apart(value):
    count, wide = lax.axis_size("gx"), lax.axis_size("gy")
    ways = [
        (i * wide + j, i * wide + j + (1 if i % 2 == 0 else -1))
        for i in range(count)
        for j in range(wide)
        if 0 <= j + (1 if i % 2 == 0 else -1) < wide
    ]
    return lax.ppermute(value, ("gx", "gy"), ways)


def body(source, absorb, beta):
    members = lax.axis_size("gx")
    wide = lax.axis_size("gy")
    layers = members // LAYER
    near = [[LAYER * z + c for c in range(LAYER)] for z in range(layers)]
    chips = [[2 * chip, 2 * chip + 1] for chip in range(members // 2)]
    column = [[LAYER * z + c for z in range(layers)] for c in range(LAYER)]
    cores = [
        [(LAYER * z + 2 * chip + core) * wide + y for chip in range(2) for y in range(wide)]
        for z in range(layers)
        for core in range(2)
    ]
    first_core = lax.axis_index("gx") % 2 == 0

    def both(value):
        return lax.all_gather(value, "gx", axis_index_groups=chips)

    local = jnp.stack([source, absorb, beta])
    own = lax.all_gather(local, "gx", axis_index_groups=near)
    def tiles_of(arrays):
        return jnp.concatenate([x.reshape(-1, 8, LANES) for x in arrays])

    sides = columns_apart(own)
    outer = layers_apart(own, 1)
    sides = both(sides)
    layer = jnp.concatenate([sides[0], own, sides[1]], axis=-2)
    rims = jnp.concatenate([sides[0, ..., 8:, :], sides[1, ..., :8, :]], axis=-2)
    ends = jnp.concatenate([sides[0, ..., :8, :], sides[1, ..., 8:, :]], axis=-2)
    sent = []
    for rows, reaches in ((rims, RIM_REACH), (ends, END_REACH)):
        for kind, reach in enumerate(reaches):
            sent.append(jnp.where(first_core, rows[LAYER - reach :, kind], rows[:reach, kind]))
    rest = layers_apart(tiles_of(sent), 1)
    outer = both(tiles_of([outer]))
    kept0, rest1, beta1, diag1, absorb1 = pre0(layer, outer, both(rest))

    upwards = jnp.concatenate([rest1[0:5], beta1[0:6], diag1[0:5]])
    downwards = jnp.concatenate([rest1[1:6], beta1[2:8], diag1[1:6]])
    outer = both(layers_apart(jnp.where(first_core, upwards, downwards), 1))
    pay, *kept1 = pre1(rest1, beta1, diag1, outer, absorb1)

    place = lax.axis_index("gx")
    start = (place >> 2) + (((place & 3) ^ 3) >> 1)
    pay, start = lax.optimization_barrier((pay, start))
    rows = lax.all_to_all(pay, "gx", 0, 0, axis_index_groups=column)
    rows, start = lax.optimization_barrier((rows, start))
    fields = jnp.pad(rows[:, 2 * LANES :], ((2, 2), (0, 0)))
    fields = lax.dynamic_slice_in_dim(fields, start, 4)
    rows = jnp.concatenate([x.reshape(-1, LANES) for x in (rows[:, : 2 * LANES], fields)])
    rows = jnp.broadcast_to(rows, (2 * wide,) + rows.shape)
    rows = lax.all_to_all(rows, ("gx", "gy"), 0, 0, axis_index_groups=cores)
    packed = both(rows).reshape(-1, SLOT, LANES)
    return finish(packed.reshape(-1, LANES), packed, *kept1, kept0)


def solution(mesh):
    placed = (P("gx", "gy", None), P("gx", "gy", None), P("gx", "gy", None))
    return jax.shard_map(
        body, mesh=mesh, in_specs=placed, out_specs=P("gx", "gy", None), check_vma=False
    )
```

```python
import jax
import jax.numpy as jnp
from jax import lax
from jax.experimental import pallas as pl
from jax.experimental.pallas import tpu as pltpu
from jax.sharding import PartitionSpec as P

SWEEPS = 4
BOTTOM = 8
LANES = 128
VMEM = 24 * 1024 * 1024

LAYER = 4
PACK = (1, 2, 4, 8)


def face(level):
    return 0.5 * 0.25**level


def chebyshev_table(count):
    centre = 1.125
    half_width = 0.875
    ratio = centre / half_width
    factor = 1.0 / ratio
    table = [(0.0, 1.0 / centre)]
    for order in range(1, count):
        fresh_factor = 1.0 / (2.0 * ratio - factor)
        table.append((fresh_factor * factor, 2.0 * fresh_factor / half_width))
        factor = fresh_factor
    return table


def position():
    return lax.axis_index("gx")


def column_position():
    return lax.axis_index("gy")


def lanes_of(rows):
    return lax.broadcasted_iota(jnp.int32, (rows, LANES), 1)


def rows_of(rows):
    return lax.broadcasted_iota(jnp.int32, (rows, LANES), 0)


def along(value, steps):
    return pltpu.roll(value, (-steps) % LANES, value.ndim - 1)


def across(value, steps):
    rows = value.shape[-2]
    return pltpu.roll(value, (-steps) % rows, value.ndim - 2)


class Packed:
    def __init__(self, pack, period, whole):
        self.pack = pack
        self.period = period
        self.whole = whole
        self.kept = {}

    def masks(self, value):
        if value.shape not in self.kept:
            pack, dims = self.pack, value.ndim
            lane = lax.broadcasted_iota(jnp.int32, value.shape, dims - 1)
            row = lax.broadcasted_iota(jnp.int32, value.shape, dims - 2) & (self.period - 1)
            inner = lane & (pack - 1)
            self.kept[value.shape] = dict(
                up=inner < pack - 1,
                down=inner > 0,
                third_last=lane >= LANES - pack,
                third_first=lane < pack,
                second_last=(row == self.period - 1) & (inner == pack - 1),
                second_first=(row == 0) & (inner == 0),
            )
        return self.kept[value.shape]

    def second_up(self, value):
        if self.pack == 1:
            return across(value, 1)
        mask = self.masks(value)["up"]
        return jnp.where(mask, along(value, 1), across(along(value, 1 - self.pack), 1))

    def second_down(self, value):
        if self.pack == 1:
            return across(value, -1)
        mask = self.masks(value)["down"]
        return jnp.where(mask, along(value, -1), across(along(value, self.pack - 1), -1))

    def faces(self, beta, half):
        mask = self.masks(beta)
        up = self.second_up(beta)
        if self.whole:
            up = jnp.where(mask["second_last"], 0.0, up)
        second = half * (beta + up)
        down = self.second_down(beta)
        if self.whole:
            down = jnp.where(mask["second_first"], 0.0, down)
        share = half * (beta + down) + second
        if self.whole:
            second = jnp.where(mask["second_last"], 0.0, second)
        third_up = jnp.where(mask["third_last"], 0.0, along(beta, self.pack))
        third = half * (beta + third_up)
        third_down = jnp.where(mask["third_first"], 0.0, along(beta, -self.pack))
        share = share + half * (beta + third_down) + third
        return second, jnp.where(mask["third_last"], 0.0, third), share

    def coupled(self, value, second, third):
        total = second * self.second_up(value) + self.second_down(second * value)
        total = total + third * along(value, self.pack)
        return total + along(third * value, -self.pack)


def pair_sum(value, width):
    low = (lax.broadcasted_iota(jnp.int32, value.shape, value.ndim - 1) & width) == 0
    return value + jnp.where(low, along(value, width), along(value, -width))


def residual(shape, source, parts, field, start, stop):
    diag, _, first, second, third = parts
    here = field[start:stop]
    total = source(start, stop) - diag[start:stop] * here
    total = total + first[start:stop] * field[start + 1 : stop + 1]
    total = total + first[start - 1 : stop - 1] * field[start - 1 : stop - 1]
    return total + shape.coupled(here, second[start:stop], third[start:stop])


def sweep(shape, orders, source, parts, buffers, ranges, chunk):
    inverse = parts[1]
    current, previous = buffers
    for (order, (carry, push)), (low, high) in zip(orders, ranges):
        for start in range(low, high, chunk):
            stop = min(start + chunk, high)
            rest = residual(shape, source, parts, current, start, stop)
            here = current[start:stop]
            fresh = here + push * (inverse[start:stop] * rest)
            if order > 0:
                fresh = fresh + carry * (here - previous[start:stop])
            previous[start:stop] = fresh
        current, previous = previous, current
    return current, previous


def begin(table, inverse, source, buffers, low, high, chunk):
    for start in range(low, high, chunk):
        stop = min(start + chunk, high)
        fresh = table[0][1] * (inverse[start:stop] * source(start, stop))
        buffers[0][start:stop] = fresh
        buffers[1][start:stop] = jnp.zeros_like(fresh)


ROWS0 = 48


CHUNK0 = 2


def level0_parts(shape, beta, absorb, parts, low, high):
    diag, inverse, first, second, third = parts
    half = face(0)
    first[low - 1 : low] = half * (beta(low - 1, low) + beta(low, low + 1))
    for start in range(low, high, CHUNK0):
        stop = min(start + CHUNK0, high)
        here = beta(start, stop)
        first[start:stop] = half * (here + beta(start + 1, stop + 1))
        lower = half * (beta(start - 1, stop - 1) + here)
        second[start:stop], third[start:stop], share = shape.faces(here, half)
        total = absorb(start, stop) + lower + first[start:stop] + share
        diag[start:stop] = total
        inverse[start:stop] = jnp.where(here > 0.0, 1.0 / total, 0.0)


def pairs(value):
    return jnp.stack([value[at] + value[at + 1] for at in range(0, value.shape[0], 2)])


def coarse_rows(ref, value):
    count = value.shape[0]
    zero = jnp.zeros((count, 8, LANES), jnp.float32)
    ref[0:count, 0:8, :] = zero
    ref[0:count, 8:56, :] = pair_sum(value, 1)
    ref[0:count, 56:64, :] = zero

    def take(offset):
        halves = [
            [ref[at, pl.ds(32 * half + offset, 8, stride=4), :] for half in range(2)]
            for at in range(count)
        ]
        return jnp.stack([jnp.concatenate(both) for both in halves])

    even = (lax.broadcasted_iota(jnp.int32, (count, ROWS1, LANES), 2) & 1) == 0
    return 0.125 * jnp.where(even, take(0) + take(1), take(2) + take(3))


RIM_REACH = (3, 3, 4)
END_REACH = (2, 2, 3)
RIMS = (0, 12, 24)
ENDS = (40, 48, 56)
KEPT0 = 10
KEPT_ROWS0 = 32


def pre0_kernel(
    own, outer, rims, kept_out, rest_out, beta_out, diag_out, absorb_out, send_out,
    diag, inverse, first, second, third, one, two, tmp,
):
    zero = jnp.zeros((8, LANES), jnp.float32)

    def piece(kind):
        def planes(start, stop):
            found = []
            for plane in range(start, stop):
                part, member = plane // 8, plane % 8 // 2
                if part == 1:
                    found.append(own[member, kind, plane % 2])
                    continue
                side = part // 2
                at = 2 * (6 * member + 2 * kind + plane % 2)
                own_rows = [outer[side, at], outer[side, at + 1]]
                outward = LAYER - 1 - member if side == 0 else member
                found_tiles = []
                for first_tile, reach in ((RIMS[kind], RIM_REACH[kind]), (ENDS[kind], END_REACH[kind])):
                    if outward < reach:
                        index = reach - 1 - outward if side == 0 else outward
                        at = first_tile + 2 * (2 * index + plane % 2)
                        found_tiles.append((rims[side, at], rims[side, at + 1]))
                    else:
                        found_tiles.append((zero, zero))
                rim, ends = found_tiles
                rows = [rim[0], *own_rows, rim[1]]
                found.append(jnp.concatenate([ends[0], *rows, ends[1]]))
            return jnp.stack(found)

        return planes

    source, absorb, beta = piece(0), piece(1), piece(2)
    shape = Packed(1, ROWS0, False)
    parts = (diag, inverse, first, second, third)
    level0_parts(shape, beta, absorb, parts, 1, 23)
    table = chebyshev_table(SWEEPS)
    begin(table, inverse, source, (one, two), 1, 23, CHUNK0)
    ranges = [(1 + order, 23 - order) for order in range(1, SWEEPS)]
    current, previous = sweep(
        shape, list(enumerate(table))[1:], source, parts, (one, two), ranges, CHUNK0
    )
    previous[4:20] = source(4, 20)
    base = 2 * (position() % LAYER) + 4
    for plane in range(KEPT0):
        for number, kept in enumerate((current, previous) + parts):
            kept_out[number, plane] = kept[base + plane, 8:40, :]
    coarse = Packed(2, ROWS1, False)
    half = face(1)
    betas = coarse_rows(tmp.at[0:8], pairs(beta(4, 20)))
    wide = coarse_rows(tmp.at[8:14], pairs(absorb(6, 18)))
    rest = [residual(shape, source, parts, current, p, p + 2) for p in range(6, 18, 2)]
    rest_out[...] = coarse_rows(tmp.at[14:20], jnp.stack([x[0] + x[1] for x in rest]))
    here = betas[1:7]
    _, _, share = coarse.faces(here, half)
    beta_out[...] = betas
    diag_out[...] = wide + half * (here + betas[0:6]) + half * (here + betas[2:8]) + share
    absorb_out[...] = wide[1:5]
    core = position() & 1
    at = 0
    for ref, count, first_plane in ((rest_out, 5, core), (beta_out, 6, 2 * core), (diag_out, 5, core)):
        for plane in range(count):
            send_out[at : at + 12, :] = ref[first_plane + plane, 2:14, :]
            at += 12


DEPTH1 = 16
ROWS1 = 16


def gather_level1(region, rest, beta, diag, outer):
    blank = jnp.zeros((2, LANES), jnp.float32)
    for side, start in ((0, 0), (1, 10)):
        at = 0
        for kind, first_plane, count in ((0, 1 - side, 5), (1, 0, 6), (2, 1 - side, 5)):
            for plane in range(start + first_plane, start + first_plane + count):
                region[kind, plane, 0:2, :] = blank
                region[kind, plane, 2:14, :] = outer[side, at : at + 12, :]
                region[kind, plane, 14:16, :] = blank
                at += 12
    region[0, 6:10] = rest[1:5]
    region[1, 6:10] = beta[2:6]
    region[2, 6:10] = diag[1:5]


CHUNK1 = 4


def level1_parts(shape, region, inverse, first, second, third):
    half = face(1)
    beta = region.at[1]
    first[0:1] = half * (beta[0:1] + beta[1:2])
    for start in range(1, DEPTH1 - 1, CHUNK1):
        stop = min(start + CHUNK1, DEPTH1 - 1)
        here = beta[start:stop]
        second[start:stop], third[start:stop], _ = shape.faces(here, half)
        inverse[start:stop] = jnp.where(here > 0.0, 1.0 / region[2, start:stop], 0.0)
        first[start:stop] = half * (here + beta[start + 1 : stop + 1])


def coarser_rows(ref, value, start):
    ref[...] = pair_sum(pair_sum(value, 1), 2)
    inner = lanes_of(1) & 3
    rows = []
    for at in range(value.shape[0]):
        row = ref[at, start : start + 1, :]
        for offset in range(1, 4):
            row = jnp.where(inner == offset, ref[at, start + offset : start + offset + 1, :], row)
        rows.append(0.125 * row)
    return rows


def pre1_kernel(
    rest1, beta1, diag1, outer, absorb, pay_out, region, inverse, first, second, third,
    one, two, tmp, tile,
):
    gather_level1(region, rest1, beta1, diag1, outer)
    shape = Packed(2, ROWS1, False)
    level1_parts(shape, region, inverse, first, second, third)
    source = lambda start, stop: region[0, start:stop]
    parts = (region.at[2], inverse, first, second, third)
    table = chebyshev_table(SWEEPS)
    begin(table, inverse, source, (one, two), 2, 14, CHUNK1)
    ranges = [(2 + order, 14 - order) for order in range(1, SWEEPS)]
    current, _ = sweep(
        shape, list(enumerate(table))[1:], source, parts, (one, two), ranges, CHUNK1
    )
    rest = residual(shape, source, parts, current, 6, 10)
    totals = [pairs(rest), pairs(region[1, 6:10]), pairs(absorb[...])]
    rows = coarser_rows(tmp, jnp.concatenate(totals), 6)
    for at in range(6):
        tile[at : at + 1, :] = rows[at]
    tile[6:8, :] = jnp.zeros((2, LANES), jnp.float32)
    member = position() % LAYER
    tile[8:10, :] = tile[pl.ds(2 * member, 2), :]
    tile[10:14, :] = current[6 + member, 6:10, :]
    for at in range(6):
        row = jnp.broadcast_to(tile[8 + at : 9 + at, :], (16, LANES))
        pay_out[:, at * LANES : (at + 1) * LANES] = row


DEPTH2 = 32
SLOT = 48
KIND_AT = (0, 2, 1)
ROWS2 = 8


CHUNK2 = 4


def level2_parts(shape, beta, absorb, parts):
    diag, inverse, first, second, third = parts
    half = face(2)
    first[0:1] = jnp.zeros((1, ROWS2, LANES), jnp.float32)
    for start in range(1, DEPTH2 + 1, CHUNK2):
        stop = start + CHUNK2
        here = beta[start:stop]
        upper = half * (here + beta[start + 1 : stop + 1])
        lower = half * (here + beta[start - 1 : stop - 1])
        second[start:stop], third[start:stop], share = shape.faces(here, half)
        total = absorb[start:stop] + lower + upper + share
        first[start:stop] = upper
        diag[start:stop] = total
        inverse[start:stop] = 1.0 / total


def bottom_rows(ref, planes):
    value = planes(1, DEPTH2 + 1)
    value = jnp.concatenate([value[at] + value[at + 1] for at in range(0, DEPTH2, 2)])
    ref[...] = pair_sum(pair_sum(value, 1), 4)
    inner = lanes_of(32) & 7
    total = None
    for offset in range(4):
        value = jnp.concatenate(
            [ref[pl.ds(32 * block + offset, 8, stride=4), :] for block in range(4)]
        )
        moved = along(value, 1 if offset % 2 == 0 else -1)
        same = 2 * offset + offset % 2
        value = jnp.where(inner == same, value, moved)
        total = value if total is None else jnp.where(inner >> 1 == offset, value, total)
    return 0.125 * total


def bottom_solve(source, absorb, beta):
    shape = Packed(8, 2, True)
    half = face(3)
    row = rows_of(32)
    last, initial = row >= 30, row < 2
    up = jnp.where(last, 0.0, across(beta, 2))
    down = jnp.where(initial, 0.0, across(beta, -2))
    second, third, share = shape.faces(beta, half)
    upper = half * (beta + up)
    diag = absorb + half * (beta + down) + upper + share
    first = jnp.where(last, 0.0, upper)
    inverse = 1.0 / diag
    table = chebyshev_table(BOTTOM)
    current = table[0][1] * (inverse * source)
    previous = jnp.zeros_like(current)
    for carry, push in table[1:]:
        rest = source - diag * current + first * across(current, 2) + across(first * current, -2)
        rest = rest + shape.coupled(current, second, third)
        fresh = current + carry * (current - previous) + push * (inverse * rest)
        current, previous = fresh, current
    return current


def bottom_prolong(ref, value):
    inner = lanes_of(32) & 7
    part = inner & 3
    back1, back2 = along(value, -1), along(value, -2)
    fore1, fore2 = along(value, 1), along(value, 2)
    low = jnp.where(part == 0, value, jnp.where(part == 3, back2, back1))
    high = jnp.where(part == 3, value, jnp.where(part == 0, fore2, fore1))
    left = inner < 4
    for offset in range(4):
        base = low if offset % 2 == 0 else high
        if offset < 2:
            moved = jnp.where(left, base, along(base, -4))
        else:
            moved = jnp.where(left, along(base, 4), base)
        for block in range(4):
            ref[pl.ds(32 * block + offset, 8, stride=4), :] = moved[8 * block : 8 * block + 8]


def solve23(gathered, rows2, parts2, one2, two2, tall):
    shape = Packed(4, ROWS2, True)
    zero = jnp.zeros((ROWS2, LANES), jnp.float32)
    for number in range(3):
        for plane in range(DEPTH2):
            at = SLOT * 8 * KIND_AT[number] + plane
            rows2[number, plane + 1] = gathered[pl.ds(at, 8, stride=SLOT), :]
    for ref in (rows2.at[1], one2, two2):
        ref[0] = zero
        ref[DEPTH2 + 1] = zero

    source2 = lambda start, stop: rows2[0, start:stop]
    level2_parts(shape, rows2.at[1], rows2.at[2], parts2)
    table = chebyshev_table(SWEEPS)
    begin(table, parts2[1], source2, (one2, two2), 1, DEPTH2 + 1, CHUNK2)
    everywhere = [(1, DEPTH2 + 1)] * SWEEPS
    current, previous = sweep(
        shape, list(enumerate(table))[1:], source2, parts2, (one2, two2), everywhere, CHUNK2
    )
    source3 = bottom_rows(
        tall.at[0], lambda start, stop: residual(shape, source2, parts2, current, start, stop)
    )
    absorb3 = bottom_rows(tall.at[1], lambda start, stop: rows2[2, start:stop])
    beta3 = bottom_rows(tall.at[2], lambda start, stop: rows2[1, start:stop])
    bottom_prolong(tall.at[0], bottom_solve(source3, absorb3, beta3))
    for plane in range(DEPTH2):
        pair = plane // 2
        current[plane + 1] = current[plane + 1] + tall[0, 8 * pair : 8 * pair + 8, :]
    current, previous = sweep(
        shape, list(enumerate(table)), source2, parts2, (current, previous), everywhere, CHUNK2
    )
    return current


def post1(packed, whole, region, parts, one, two, wide, tmp):
    inverse, first, second, third = parts
    shape = Packed(2, ROWS1, False)
    layer = position() // LAYER
    row = column_position() + 6
    zero = jnp.zeros((8, LANES), jnp.float32)
    for plane in range(DEPTH2 + 6):
        wide[plane, 0:8, :] = zero
        wide[plane, 16:24, :] = zero
        inside = 3 <= plane < DEPTH2 + 3
        wide[plane, 8:16, :] = whole[plane - 2] if inside else zero
    value = jnp.stack([wide[2 * layer + pair, pl.ds(row, 8), :] for pair in range(8)])
    inner = lax.broadcasted_iota(jnp.int32, value.shape, 2) & 3
    moved = {steps: along(value, steps) for steps in range(-3, 4) if steps}
    moved[0] = value
    for offset in range(4):
        picked = moved[offset]
        for lane in range(1, 4):
            picked = jnp.where(inner == lane, moved[offset - lane], picked)
        for pair in range(8):
            tmp[pair, pl.ds(offset, 8, stride=4), :] = picked[pair]
    place = column_position()
    columns = (
        (jnp.maximum(place - 1, 0), jnp.where(place > 0, 1.0, 0.0)),
        (place, 1.0),
        (jnp.minimum(place + 1, 7), jnp.where(place < 7, 1.0, 0.0)),
    )
    blank = jnp.zeros((2, LANES), jnp.float32)
    for plane in range(DEPTH1):
        member = (plane - 6) % LAYER
        at = 16 * (member % 2) + 8 * (member // 2)
        row = 32 + 4 * (plane // LAYER)
        one[plane, 0:2, :] = blank
        for number, (who, there) in enumerate(columns):
            start = 2 + 4 * number
            one[plane, start : start + 4, :] = there * packed[at + who, row : row + 4, :]
        one[plane, 14:16, :] = blank
    for plane in range(DEPTH1):
        one[plane] = one[plane] + tmp[plane // 2, 2:18, :]
    table = chebyshev_table(SWEEPS)
    ranges = [(order, DEPTH1 - order) for order in range(1, SWEEPS + 1)]
    current, _ = sweep(
        shape, list(enumerate(table)), lambda start, stop: region[0, start:stop],
        (region.at[2], inverse, first, second, third), (one, two), ranges, CHUNK1,
    )
    return current


def post0(kept, coarse, out, one, two, tmp):
    field, source = kept.at[0], kept.at[1]
    parts = tuple(kept.at[number] for number in range(2, 7))
    member = position() % LAYER
    shape = Packed(1, ROWS0, False)
    value = jnp.stack([coarse[4 + member + pair, 4:12, :] for pair in range(5)])
    even = (lax.broadcasted_iota(jnp.int32, value.shape, 2) & 1) == 0
    upper_rows = jnp.where(even, value, along(value, -1))
    lower_rows = jnp.where(even, along(value, 1), value)
    for pair in range(5):
        for offset in range(4):
            rows = upper_rows if offset < 2 else lower_rows
            tmp[pair, pl.ds(offset, 8, stride=4), :] = rows[pair]
    for plane in range(KEPT0):
        one[plane] = field[plane] + tmp[plane // 2]
    table = chebyshev_table(SWEEPS)
    ranges = [(1 + order, KEPT0 - 1 - order) for order in range(SWEEPS)]
    current, _ = sweep(
        shape, list(enumerate(table)), lambda start, stop: source[start:stop], parts,
        (one, two), ranges, CHUNK0,
    )
    out[...] = current[4:6, 8:24, :]


def finish_kernel(
    gathered, packed, region1, inverse1, first1, second1, third1, kept0, out,
    rows2, diag2, inverse2, first2, second2, third2, one2, two2, tall,
    one1, two1, wide1, tmp1, one0, two0, tmp0,
):
    parts2 = (diag2, inverse2, first2, second2, third2)
    whole = solve23(gathered, rows2, parts2, one2, two2, tall)
    parts1 = (inverse1, first1, second1, third1)
    coarse = post1(packed, whole, region1, parts1, one1, two1, wide1, tmp1)
    post0(kept0, coarse, out, one0, two0, tmp0)


def f32(*shape):
    return jax.ShapeDtypeStruct(shape, jnp.float32)


def buffer(*shape):
    return pltpu.VMEM(shape, jnp.float32)


def call(kernel, out, scratch, name, *operands):
    return pl.pallas_call(
        kernel,
        out_shape=out,
        scratch_shapes=scratch,
        name=name,
        compiler_params=pltpu.CompilerParams(vmem_limit_bytes=VMEM),
    )(*operands)


def pre0(*pieces):
    plane = buffer(24, ROWS0, LANES)
    scratch = [plane] * 7 + [buffer(20, 64, LANES)]
    coarse = lambda count: f32(count, ROWS1, LANES)
    out = (f32(7, KEPT0, KEPT_ROWS0, LANES), coarse(6), coarse(8), coarse(6), coarse(4), f32(192, LANES))
    return call(pre0_kernel, out, scratch, "pre0", *pieces)


def pre1(*pieces):
    plane, work = f32(DEPTH1, ROWS1, LANES), buffer(DEPTH1, ROWS1, LANES)
    scratch = [work, work, buffer(6, ROWS1, LANES), buffer(16, LANES)]
    out = (f32(16, 6 * LANES), f32(3, DEPTH1, ROWS1, LANES)) + (plane,) * 4
    return call(pre1_kernel, out, scratch, "pre1", *pieces)


def finish(*pieces):
    plane2 = buffer(DEPTH2 + 2, ROWS2, LANES)
    plane1 = buffer(DEPTH1, ROWS1, LANES)
    plane0 = buffer(KEPT0, KEPT_ROWS0, LANES)
    scratch = [buffer(3, DEPTH2 + 2, ROWS2, LANES)] + [plane2] * 7 + [buffer(3, 128, LANES)]
    scratch += [plane1] * 2 + [buffer(DEPTH2 + 6, 24, LANES), buffer(8, 32, LANES)]
    scratch += [plane0] * 2 + [buffer(5, KEPT_ROWS0, LANES)]
    return call(finish_kernel, f32(2, 16, LANES), scratch, "finish", *pieces)


def layers_apart(value, steps):
    count = lax.axis_size("gx")
    ways = [(i, i + (LAYER * steps if i % 2 == 0 else -LAYER * steps)) for i in range(count)]
    return lax.ppermute(value, "gx", [(i, j) for i, j in ways if 0 <= j < count])


def columns_apart(value):
    count, wide = lax.axis_size("gx"), lax.axis_size("gy")
    ways = [
        (i * wide + j, i * wide + j + (1 if i % 2 == 0 else -1))
        for i in range(count)
        for j in range(wide)
        if 0 <= j + (1 if i % 2 == 0 else -1) < wide
    ]
    return lax.ppermute(value, ("gx", "gy"), ways)


def body(source, absorb, beta):
    members = lax.axis_size("gx")
    wide = lax.axis_size("gy")
    layers = members // LAYER
    near = [[LAYER * z + c for c in range(LAYER)] for z in range(layers)]
    chips = [[2 * chip, 2 * chip + 1] for chip in range(members // 2)]
    column = [[LAYER * z + c for z in range(layers)] for c in range(LAYER)]
    cores = [
        [(LAYER * z + 2 * chip + core) * wide + y for chip in range(2) for y in range(wide)]
        for z in range(layers)
        for core in range(2)
    ]
    first_core = lax.axis_index("gx") % 2 == 0

    def both(value):
        return lax.all_gather(value, "gx", axis_index_groups=chips)

    local = jnp.stack([source, absorb, beta])
    own = lax.all_gather(local, "gx", axis_index_groups=near)
    def tiles_of(arrays):
        return jnp.concatenate([x.reshape(-1, 8, LANES) for x in arrays])

    sides = columns_apart(own)
    outer = layers_apart(own, 1)
    sides = both(sides)
    layer = jnp.concatenate([sides[0], own, sides[1]], axis=-2)
    rims = jnp.concatenate([sides[0, ..., 8:, :], sides[1, ..., :8, :]], axis=-2)
    ends = jnp.concatenate([sides[0, ..., :8, :], sides[1, ..., 8:, :]], axis=-2)
    sent = []
    for rows, reaches in ((rims, RIM_REACH), (ends, END_REACH)):
        for kind, reach in enumerate(reaches):
            sent.append(jnp.where(first_core, rows[LAYER - reach :, kind], rows[:reach, kind]))
    rest = layers_apart(tiles_of(sent), 1)
    outer = both(tiles_of([outer]))
    kept0, rest1, beta1, diag1, absorb1, sent1 = pre0(layer, outer, both(rest))

    outer = both(layers_apart(sent1, 1))
    pay, *kept1 = pre1(rest1, beta1, diag1, outer, absorb1)

    place = lax.axis_index("gx")
    start = (place >> 2) + (((place & 3) ^ 3) >> 1)
    pay, start = lax.optimization_barrier((pay, start))
    rows = lax.all_to_all(pay, "gx", 0, 0, axis_index_groups=column)
    rows, start = lax.optimization_barrier((rows, start))
    fields = jnp.pad(rows[:, 2 * LANES :], ((2, 2), (0, 0)))
    fields = lax.dynamic_slice_in_dim(fields, start, 4)
    rows = jnp.concatenate([x.reshape(-1, LANES) for x in (rows[:, : 2 * LANES], fields)])
    rows = jnp.broadcast_to(rows, (2 * wide,) + rows.shape)
    rows = lax.all_to_all(rows, ("gx", "gy"), 0, 0, axis_index_groups=cores)
    packed = both(rows).reshape(-1, SLOT, LANES)
    return finish(packed.reshape(-1, LANES), packed, *kept1, kept0)


def solution(mesh):
    placed = (P("gx", "gy", None), P("gx", "gy", None), P("gx", "gy", None))
    return jax.shard_map(
        body, mesh=mesh, in_specs=placed, out_specs=P("gx", "gy", None), check_vma=False
    )
```

```python
import jax
import jax.numpy as jnp
from jax import lax
from jax.experimental import pallas as pl
from jax.experimental.pallas import tpu as pltpu
from jax.sharding import PartitionSpec as P

SWEEPS = 4
BOTTOM = 8
LANES = 128
VMEM = 24 * 1024 * 1024

LAYER = 4
PACK = (1, 2, 4, 8)


def face(level):
    return 0.5 * 0.25**level


def chebyshev_table(count):
    centre = 1.125
    half_width = 0.875
    ratio = centre / half_width
    factor = 1.0 / ratio
    table = [(0.0, 1.0 / centre)]
    for order in range(1, count):
        fresh_factor = 1.0 / (2.0 * ratio - factor)
        table.append((fresh_factor * factor, 2.0 * fresh_factor / half_width))
        factor = fresh_factor
    return table


def position():
    return lax.axis_index("gx")


def column_position():
    return lax.axis_index("gy")


def lanes_of(rows):
    return lax.broadcasted_iota(jnp.int32, (rows, LANES), 1)


def rows_of(rows):
    return lax.broadcasted_iota(jnp.int32, (rows, LANES), 0)


def along(value, steps):
    return pltpu.roll(value, (-steps) % LANES, value.ndim - 1)


def across(value, steps):
    rows = value.shape[-2]
    return pltpu.roll(value, (-steps) % rows, value.ndim - 2)


class Packed:
    def __init__(self, pack, period, whole):
        self.pack = pack
        self.period = period
        self.whole = whole
        self.kept = {}

    def masks(self, value):
        if value.shape not in self.kept:
            pack, dims = self.pack, value.ndim
            lane = lax.broadcasted_iota(jnp.int32, value.shape, dims - 1)
            row = lax.broadcasted_iota(jnp.int32, value.shape, dims - 2) & (self.period - 1)
            inner = lane & (pack - 1)
            self.kept[value.shape] = dict(
                up=inner < pack - 1,
                down=inner > 0,
                third_last=lane >= LANES - pack,
                third_first=lane < pack,
                second_last=(row == self.period - 1) & (inner == pack - 1),
                second_first=(row == 0) & (inner == 0),
            )
        return self.kept[value.shape]

    def second_up(self, value):
        if self.pack == 1:
            return across(value, 1)
        mask = self.masks(value)["up"]
        return jnp.where(mask, along(value, 1), across(along(value, 1 - self.pack), 1))

    def second_down(self, value):
        if self.pack == 1:
            return across(value, -1)
        mask = self.masks(value)["down"]
        return jnp.where(mask, along(value, -1), across(along(value, self.pack - 1), -1))

    def faces(self, beta, half):
        mask = self.masks(beta)
        up = self.second_up(beta)
        if self.whole:
            up = jnp.where(mask["second_last"], 0.0, up)
        second = half * (beta + up)
        down = self.second_down(beta)
        if self.whole:
            down = jnp.where(mask["second_first"], 0.0, down)
        share = half * (beta + down) + second
        if self.whole:
            second = jnp.where(mask["second_last"], 0.0, second)
        third_up = jnp.where(mask["third_last"], 0.0, along(beta, self.pack))
        third = half * (beta + third_up)
        third_down = jnp.where(mask["third_first"], 0.0, along(beta, -self.pack))
        share = share + half * (beta + third_down) + third
        return second, jnp.where(mask["third_last"], 0.0, third), share

    def coupled(self, value, second, third):
        total = second * self.second_up(value) + self.second_down(second * value)
        total = total + third * along(value, self.pack)
        return total + along(third * value, -self.pack)


def pair_sum(value, width):
    low = (lax.broadcasted_iota(jnp.int32, value.shape, value.ndim - 1) & width) == 0
    return value + jnp.where(low, along(value, width), along(value, -width))


def residual(shape, source, parts, field, start, stop):
    diag, _, first, second, third = parts
    here = field[start:stop]
    total = source(start, stop) - diag[start:stop] * here
    total = total + first[start:stop] * field[start + 1 : stop + 1]
    total = total + first[start - 1 : stop - 1] * field[start - 1 : stop - 1]
    return total + shape.coupled(here, second[start:stop], third[start:stop])


def sweep(shape, orders, source, parts, buffers, ranges, chunk):
    inverse = parts[1]
    current, previous = buffers
    for (order, (carry, push)), (low, high) in zip(orders, ranges):
        for start in range(low, high, chunk):
            stop = min(start + chunk, high)
            rest = residual(shape, source, parts, current, start, stop)
            here = current[start:stop]
            fresh = here + push * (inverse[start:stop] * rest)
            if order > 0:
                fresh = fresh + carry * (here - previous[start:stop])
            previous[start:stop] = fresh
        current, previous = previous, current
    return current, previous


def begin(table, inverse, source, buffers, low, high, chunk):
    for start in range(low, high, chunk):
        stop = min(start + chunk, high)
        fresh = table[0][1] * (inverse[start:stop] * source(start, stop))
        buffers[0][start:stop] = fresh
        buffers[1][start:stop] = jnp.zeros_like(fresh)


ROWS0 = 48


CHUNK0 = 2


def level0_parts(shape, beta, absorb, parts, low, high):
    diag, inverse, first, second, third = parts
    half = face(0)
    first[low - 1 : low] = half * (beta(low - 1, low) + beta(low, low + 1))
    for start in range(low, high, CHUNK0):
        stop = min(start + CHUNK0, high)
        here = beta(start, stop)
        first[start:stop] = half * (here + beta(start + 1, stop + 1))
        lower = half * (beta(start - 1, stop - 1) + here)
        second[start:stop], third[start:stop], share = shape.faces(here, half)
        total = absorb(start, stop) + lower + first[start:stop] + share
        diag[start:stop] = total
        inverse[start:stop] = jnp.where(here > 0.0, 1.0 / total, 0.0)


def pairs(value):
    return jnp.stack([value[at] + value[at + 1] for at in range(0, value.shape[0], 2)])


def coarse_rows(ref, value):
    count = value.shape[0]
    zero = jnp.zeros((count, 8, LANES), jnp.float32)
    ref[0:count, 0:8, :] = zero
    ref[0:count, 8:56, :] = pair_sum(value, 1)
    ref[0:count, 56:64, :] = zero

    def take(offset):
        halves = [
            [ref[at, pl.ds(32 * half + offset, 8, stride=4), :] for half in range(2)]
            for at in range(count)
        ]
        return jnp.stack([jnp.concatenate(both) for both in halves])

    even = (lax.broadcasted_iota(jnp.int32, (count, ROWS1, LANES), 2) & 1) == 0
    return 0.125 * jnp.where(even, take(0) + take(1), take(2) + take(3))


RIM_REACH = (3, 3, 4)
END_REACH = (2, 2, 3)
RIMS = (0, 12, 24)
ENDS = (40, 48, 56)
KEPT0 = 10
KEPT_ROWS0 = 32


MESSAGE1 = [(kind, away) for kind in range(3) for away in range(1, 7 if kind == 1 else 6)]


def message_rows(kind, away):
    return (2, 14) if away < (3 if kind == 1 else 2) else (4, 12)


def pre0_kernel(
    own, outer, rims, kept_out, rest_out, beta_out, diag_out, absorb_out, send_out,
    diag, inverse, first, second, third, one, two, tmp,
):
    zero = jnp.zeros((8, LANES), jnp.float32)

    def piece(kind):
        def planes(start, stop):
            found = []
            for plane in range(start, stop):
                part, member = plane // 8, plane % 8 // 2
                if part == 1:
                    found.append(own[member, kind, plane % 2])
                    continue
                side = part // 2
                at = 2 * (6 * member + 2 * kind + plane % 2)
                own_rows = [outer[side, at], outer[side, at + 1]]
                outward = LAYER - 1 - member if side == 0 else member
                found_tiles = []
                for first_tile, reach in ((RIMS[kind], RIM_REACH[kind]), (ENDS[kind], END_REACH[kind])):
                    if outward < reach:
                        index = reach - 1 - outward if side == 0 else outward
                        at = first_tile + 2 * (2 * index + plane % 2)
                        found_tiles.append((rims[side, at], rims[side, at + 1]))
                    else:
                        found_tiles.append((zero, zero))
                rim, ends = found_tiles
                rows = [rim[0], *own_rows, rim[1]]
                found.append(jnp.concatenate([ends[0], *rows, ends[1]]))
            return jnp.stack(found)

        return planes

    source, absorb, beta = piece(0), piece(1), piece(2)
    shape = Packed(1, ROWS0, False)
    parts = (diag, inverse, first, second, third)
    level0_parts(shape, beta, absorb, parts, 1, 23)
    table = chebyshev_table(SWEEPS)
    begin(table, inverse, source, (one, two), 1, 23, CHUNK0)
    ranges = [(1 + order, 23 - order) for order in range(1, SWEEPS)]
    current, previous = sweep(
        shape, list(enumerate(table))[1:], source, parts, (one, two), ranges, CHUNK0
    )
    previous[4:20] = source(4, 20)
    base = 2 * (position() % LAYER) + 4
    for plane in range(KEPT0):
        for number, kept in enumerate((current, previous) + parts):
            kept_out[number, plane] = kept[base + plane, 8:40, :]
    coarse = Packed(2, ROWS1, False)
    half = face(1)
    betas = coarse_rows(tmp.at[0:8], pairs(beta(4, 20)))
    wide = coarse_rows(tmp.at[8:14], pairs(absorb(6, 18)))
    rest = [residual(shape, source, parts, current, p, p + 2) for p in range(6, 18, 2)]
    rest_out[...] = coarse_rows(tmp.at[14:20], jnp.stack([x[0] + x[1] for x in rest]))
    here = betas[1:7]
    _, _, share = coarse.faces(here, half)
    beta_out[...] = betas
    diag_out[...] = wide + half * (here + betas[0:6]) + half * (here + betas[2:8]) + share
    absorb_out[...] = wide[1:5]
    core = position() & 1
    at = 0
    for kind, away in MESSAGE1:
        ref, near = ((rest_out, 5), (beta_out, 6), (diag_out, 5))[kind]
        low, high = message_rows(kind, away)
        plane = near - away + core * (2 * away - 5)
        send_out[at : at + high - low, :] = ref[plane, low:high, :]
        at += high - low


DEPTH1 = 16
ROWS1 = 16


def gather_level1(region, rest, beta, diag, outer):
    for side in range(2):
        at = 0
        for kind, away in MESSAGE1:
            plane = 6 - away if side == 0 else 9 + away
            low, high = message_rows(kind, away)
            region[kind, plane, 0:low, :] = jnp.zeros((low, LANES), jnp.float32)
            region[kind, plane, low:high, :] = outer[side, at : at + high - low, :]
            region[kind, plane, high:16, :] = jnp.zeros((16 - high, LANES), jnp.float32)
            at += high - low
    region[0, 6:10] = rest[1:5]
    region[1, 6:10] = beta[2:6]
    region[2, 6:10] = diag[1:5]


CHUNK1 = 4


def level1_parts(shape, region, inverse, first, second, third):
    half = face(1)
    beta = region.at[1]
    first[0:1] = half * (beta[0:1] + beta[1:2])
    for start in range(1, DEPTH1 - 1, CHUNK1):
        stop = min(start + CHUNK1, DEPTH1 - 1)
        here = beta[start:stop]
        second[start:stop], third[start:stop], _ = shape.faces(here, half)
        inverse[start:stop] = jnp.where(here > 0.0, 1.0 / region[2, start:stop], 0.0)
        first[start:stop] = half * (here + beta[start + 1 : stop + 1])


def coarser_rows(ref, value, start):
    ref[...] = pair_sum(pair_sum(value, 1), 2)
    inner = lanes_of(1) & 3
    rows = []
    for at in range(value.shape[0]):
        row = ref[at, start : start + 1, :]
        for offset in range(1, 4):
            row = jnp.where(inner == offset, ref[at, start + offset : start + offset + 1, :], row)
        rows.append(0.125 * row)
    return rows


def pre1_kernel(
    rest1, beta1, diag1, outer, absorb, pay_out, region, inverse, first, second, third,
    one, two, tmp, tile,
):
    gather_level1(region, rest1, beta1, diag1, outer)
    shape = Packed(2, ROWS1, False)
    level1_parts(shape, region, inverse, first, second, third)
    source = lambda start, stop: region[0, start:stop]
    parts = (region.at[2], inverse, first, second, third)
    table = chebyshev_table(SWEEPS)
    begin(table, inverse, source, (one, two), 2, 14, CHUNK1)
    ranges = [(2 + order, 14 - order) for order in range(1, SWEEPS)]
    current, _ = sweep(
        shape, list(enumerate(table))[1:], source, parts, (one, two), ranges, CHUNK1
    )
    rest = residual(shape, source, parts, current, 6, 10)
    totals = [pairs(rest), pairs(region[1, 6:10]), pairs(absorb[...])]
    rows = coarser_rows(tmp, jnp.concatenate(totals), 6)
    for at in range(6):
        tile[at : at + 1, :] = rows[at]
    tile[6:8, :] = jnp.zeros((2, LANES), jnp.float32)
    member = position() % LAYER
    tile[8:10, :] = tile[pl.ds(2 * member, 2), :]
    tile[10:14, :] = current[6 + member, 6:10, :]
    for at in range(6):
        row = jnp.broadcast_to(tile[8 + at : 9 + at, :], (16, LANES))
        pay_out[:, at * LANES : (at + 1) * LANES] = row


DEPTH2 = 32
SLOT = 48
KIND_AT = (0, 2, 1)
ROWS2 = 8


CHUNK2 = 4


def level2_parts(shape, beta, absorb, parts):
    diag, inverse, first, second, third = parts
    half = face(2)
    first[0:1] = jnp.zeros((1, ROWS2, LANES), jnp.float32)
    for start in range(1, DEPTH2 + 1, CHUNK2):
        stop = start + CHUNK2
        here = beta[start:stop]
        upper = half * (here + beta[start + 1 : stop + 1])
        lower = half * (here + beta[start - 1 : stop - 1])
        second[start:stop], third[start:stop], share = shape.faces(here, half)
        total = absorb[start:stop] + lower + upper + share
        first[start:stop] = upper
        diag[start:stop] = total
        inverse[start:stop] = 1.0 / total


def bottom_rows(ref, planes):
    value = planes(1, DEPTH2 + 1)
    value = jnp.concatenate([value[at] + value[at + 1] for at in range(0, DEPTH2, 2)])
    ref[...] = pair_sum(pair_sum(value, 1), 4)
    inner = lanes_of(32) & 7
    total = None
    for offset in range(4):
        value = jnp.concatenate(
            [ref[pl.ds(32 * block + offset, 8, stride=4), :] for block in range(4)]
        )
        moved = along(value, 1 if offset % 2 == 0 else -1)
        same = 2 * offset + offset % 2
        value = jnp.where(inner == same, value, moved)
        total = value if total is None else jnp.where(inner >> 1 == offset, value, total)
    return 0.125 * total


def bottom_solve(source, absorb, beta):
    shape = Packed(8, 2, True)
    half = face(3)
    row = rows_of(32)
    last, initial = row >= 30, row < 2
    up = jnp.where(last, 0.0, across(beta, 2))
    down = jnp.where(initial, 0.0, across(beta, -2))
    second, third, share = shape.faces(beta, half)
    upper = half * (beta + up)
    diag = absorb + half * (beta + down) + upper + share
    first = jnp.where(last, 0.0, upper)
    inverse = 1.0 / diag
    table = chebyshev_table(BOTTOM)
    current = table[0][1] * (inverse * source)
    previous = jnp.zeros_like(current)
    for carry, push in table[1:]:
        rest = source - diag * current + first * across(current, 2) + across(first * current, -2)
        rest = rest + shape.coupled(current, second, third)
        fresh = current + carry * (current - previous) + push * (inverse * rest)
        current, previous = fresh, current
    return current


def bottom_prolong(ref, value):
    inner = lanes_of(32) & 7
    part = inner & 3
    back1, back2 = along(value, -1), along(value, -2)
    fore1, fore2 = along(value, 1), along(value, 2)
    low = jnp.where(part == 0, value, jnp.where(part == 3, back2, back1))
    high = jnp.where(part == 3, value, jnp.where(part == 0, fore2, fore1))
    left = inner < 4
    for offset in range(4):
        base = low if offset % 2 == 0 else high
        if offset < 2:
            moved = jnp.where(left, base, along(base, -4))
        else:
            moved = jnp.where(left, along(base, 4), base)
        for block in range(4):
            ref[pl.ds(32 * block + offset, 8, stride=4), :] = moved[8 * block : 8 * block + 8]


def solve23(gathered, rows2, parts2, one2, two2, tall):
    shape = Packed(4, ROWS2, True)
    zero = jnp.zeros((ROWS2, LANES), jnp.float32)
    for number in range(3):
        for plane in range(DEPTH2):
            at = SLOT * 8 * KIND_AT[number] + plane
            rows2[number, plane + 1] = gathered[pl.ds(at, 8, stride=SLOT), :]
    for ref in (rows2.at[1], one2, two2):
        ref[0] = zero
        ref[DEPTH2 + 1] = zero

    source2 = lambda start, stop: rows2[0, start:stop]
    level2_parts(shape, rows2.at[1], rows2.at[2], parts2)
    table = chebyshev_table(SWEEPS)
    begin(table, parts2[1], source2, (one2, two2), 1, DEPTH2 + 1, CHUNK2)
    everywhere = [(1, DEPTH2 + 1)] * SWEEPS
    current, previous = sweep(
        shape, list(enumerate(table))[1:], source2, parts2, (one2, two2), everywhere, CHUNK2
    )
    source3 = bottom_rows(
        tall.at[0], lambda start, stop: residual(shape, source2, parts2, current, start, stop)
    )
    absorb3 = bottom_rows(tall.at[1], lambda start, stop: rows2[2, start:stop])
    beta3 = bottom_rows(tall.at[2], lambda start, stop: rows2[1, start:stop])
    bottom_prolong(tall.at[0], bottom_solve(source3, absorb3, beta3))
    for plane in range(DEPTH2):
        pair = plane // 2
        current[plane + 1] = current[plane + 1] + tall[0, 8 * pair : 8 * pair + 8, :]
    current, previous = sweep(
        shape, list(enumerate(table)), source2, parts2, (current, previous), everywhere, CHUNK2
    )
    return current


def post1(packed, whole, region, parts, one, two, wide, tmp):
    inverse, first, second, third = parts
    shape = Packed(2, ROWS1, False)
    layer = position() // LAYER
    row = column_position() + 6
    zero = jnp.zeros((8, LANES), jnp.float32)
    for plane in range(DEPTH2 + 6):
        wide[plane, 0:8, :] = zero
        wide[plane, 16:24, :] = zero
        inside = 3 <= plane < DEPTH2 + 3
        wide[plane, 8:16, :] = whole[plane - 2] if inside else zero
    value = jnp.stack([wide[2 * layer + pair, pl.ds(row, 8), :] for pair in range(8)])
    inner = lax.broadcasted_iota(jnp.int32, value.shape, 2) & 3
    moved = {steps: along(value, steps) for steps in range(-3, 4) if steps}
    moved[0] = value
    for offset in range(4):
        picked = moved[offset]
        for lane in range(1, 4):
            picked = jnp.where(inner == lane, moved[offset - lane], picked)
        for pair in range(8):
            tmp[pair, pl.ds(offset, 8, stride=4), :] = picked[pair]
    place = column_position()
    columns = (
        (jnp.maximum(place - 1, 0), jnp.where(place > 0, 1.0, 0.0)),
        (place, 1.0),
        (jnp.minimum(place + 1, 7), jnp.where(place < 7, 1.0, 0.0)),
    )
    blank = jnp.zeros((2, LANES), jnp.float32)
    for plane in range(DEPTH1):
        member = (plane - 6) % LAYER
        at = 16 * (member % 2) + 8 * (member // 2)
        row = 32 + 4 * (plane // LAYER)
        one[plane, 0:2, :] = blank
        for number, (who, there) in enumerate(columns):
            start = 2 + 4 * number
            one[plane, start : start + 4, :] = there * packed[at + who, row : row + 4, :]
        one[plane, 14:16, :] = blank
    for plane in range(DEPTH1):
        one[plane] = one[plane] + tmp[plane // 2, 2:18, :]
    table = chebyshev_table(SWEEPS)
    ranges = [(order, DEPTH1 - order) for order in range(1, SWEEPS + 1)]
    current, _ = sweep(
        shape, list(enumerate(table)), lambda start, stop: region[0, start:stop],
        (region.at[2], inverse, first, second, third), (one, two), ranges, CHUNK1,
    )
    return current


def post0(kept, coarse, out, one, two, tmp):
    field, source = kept.at[0], kept.at[1]
    parts = tuple(kept.at[number] for number in range(2, 7))
    member = position() % LAYER
    shape = Packed(1, ROWS0, False)
    value = jnp.stack([coarse[4 + member + pair, 4:12, :] for pair in range(5)])
    even = (lax.broadcasted_iota(jnp.int32, value.shape, 2) & 1) == 0
    upper_rows = jnp.where(even, value, along(value, -1))
    lower_rows = jnp.where(even, along(value, 1), value)
    for pair in range(5):
        for offset in range(4):
            rows = upper_rows if offset < 2 else lower_rows
            tmp[pair, pl.ds(offset, 8, stride=4), :] = rows[pair]
    for plane in range(KEPT0):
        one[plane] = field[plane] + tmp[plane // 2]
    table = chebyshev_table(SWEEPS)
    ranges = [(1 + order, KEPT0 - 1 - order) for order in range(SWEEPS)]
    current, _ = sweep(
        shape, list(enumerate(table)), lambda start, stop: source[start:stop], parts,
        (one, two), ranges, CHUNK0,
    )
    out[...] = current[4:6, 8:24, :]


def finish_kernel(
    gathered, packed, region1, inverse1, first1, second1, third1, kept0, out,
    rows2, diag2, inverse2, first2, second2, third2, one2, two2, tall,
    one1, two1, wide1, tmp1, one0, two0, tmp0,
):
    parts2 = (diag2, inverse2, first2, second2, third2)
    whole = solve23(gathered, rows2, parts2, one2, two2, tall)
    parts1 = (inverse1, first1, second1, third1)
    coarse = post1(packed, whole, region1, parts1, one1, two1, wide1, tmp1)
    post0(kept0, coarse, out, one0, two0, tmp0)


def f32(*shape):
    return jax.ShapeDtypeStruct(shape, jnp.float32)


def buffer(*shape):
    return pltpu.VMEM(shape, jnp.float32)


def call(kernel, out, scratch, name, *operands):
    return pl.pallas_call(
        kernel,
        out_shape=out,
        scratch_shapes=scratch,
        name=name,
        compiler_params=pltpu.CompilerParams(vmem_limit_bytes=VMEM),
    )(*operands)


def pre0(*pieces):
    plane = buffer(24, ROWS0, LANES)
    scratch = [plane] * 7 + [buffer(20, 64, LANES)]
    coarse = lambda count: f32(count, ROWS1, LANES)
    out = (f32(7, KEPT0, KEPT_ROWS0, LANES), coarse(6), coarse(8), coarse(6), coarse(4), f32(144, LANES))
    return call(pre0_kernel, out, scratch, "pre0", *pieces)


def pre1(*pieces):
    plane, work = f32(DEPTH1, ROWS1, LANES), buffer(DEPTH1, ROWS1, LANES)
    scratch = [work, work, buffer(6, ROWS1, LANES), buffer(16, LANES)]
    out = (f32(16, 6 * LANES), f32(3, DEPTH1, ROWS1, LANES)) + (plane,) * 4
    return call(pre1_kernel, out, scratch, "pre1", *pieces)


def finish(*pieces):
    plane2 = buffer(DEPTH2 + 2, ROWS2, LANES)
    plane1 = buffer(DEPTH1, ROWS1, LANES)
    plane0 = buffer(KEPT0, KEPT_ROWS0, LANES)
    scratch = [buffer(3, DEPTH2 + 2, ROWS2, LANES)] + [plane2] * 7 + [buffer(3, 128, LANES)]
    scratch += [plane1] * 2 + [buffer(DEPTH2 + 6, 24, LANES), buffer(8, 32, LANES)]
    scratch += [plane0] * 2 + [buffer(5, KEPT_ROWS0, LANES)]
    return call(finish_kernel, f32(2, 16, LANES), scratch, "finish", *pieces)


def layers_apart(value, steps):
    count = lax.axis_size("gx")
    ways = [(i, i + (LAYER * steps if i % 2 == 0 else -LAYER * steps)) for i in range(count)]
    return lax.ppermute(value, "gx", [(i, j) for i, j in ways if 0 <= j < count])


def columns_apart(value):
    count, wide = lax.axis_size("gx"), lax.axis_size("gy")
    ways = [
        (i * wide + j, i * wide + j + (1 if i % 2 == 0 else -1))
        for i in range(count)
        for j in range(wide)
        if 0 <= j + (1 if i % 2 == 0 else -1) < wide
    ]
    return lax.ppermute(value, ("gx", "gy"), ways)


def body(source, absorb, beta):
    members = lax.axis_size("gx")
    wide = lax.axis_size("gy")
    layers = members // LAYER
    near = [[LAYER * z + c for c in range(LAYER)] for z in range(layers)]
    chips = [[2 * chip, 2 * chip + 1] for chip in range(members // 2)]
    column = [[LAYER * z + c for z in range(layers)] for c in range(LAYER)]
    cores = [
        [(LAYER * z + 2 * chip + core) * wide + y for chip in range(2) for y in range(wide)]
        for z in range(layers)
        for core in range(2)
    ]
    first_core = lax.axis_index("gx") % 2 == 0

    def both(value):
        return lax.all_gather(value, "gx", axis_index_groups=chips)

    local = jnp.stack([source, absorb, beta])
    own = lax.all_gather(local, "gx", axis_index_groups=near)
    def tiles_of(arrays):
        return jnp.concatenate([x.reshape(-1, 8, LANES) for x in arrays])

    sides = columns_apart(own)
    outer = layers_apart(own, 1)
    sides = both(sides)
    layer = jnp.concatenate([sides[0], own, sides[1]], axis=-2)
    rims = jnp.concatenate([sides[0, ..., 8:, :], sides[1, ..., :8, :]], axis=-2)
    ends = jnp.concatenate([sides[0, ..., :8, :], sides[1, ..., 8:, :]], axis=-2)
    sent = []
    for rows, reaches in ((rims, RIM_REACH), (ends, END_REACH)):
        for kind, reach in enumerate(reaches):
            sent.append(jnp.where(first_core, rows[LAYER - reach :, kind], rows[:reach, kind]))
    rest = layers_apart(tiles_of(sent), 1)
    outer = both(tiles_of([outer]))
    kept0, rest1, beta1, diag1, absorb1, sent1 = pre0(layer, outer, both(rest))

    outer = both(layers_apart(sent1, 1))
    pay, *kept1 = pre1(rest1, beta1, diag1, outer, absorb1)

    place = lax.axis_index("gx")
    start = (place >> 2) + (((place & 3) ^ 3) >> 1)
    pay, start = lax.optimization_barrier((pay, start))
    rows = lax.all_to_all(pay, "gx", 0, 0, axis_index_groups=column)
    rows, start = lax.optimization_barrier((rows, start))
    fields = jnp.pad(rows[:, 2 * LANES :], ((2, 2), (0, 0)))
    fields = lax.dynamic_slice_in_dim(fields, start, 4)
    rows = jnp.concatenate([x.reshape(-1, LANES) for x in (rows[:, : 2 * LANES], fields)])
    rows = jnp.broadcast_to(rows, (2 * wide,) + rows.shape)
    rows = lax.all_to_all(rows, ("gx", "gy"), 0, 0, axis_index_groups=cores)
    packed = both(rows).reshape(-1, SLOT, LANES)
    return finish(packed.reshape(-1, LANES), packed, *kept1, kept0)


def solution(mesh):
    placed = (P("gx", "gy", None), P("gx", "gy", None), P("gx", "gy", None))
    return jax.shard_map(
        body, mesh=mesh, in_specs=placed, out_specs=P("gx", "gy", None), check_vma=False
    )
```
